32 devices in a mesh: row: 8 (over y, x, core), col: 4 (over z).
Axes of the slice: x: 2, y: 2, z: 4, core: 2. Of those that a mesh axis runs over, the one named last changes fastest.
Arguments:
- hidden_states: bfloat16 [8192, 2048], P('row', 'col'), may hold values from -21 to 21
- lengths: int32 [16], P('row'), may hold values from 16 to 512, as said below
- qkvg_master: float32 [2048, 12288], P(('row', 'col')), may hold values from -0.125 to 0.125
- gateup_master: float32 [2, 2048, 4096], P(None, ('row', 'col')), may hold values from -0.125 to 0.125
- out_master: float32 [4096, 2048], P(None, ('row', 'col')), may hold values from -0.09375 to 0.09375
- down_master: float32 [4096, 2048], P(None, ('row', 'col')), may hold values from -0.09375 to 0.09375
Outputs:
- layer_output: bfloat16 [8192, 2048], P('row', 'col')
- qkvg_weight: bfloat16 [2048, 12288], P('row', 'col')
- gateup_weight: bfloat16 [2, 2048, 4096], P(None, 'row', 'col')
- mixing_weight: bfloat16 [4096, 2048], P('col', 'row')
- down_weight: bfloat16 [4096, 2048], P('col', 'row')
The draws below stay inside these ranges and needn't reach their ends.
Inputs may be any that keep to these rules, and one draw needn't show every extreme that they name: `lengths`: prompt length of each request; the positions of a request from its length on are padding. Some request has length 512 in every draw.
All inputs are finite; a program needn't handle non-finite values.
Results may differ from the reference program's by a relative error of at most 0.014.
Values may be sent and summed in bfloat16 or wider, within the bound.
No kernel may reach another device: no remote copies, remote signals or barrier semaphores. Data moves between devices by JAX's collectives and lax.ppermute only.
A program may use at most 128 MiB of HBM per device.

```python
import math
import jax
import jax.numpy as jnp
from jax import lax

D = 2048
HEADS = 8
KEY = 256
VAL = 512
FF = 4096
S = 512
BLOCK = 256
REQ = 16
TOKENS = 8192
N_COL = 4


def draw_hidden_states(key, part):
    first_key, second_key = jax.random.split(key, 2)
    column_scale = jnp.exp(jax.random.uniform(first_key, (D,), jnp.float32, math.log(0.3), math.log(3.0)))
    values = jnp.clip(jax.random.normal(second_key, (TOKENS, D), jnp.float32), -6.0, 6.0) * column_scale[None, :]
    return values.astype(jnp.bfloat16)


def draw_lengths(key, part):
    first_key, second_key, third_key = jax.random.split(key, 3)
    short = jax.random.randint(first_key, (REQ,), 16, min(65, S))
    coin = jax.random.randint(second_key, (REQ,), 0, 20)
    chosen = jax.random.randint(third_key, (), 0, REQ)
    longer = (coin < 7) | (jnp.arange(REQ) == chosen)
    return jnp.where(longer, S, short).astype(jnp.int32)


def steps_of(own_key, extent, shards, smallest, high):
    factor_of, own = 1.0, jax.random.fold_in(own_key, 6)
    for dim, shards_of in shards:
        draws = jnp.exp(jax.random.uniform(jax.random.fold_in(own, dim), (shards_of,), jnp.float32, smallest / len(shards), high / len(shards)))
        factor_of = factor_of * jnp.repeat(draws, extent[dim] // shards_of).reshape([-1 if axis == dim else 1 for axis in range(len(extent))])
    return factor_of


def bell_draw(rng, dims, scale, most, cuts=(), kind=jnp.bfloat16):
    values = scale * jax.random.normal(rng, dims, jnp.float32)
    if cuts:
        values = values * steps_of(rng, dims, cuts, -0.22, 0.18)
    return jnp.clip(values, -most, most).astype(kind)


def setup_inputs(seed: int = 0) -> dict:
    keys = jax.random.split(jax.random.key(seed), 7)
    return {
        "hidden_states": draw_hidden_states(jax.random.fold_in(keys[6], 71), 0),
        "lengths": draw_lengths(jax.random.fold_in(keys[6], 71), 0),
        "qkvg_master": bell_draw(keys[2], (D, HEADS * (2 * KEY + 2 * VAL)), D ** -0.5, 0.125, ((0, 32),), jnp.float32),
        "gateup_master": bell_draw(keys[3], (2, D, FF), D ** -0.5, 0.125, ((1, 32),), jnp.float32),
        "out_master": bell_draw(keys[4], (HEADS * VAL, D), (HEADS * VAL) ** -0.5, 0.09375, ((1, 32),), jnp.float32),
        "down_master": bell_draw(keys[5], (FF, D), FF ** -0.5, 0.09375, ((1, 32),), jnp.float32),
    }


epsilon = 1e-05

def to_half(values):
    return lax.optimization_barrier(values.astype(jnp.bfloat16))

def rms_round(values):
    scale = lax.rsqrt(lax.optimization_barrier(jnp.mean(values * values, axis=-1, keepdims=True)) + epsilon)
    return to_half(values * scale)

def rotate(values, positions):
    half = values.shape[-1] // 2
    freq = jnp.power(10000.0, -2.0 * jnp.arange(half).astype(jnp.float32) / values.shape[-1])
    angle = positions.astype(jnp.float32)[:, None] * freq[None, :]
    cosine = jnp.cos(angle)[:, None, :]
    sine = jnp.sin(angle)[:, None, :]
    first = values[..., :half]
    second = values[..., half:]
    return jnp.concatenate([first * cosine - second * sine, first * sine + second * cosine], axis=-1)

def retain(gammas, query, keyed, value):
    heads = query.shape[1]
    blocks = S // BLOCK
    offsets = jnp.arange(BLOCK)
    lag = offsets[:, None] - offsets[None, :]
    within = jnp.where((lag >= 0)[None], jnp.power(gammas[:, None, None], jnp.maximum(lag, 0).astype(jnp.float32)[None]), 0.0)
    into = jnp.power(gammas[:, None], (offsets + 1).astype(jnp.float32)[None, :])
    leaving = jnp.power(gammas[:, None], (BLOCK - 1 - offsets).astype(jnp.float32)[None, :])
    across_blocks_sum = jnp.power(gammas, 1.0 * BLOCK)
    upper_bound = lax.Precision.HIGHEST

    def advance(carry, inputs):
        retention_state, key_sum = carry
        query_block, key_block, value_tile_rows = inputs
        query_float = query_block.astype(jnp.float32)
        key_float = key_block.astype(jnp.float32)
        value_single_float = value_tile_rows.astype(jnp.float32)
        scores = jnp.einsum('thk,shk->hts', query_float, key_float, precision=upper_bound) * within
        denom_inside = lax.optimization_barrier(jnp.sum(scores, axis=2))
        weights = to_half(scores).astype(jnp.float32)
        inside = jnp.einsum('hts,shv->thv', weights, value_single_float, precision=upper_bound)
        damped_query_rows = query_float * jnp.transpose(into)[:, :, None]
        carried_state = jnp.einsum('swc,wcm->swm', damped_query_rows, retention_state, precision=upper_bound)
        denom_carried = jnp.einsum('thk,hk->th', damped_query_rows, key_sum, precision=upper_bound)
        damped_key_rows = key_float * jnp.transpose(leaving)[:, :, None]
        retention_state = across_blocks_sum[:, None, None] * retention_state + jnp.einsum('wat,wag->atg', damped_key_rows, value_single_float, precision=upper_bound)
        key_sum = across_blocks_sum[:, None] * key_sum + lax.optimization_barrier(jnp.sum(damped_key_rows, axis=0))
        denom = jnp.transpose(denom_inside) + denom_carried
        result = (inside + carried_state) / jnp.maximum(jnp.abs(denom), 1.0)[:, :, None]
        return ((retention_state, key_sum), result)
    start = (jnp.zeros((heads, KEY, VAL), jnp.float32), jnp.zeros((heads, KEY), jnp.float32))
    sliced = (query.reshape(blocks, BLOCK, heads, KEY), keyed.reshape(blocks, BLOCK, heads, KEY), value.reshape(blocks, BLOCK, heads, VAL))
    _, results = lax.scan(advance, start, sliced)
    return results.reshape(S, heads, VAL)

def gate_heads(retained, gate):
    centre = lax.optimization_barrier(jnp.mean(retained, axis=-1, keepdims=True))
    centred = retained - centre
    spread = lax.optimization_barrier(jnp.mean(centred * centred, axis=-1, keepdims=True))
    grouped = centred * lax.rsqrt(spread + epsilon)
    return to_half(jax.nn.silu(gate.astype(jnp.float32)) * grouped)

def group_sum(left, right):
    width = left.shape[1] // N_COL
    terms = jnp.einsum('tcv,cvd->ctd', left.astype(jnp.float32).reshape(left.shape[0], N_COL, width), right.astype(jnp.float32).reshape(N_COL, width, right.shape[1]), precision=lax.Precision.HIGHEST)
    return lax.optimization_barrier(jnp.sum(to_half(terms).astype(jnp.float32), axis=0))

def request_layer(inputs, qkvg_weight, gateup_weight, mixing_weight, down_weight):
    tokens, length = inputs
    normed = rms_round(tokens.astype(jnp.float32))
    projected = to_half(jnp.dot(normed, qkvg_weight, preferred_element_type=jnp.float32)).reshape(S, HEADS, 2 * KEY + 2 * VAL)
    positions = jnp.arange(S)
    query = to_half(rotate(projected[:, :, :KEY].astype(jnp.float32), positions))
    keyed = to_half(rotate(projected[:, :, KEY:2 * KEY].astype(jnp.float32), positions) * (1.0 / math.sqrt(KEY)))
    value = projected[:, :, 2 * KEY:2 * KEY + VAL]
    gate = projected[:, :, 2 * KEY + VAL:]
    gammas = 1.0 - jnp.power(2.0, -5.0 - jnp.arange(HEADS).astype(jnp.float32))
    retained = retain(gammas, query, keyed, value)
    mixed = gate_heads(retained, gate).reshape(S, HEADS * VAL)
    residual = tokens.astype(jnp.float32) + group_sum(mixed, mixing_weight)
    normed_mid = rms_round(residual)
    gate_part = jnp.dot(normed_mid, gateup_weight[0], preferred_element_type=jnp.float32)
    up_part = jnp.dot(normed_mid, gateup_weight[1], preferred_element_type=jnp.float32)
    hidden = to_half(jax.nn.silu(gate_part) * up_part)
    feed = group_sum(hidden, down_weight)
    live = positions < length
    return jnp.where(live[:, None], residual + feed, 0.0).astype(jnp.bfloat16)

def reference(hidden_states, lengths, qkvg_master, gateup_master, out_master, down_master):
    qkvg_weight = qkvg_master.astype(jnp.bfloat16)
    gateup_weight = gateup_master.astype(jnp.bfloat16)
    mixing_weight = out_master.astype(jnp.bfloat16)
    down_weight = down_master.astype(jnp.bfloat16)

    def one_request(inputs):
        return request_layer(inputs, qkvg_weight, gateup_weight, mixing_weight, down_weight)
    outputs = lax.map(one_request, (hidden_states.reshape(REQ, S, D), lengths))
    return (outputs.reshape(TOKENS, D), qkvg_weight, gateup_weight, mixing_weight, down_weight)
```

```python
import functools
import math

import jax
import jax.numpy as jnp
from jax import lax
from jax.experimental import pallas as pl
from jax.experimental.pallas import tpu as pltpu
from jax.sharding import PartitionSpec as P

D = 2048
HEADS = 8
KEY = 256
VAL = 512
S = 512
TILE = 16
TILES = S // TILE
HEAD_WIDTH = 2 * KEY + 2 * VAL

epsilon = 1e-05
VMEM_LIMIT = 56 * 1024 * 1024

SMEM = pl.BlockSpec(memory_space=pltpu.SMEM)
VMEM = pl.BlockSpec(memory_space=pltpu.VMEM)
ANY = pl.BlockSpec(memory_space=pl.ANY)


def params():
    return pltpu.CompilerParams(vmem_limit_bytes=VMEM_LIMIT)


def cost(flops, moved):
    return pl.CostEstimate(flops=int(flops), bytes_accessed=int(moved), transcendentals=0)


def swap(block, bit):
    size = lax.axis_size("row")
    return lax.ppermute(block, "row", [(i, i ^ bit) for i in range(size)])


def shift(block, step):
    size = lax.axis_size("col")
    return lax.ppermute(block, "col", [(i, (i + step) % size) for i in range(size)])


def gather_rows(block):
    size = lax.axis_size("row")
    pieces = {0: block}
    if size == 8:
        half = block.shape[0] // 2
        pieces[2] = swap(block, 2)
        pieces[4] = swap(block, 4)
        pieces[6] = jnp.concatenate([swap(pieces[4][:half], 2), swap(pieces[2][half:], 4)], axis=0)
        bits = [1]
    else:
        bits = [1 << i for i in reversed(range(size.bit_length() - 1))]
    for bit in bits:
        for j in sorted(pieces):
            pieces[j | bit] = swap(pieces[j], bit)
    return [pieces[j] for j in range(size)]


def gather_cols(block):
    return [block] + [shift(block, k) for k in range(1, lax.axis_size("col"))]


def cut_qkvg_kernel(cols, place, master, *outs):
    width = outs[0].shape[1]
    for k in range(cols):
        target = lax.rem(place[1] + k, cols)
        outs[k][...] = master[:, pl.ds(pl.multiple_of(target * width, 128), width)].astype(jnp.bfloat16)


def cut_rest_kernel(cols, place, out_master, down_master, gateup_master, *outs):
    width = outs[0].shape[2]
    for k in range(cols):
        target = lax.rem(place[1] + k, cols)
        rows = pl.ds(pl.multiple_of(target * width, 128), width)
        outs[k][0] = out_master[rows, :].T.astype(jnp.bfloat16)
        outs[k][1] = down_master[rows, :].T.astype(jnp.bfloat16)
        outs[k][2] = gateup_master[0, :, rows].astype(jnp.bfloat16)
        outs[k][3] = gateup_master[1, :, rows].astype(jnp.bfloat16)


def join_kernel(cols, place, *refs):
    out = refs[-1]
    rows = refs[0].shape[-2]
    for k in range(cols):
        source = lax.rem(place[1] - k + cols, cols)
        where = pl.ds(pl.multiple_of(source * rows, 16), rows)
        if len(out.shape) == 2:
            out[where, :] = refs[k][...]
        else:
            out[:, where, :] = refs[k][...]


def cut(kernel, shape, place, *masters):
    cols = lax.axis_size("col")
    return pl.pallas_call(
        functools.partial(kernel, cols),
        out_shape=[jax.ShapeDtypeStruct(shape, jnp.bfloat16)] * cols,
        in_specs=[SMEM] + [VMEM] * len(masters),
        out_specs=[VMEM] * cols,
        compiler_params=params(),
        cost_estimate=cost(0, 8 * math.prod(shape) * cols),
    )(place, *masters)


def join(blocks, place):
    cols = len(blocks)
    shape = list(blocks[0].shape)
    shape[-2] *= cols
    return pl.pallas_call(
        functools.partial(join_kernel, cols),
        out_shape=jax.ShapeDtypeStruct(tuple(shape), jnp.bfloat16),
        in_specs=[SMEM] + [VMEM] * cols,
        out_specs=VMEM,
        compiler_params=params(),
        cost_estimate=cost(0, 4 * math.prod(shape)),
    )(place, *blocks)


def pack_kernel(requests, rows, passes, place, lengths, table, bins, starts, count, used):
    row = place[0]

    def clear(i, carry):
        table[i] = -1
        return carry

    lax.fori_loop(0, passes * TILES, clear, 0)

    def clear_used(i, carry):
        used[i] = 0
        return carry

    lax.fori_loop(0, requests, clear_used, 0)

    def put(q, top):
        tiles = (lengths[q] + (TILE - 1)) // TILE

        def look(i, best):
            b = requests - 1 - i
            return jnp.where(used[b] + tiles <= TILES, b, best)

        b = lax.fori_loop(0, requests, look, requests - 1)
        start = used[b]
        used[b] = start + tiles
        bins[q] = b
        starts[q] = start
        turn = b // rows

        @pl.when(b - turn * rows == row)
        def _():
            def note(i, carry):
                table[turn * TILES + start + i] = q * TILES + i
                return carry

            lax.fori_loop(0, tiles, note, 0)

        return jnp.maximum(top, b + 1)

    count[0] = lax.fori_loop(0, requests, put, 0)


def pack(place, lengths, rows):
    requests = lengths.shape[0]
    passes = requests // rows
    whole = lambda n: jax.ShapeDtypeStruct((n,), jnp.int32)
    return pl.pallas_call(
        functools.partial(pack_kernel, requests, rows, passes),
        out_shape=[whole(passes * TILES), whole(requests), whole(requests), whole(1)],
        in_specs=[SMEM, SMEM],
        out_specs=[SMEM] * 4,
        scratch_shapes=[pltpu.SMEM((requests,), jnp.int32)],
        compiler_params=params(),
    )(place, lengths)


def pick_kernel(rows, per_row, turn, place, table, *refs):
    pieces, out, sem = refs[:rows], refs[rows], refs[rows + 1]
    row = place[0]

    def step(i, carry):
        code = jnp.maximum(table[turn * TILES + i], 0)
        request = code // TILES
        owner = request // per_row
        tile = (request - owner * per_row) * TILES + (code - request * TILES)
        piece = lax.bitwise_xor(owner, row)
        source = pl.ds(pl.multiple_of(tile * TILE, TILE), TILE)
        target = pl.ds(pl.multiple_of(i * TILE, TILE), TILE)
        for j in range(rows):

            @pl.when(piece == j)
            def _():
                pltpu.make_async_copy(pieces[j].at[source, :], out.at[target, :], sem).start()

        return carry

    lax.fori_loop(0, TILES, step, 0)
    pltpu.make_async_copy(out, out, sem).wait()


def pick(place, table, pieces, turn):
    rows = len(pieces)
    width = pieces[0].shape[1]
    return pl.pallas_call(
        functools.partial(pick_kernel, rows, pieces[0].shape[0] // S, turn),
        out_shape=jax.ShapeDtypeStruct((S, width), jnp.bfloat16),
        in_specs=[SMEM, SMEM] + [ANY] * rows,
        out_specs=VMEM,
        scratch_shapes=[pltpu.SemaphoreType.DMA],
        compiler_params=params(),
        cost_estimate=cost(0, 4 * S * width),
    )(place, table, *pieces)


def spread_kernel(rows, per_row, total, place, lengths, bins, starts, *refs):
    pieces, out = refs[:total], refs[total]
    row = place[0]
    width = out.shape[1]
    for a in range(per_row):
        request = row * per_row + a
        length = lengths[request]
        b = bins[request]
        start = starts[request]
        turn = b // rows
        index = lax.bitwise_xor(b - turn * rows, row) + turn * rows
        tiles = (length + (TILE - 1)) // TILE

        def blank(i, carry):
            out[pl.ds(pl.multiple_of(a * S + i * TILE, TILE), TILE), :] = jnp.zeros((TILE, width), jnp.bfloat16)
            return carry

        lax.fori_loop(tiles, TILES, blank, 0)
        for j in range(total):

            @pl.when(index == j)
            def _():
                def move(i, carry):
                    values = pieces[j][pl.ds(pl.multiple_of((start + i) * TILE, TILE), TILE), :]
                    position = i * TILE + lax.broadcasted_iota(jnp.int32, (TILE, width), 0)
                    kept = jnp.where(position < length, values.astype(jnp.float32), 0.0)
                    out[pl.ds(pl.multiple_of(a * S + i * TILE, TILE), TILE), :] = kept.astype(jnp.bfloat16)
                    return carry

                lax.fori_loop(0, tiles, move, 0)


def spread(place, lengths, bins, starts, pieces, rows, per_row):
    width = pieces[0].shape[1]
    return pl.pallas_call(
        functools.partial(spread_kernel, rows, per_row, len(pieces)),
        out_shape=jax.ShapeDtypeStruct((per_row * S, width), jnp.bfloat16),
        in_specs=[SMEM] * 4 + [VMEM] * len(pieces),
        out_specs=VMEM,
        compiler_params=params(),
        cost_estimate=cost(0, 2 * S * width * (len(pieces) + per_row)),
    )(place, lengths, bins, starts, *pieces)


DOT = functools.partial(jnp.dot, preferred_element_type=jnp.float32)


def dot_nt(left, right):
    return lax.dot_general(left, right, (((1,), (1,)), ((), ())), preferred_element_type=jnp.float32)


def retain_kernel(rows, cols, place, decays, cosine, sine, seg_col, seg_row, *refs):
    tokens, weights = refs[:cols], refs[cols : cols + rows]
    mixed, normed = refs[cols + rows], refs[cols + rows + 1]
    depth = D // rows
    ratio = rows // cols
    head = pl.program_id(0)

    @pl.when(head == 0)
    def _():
        total = jnp.zeros((S, 1), jnp.float32)
        for k in range(cols):
            values = tokens[k][...].astype(jnp.float32)
            total += jnp.sum(values * values, axis=1, keepdims=True)
        scale = lax.rsqrt(total / D + epsilon)
        for k in range(cols):
            source = lax.rem(place[1] - k + cols, cols)
            for i in range(ratio):
                values = tokens[k][:, i * depth : (i + 1) * depth].astype(jnp.float32)
                normed[source * ratio + i] = (values * scale).astype(jnp.bfloat16)

    def project(low, width):
        total = jnp.zeros((S, width), jnp.float32)
        for j in range(rows):
            total += DOT(normed[lax.bitwise_xor(place[0], j)], weights[j][:, low : low + width])
        return total.astype(jnp.bfloat16)

    def rotate(values):
        values = values.astype(jnp.float32)
        first, second = values[:, : KEY // 2], values[:, KEY // 2 :]
        cos, sin = cosine[...], sine[...]
        return jnp.concatenate([first * cos - second * sin, first * sin + second * cos], axis=1)

    both = project(0, 2 * KEY)
    query = rotate(both[:, :KEY]).astype(jnp.bfloat16)
    keyed = (rotate(both[:, KEY:]) * (1.0 / math.sqrt(KEY))).astype(jnp.bfloat16)
    value = project(2 * KEY, VAL)
    gate = project(2 * KEY + VAL, VAL).astype(jnp.float32)
    lag = lax.broadcasted_iota(jnp.int32, (S, S), 0) - lax.broadcasted_iota(jnp.int32, (S, S), 1)
    allowed = (lag >= 0) & (seg_col[...] == seg_row[...])
    decay = jnp.where(allowed, jnp.exp(jnp.maximum(lag, 0).astype(jnp.float32) * decays[head]), 0.0)
    scores = dot_nt(query, keyed) * decay
    denom = jnp.sum(scores, axis=1, keepdims=True)
    retained = DOT(scores.astype(jnp.bfloat16), value) / jnp.maximum(jnp.abs(denom), 1.0)
    centred = retained - jnp.mean(retained, axis=1, keepdims=True)
    spread_of = jnp.mean(centred * centred, axis=1, keepdims=True)
    grouped = centred * lax.rsqrt(spread_of + epsilon)
    mixed[...] = (gate * (1.0 / (1.0 + jnp.exp(-gate))) * grouped).astype(jnp.bfloat16)


def retain(place, decays, cosine, sine, seg_col, seg_row, tokens, weights):
    rows, cols = len(weights), len(tokens)
    depth = D // rows
    heads = HEADS // cols
    fixed = lambda shape: pl.BlockSpec(shape, lambda h: (0,) * len(shape))
    return pl.pallas_call(
        functools.partial(retain_kernel, rows, cols),
        grid=(heads,),
        out_shape=jax.ShapeDtypeStruct((S, heads * VAL), jnp.bfloat16),
        in_specs=[SMEM, SMEM]
        + [fixed(v.shape) for v in (cosine, sine, seg_col, seg_row)]
        + [fixed(v.shape) for v in tokens]
        + [pl.BlockSpec((depth, HEAD_WIDTH), lambda h: (0, h))] * rows,
        out_specs=pl.BlockSpec((S, VAL), lambda h: (0, h)),
        scratch_shapes=[pltpu.VMEM((rows, S, depth), jnp.bfloat16)],
        compiler_params=params(),
        cost_estimate=cost(2 * S * D * HEAD_WIDTH * heads * 1.3, 2 * D * HEAD_WIDTH * heads),
    )(place, decays, cosine, sine, seg_col, seg_row, *tokens, *weights)


def put_term(rows, cols, place, outs, j, term):
    ratio = rows // cols
    depth = D // rows
    owner = lax.bitwise_xor(place[0], j)
    target = owner // ratio
    slot = lax.rem(target - place[1] + cols, cols)
    columns = pl.ds(pl.multiple_of((owner - target * ratio) * depth, 128), depth)
    for k in range(cols):

        @pl.when(slot == k)
        def _():
            outs[k][:, columns] = term.astype(jnp.bfloat16)


def mix_kernel(rows, cols, place, mixed, *refs):
    weights, outs = refs[:rows], refs[rows:]
    for j in range(rows):
        put_term(rows, cols, place, outs, j, dot_nt(mixed[...], weights[j][0]))


def mix(place, mixed, weights, cols):
    rows = len(weights)
    width = D // cols
    piece = weights[0].shape
    return pl.pallas_call(
        functools.partial(mix_kernel, rows, cols),
        grid=(1,),
        out_shape=[jax.ShapeDtypeStruct((S, width), jnp.bfloat16)] * cols,
        in_specs=[SMEM, pl.BlockSpec(mixed.shape, lambda i: (0, 0))]
        + [pl.BlockSpec((1,) + piece[1:], lambda i: (0, 0, 0))] * rows,
        out_specs=[pl.BlockSpec((S, width), lambda i: (0, 0))] * cols,
        compiler_params=params(),
        cost_estimate=cost(2 * S * D * mixed.shape[1], 2 * D * mixed.shape[1]),
    )(place, mixed, *weights)


def feed_kernel(rows, cols, steps, place, *refs):
    tokens = refs[:cols]
    downs = refs[cols : cols + rows]
    pairs = refs[cols + rows : cols + 2 * rows]
    outs = refs[cols + 2 * rows : 2 * cols + 2 * rows]
    ordered, scale, hidden = refs[2 * cols + 2 * rows :]
    depth = D // rows
    ratio = rows // cols
    step = pl.program_id(0)

    @pl.when(step == 0)
    def _():
        total = jnp.zeros((S, 1), jnp.float32)
        for k in range(cols):
            source = lax.rem(place[1] - k + cols, cols)
            values = tokens[k][...].astype(jnp.float32)
            total += jnp.sum(values * values, axis=1, keepdims=True)
            for i in range(ratio):
                ordered[source * ratio + i] = tokens[k][:, i * depth : (i + 1) * depth]
        scale[...] = lax.rsqrt(total / D + epsilon)

    def product(index):
        width = pairs[0].shape[2]
        total = jnp.zeros((S, width), jnp.float32)
        for j in range(rows):
            total += DOT(ordered[lax.bitwise_xor(place[0], j)], pairs[j][index])
        return total * scale[...]

    gate = product(0)
    up = product(1)
    hidden[step] = (gate * (1.0 / (1.0 + jnp.exp(-gate))) * up).astype(jnp.bfloat16)

    @pl.when(step == steps - 1)
    def _():
        everything = jnp.concatenate([hidden[i] for i in range(steps)], axis=1)
        for j in range(rows):
            put_term(rows, cols, place, outs, j, dot_nt(everything, downs[j][0]))


def feed(place, tokens, weights):
    rows, cols = len(weights), len(tokens)
    _, depth, units = weights[0].shape
    tile = 256
    steps = units // tile
    width = D // cols
    return pl.pallas_call(
        functools.partial(feed_kernel, rows, cols, steps),
        grid=(steps,),
        out_shape=[jax.ShapeDtypeStruct((S, width), jnp.bfloat16)] * cols,
        in_specs=[SMEM]
        + [pl.BlockSpec((S, width), lambda i: (0, 0))] * cols
        + [pl.BlockSpec((1, depth, units), lambda i: (1, 0, 0))] * rows
        + [pl.BlockSpec((2, depth, tile), lambda i: (1, 0, i))] * rows,
        out_specs=[pl.BlockSpec((S, width), lambda i: (0, 0))] * cols,
        scratch_shapes=[
            pltpu.VMEM((rows, S, depth), jnp.bfloat16),
            pltpu.VMEM((S, 1), jnp.float32),
            pltpu.VMEM((steps, S, tile), jnp.bfloat16),
        ],
        compiler_params=params(),
        cost_estimate=cost(6 * S * D * units, 6 * D * units),
    )(place, *tokens, *weights, *weights)


def collect(terms):
    parts = [terms[0]] + [shift(terms[k], k) for k in range(1, len(terms))]
    return sum(part.astype(jnp.float32) for part in parts)


def shards(hidden_states, lengths, qkvg_master, gateup_master, out_master, down_master):
    rows, cols = lax.axis_size("row"), lax.axis_size("col")
    per_row = lengths.shape[0]
    heads = HEADS // cols
    place = jnp.stack([lax.axis_index("row"), lax.axis_index("col")]).astype(jnp.int32)

    all_lengths = lax.all_gather(lengths, "row", axis=0, tiled=True)
    everyone = gather_rows(hidden_states)

    depth = qkvg_master.shape[0]
    qkvg_cut = cut(cut_qkvg_kernel, (depth, heads * HEAD_WIDTH), place, qkvg_master)
    qkvg_blocks = join([qkvg_cut[0]] + [shift(qkvg_cut[k], k) for k in range(1, cols)], place)
    rest_cut = cut(
        cut_rest_kernel,
        (4, depth, gateup_master.shape[2] // cols),
        place,
        out_master,
        down_master,
        gateup_master,
    )
    rest_blocks = join([rest_cut[0]] + [shift(rest_cut[k], k) for k in range(1, cols)], place)

    table, bins, starts, count = pack(place, all_lengths, rows)
    qkvg_pieces = gather_rows(qkvg_blocks)
    rest_pieces = gather_rows(rest_blocks)

    head_ids = lax.axis_index("col") * heads + jnp.arange(heads)
    decays = jnp.log1p(-jnp.power(2.0, -5.0 - head_ids.astype(jnp.float32)))
    freq = jnp.power(10000.0, -2.0 * jnp.arange(KEY // 2).astype(jnp.float32) / KEY)

    def layer(turn):
        codes = table[turn * TILES : (turn + 1) * TILES]
        segments = jnp.where(codes < 0, -1, codes // TILES)
        seg = jnp.broadcast_to(segments[:, None], (TILES, TILE)).reshape(S)
        positions = ((jnp.maximum(codes, 0) % TILES)[:, None] * TILE + jnp.arange(TILE)[None, :]).reshape(S)
        angle = positions.astype(jnp.float32)[:, None] * freq[None, :]
        own = pick(place, table, everyone, turn)
        mixed = retain(
            place,
            decays,
            jnp.cos(angle),
            jnp.sin(angle),
            seg[:, None],
            seg[None, :],
            gather_cols(own),
            qkvg_pieces,
        )
        residual = own.astype(jnp.float32) + collect(mix(place, mixed, rest_pieces, cols))
        terms = feed(place, gather_cols(residual.astype(jnp.bfloat16)), rest_pieces)
        return gather_rows((residual + collect(terms)).astype(jnp.bfloat16))

    first = layer(0)

    def finish(pieces):
        return spread(place, all_lengths, bins, starts, pieces, rows, per_row)

    def more(pieces):
        for turn in range(1, per_row):
            pieces = pieces + layer(turn)
        return finish(pieces)

    layer_output = lax.cond(count[0] > rows, more, finish, first)
    return (
        layer_output,
        qkvg_blocks,
        rest_blocks[2:],
        rest_blocks[0].T,
        rest_blocks[1].T,
    )


def solution(mesh):
    return jax.shard_map(
        shards,
        mesh=mesh,
        in_specs=(
            P("row", "col"),
            P("row"),
            P(("row", "col"), None),
            P(None, ("row", "col"), None),
            P(None, ("row", "col")),
            P(None, ("row", "col")),
        ),
        out_specs=(
            P("row", "col"),
            P("row", "col"),
            P(None, "row", "col"),
            P("col", "row"),
            P("col", "row"),
        ),
        check_vma=False,
    )
```

```python
import functools
import math

import jax
import jax.numpy as jnp
from jax import lax
from jax.experimental import pallas as pl
from jax.experimental.pallas import tpu as pltpu
from jax.sharding import PartitionSpec as P

D = 2048
HEADS = 8
KEY = 256
VAL = 512
S = 512
TILE = 16
TILES = S // TILE
HEAD_WIDTH = 2 * KEY + 2 * VAL

epsilon = 1e-05
VMEM_LIMIT = 56 * 1024 * 1024

SMEM = pl.BlockSpec(memory_space=pltpu.SMEM)
VMEM = pl.BlockSpec(memory_space=pltpu.VMEM)
ANY = pl.BlockSpec(memory_space=pl.ANY)


def params():
    return pltpu.CompilerParams(vmem_limit_bytes=VMEM_LIMIT)


def cost(flops, moved):
    return pl.CostEstimate(flops=int(flops), bytes_accessed=int(moved), transcendentals=0)


def swap(block, axis, step):
    size = lax.axis_size(axis)
    return lax.ppermute(block, axis, [(i, i ^ step) for i in range(size)])


def after(value, *earlier):
    return lax.optimization_barrier((value,) + earlier)[0]


def gather_rows(block, direct=False):
    size = lax.axis_size("row")
    pieces = {0: block}
    if size == 8:
        half = block.shape[0] // 2
        pieces[2] = swap(block, "row", 2)
        pieces[4] = swap(block, "row", 4)
        if direct:
            pieces[6] = swap(block, "row", 6)
        else:
            upper = swap(pieces[4][:half], "row", 2)
            lower = swap(pieces[2][half:], "row", 4)
            pieces[6] = jnp.concatenate([upper, lower], axis=0)
        bits = [1]
    else:
        bits = [1 << i for i in reversed(range(size.bit_length() - 1))]
    for bit in bits:
        for j in sorted(pieces):
            pieces[j | bit] = swap(pieces[j], "row", bit)
    return [pieces[j] for j in range(size)]


def gather_lengths(lengths):
    size = lax.axis_size("row")
    bit = 1
    while bit < size:
        lengths = jnp.concatenate([lengths, swap(lengths, "row", bit)])
        bit *= 2
    return lengths


def exchange(blocks):
    return [blocks[0]] + [swap(blocks[k], "col", k) for k in range(1, len(blocks))]


def gather_cols(block):
    size = lax.axis_size("col")
    if size != 4:
        return [(block,)] + [(swap(block, "col", k),) for k in range(1, size)]
    near = swap(block, "col", 1)
    far = swap(block, "col", 2)
    middle = lax.ppermute(block, "col", [(1, 2), (2, 1)])
    ends = lax.ppermute(far, "col", [(2, 3), (1, 0)])
    return [(block,), (near,), (far,), (middle, ends)]


def collect(terms):
    size = lax.axis_size("col")
    if size != 4:
        parts = exchange(terms)
    else:
        ends = lax.ppermute(terms[3], "col", [(3, 2), (0, 1)])
        near = swap(terms[1], "col", 1)
        middle = lax.ppermute(terms[3], "col", [(1, 2), (2, 1)])
        both = terms[2].astype(jnp.float32) + ends.astype(jnp.float32)
        far = swap(both.astype(jnp.bfloat16), "col", 2)
        parts = [terms[0], near, far, middle]
    return sum(part.astype(jnp.float32) for part in parts)


def cut_kernel(cols, place, *refs):
    masters, outs = refs[:-cols], refs[-cols:]
    width = outs[0].shape[-1]
    for k in range(cols):
        target = lax.bitwise_xor(place[1], k)
        columns = pl.ds(pl.multiple_of(target * width, 128), width)
        if len(masters) == 1:
            outs[k][...] = masters[0][:, columns].astype(jnp.bfloat16)
        else:
            outs[k][0] = masters[0][:, columns].astype(jnp.bfloat16)
            outs[k][1] = masters[1][0, :, columns].astype(jnp.bfloat16)
            outs[k][2] = masters[1][1, :, columns].astype(jnp.bfloat16)


def cut(shape, place, *masters):
    cols = lax.axis_size("col")
    return pl.pallas_call(
        functools.partial(cut_kernel, cols),
        out_shape=[jax.ShapeDtypeStruct(shape, jnp.bfloat16)] * cols,
        in_specs=[SMEM] + [VMEM] * len(masters),
        out_specs=[VMEM] * cols,
        compiler_params=params(),
        cost_estimate=cost(0, 6 * math.prod(shape) * cols),
    )(place, *masters)


def turned(values):
    return values.astype(jnp.float32).T.astype(jnp.bfloat16)


def join_kernel(cols, kind, place, *refs):
    rows = refs[0].shape[-2]
    for k in range(cols):
        source = lax.bitwise_xor(place[1], k)
        where = pl.ds(pl.multiple_of(source * rows, 16), rows)
        if kind == "qkvg":
            refs[cols][where, :] = refs[k][...]
        elif kind == "out":
            refs[cols + 1][where, :] = refs[k][...]
        else:
            refs[cols + 2][where, :] = refs[k][0]
            refs[cols][0, where, :] = refs[k][1]
            refs[cols][1, where, :] = refs[k][2]
    if kind == "out":
        refs[cols][...] = turned(refs[cols + 1][...])
    elif kind == "feed":
        refs[cols + 1][...] = turned(refs[cols + 2][...])


def join(kind, blocks, place):
    cols = len(blocks)
    depth, width = blocks[0].shape[-2] * cols, blocks[0].shape[-1]
    shapes = {"qkvg": [(depth, width)], "out": [(width, depth)], "feed": [(2, depth, width), (width, depth)]}[kind]
    return pl.pallas_call(
        functools.partial(join_kernel, cols, kind),
        out_shape=[jax.ShapeDtypeStruct(shape, jnp.bfloat16) for shape in shapes],
        in_specs=[SMEM] + [VMEM] * cols,
        out_specs=[VMEM] * len(shapes),
        scratch_shapes=[] if kind == "qkvg" else [pltpu.VMEM((depth, width), jnp.bfloat16)],
        compiler_params=params(),
        cost_estimate=cost(0, 4 * math.prod(blocks[0].shape) * cols),
    )(place, *blocks)


def pack_kernel(requests, rows, passes, place, lengths, table, bins, starts, count, used):
    row = place[0]
    per_row = requests // rows

    def clear(i, carry):
        table[i] = -1
        return carry

    lax.fori_loop(0, passes * TILES, clear, 0)

    def clear_used(i, carry):
        used[i] = 0
        return carry

    lax.fori_loop(0, requests, clear_used, 0)

    def put(q, top):
        owner = q // per_row
        length = lengths[lax.bitwise_xor(owner, row) * per_row + (q - owner * per_row)]
        tiles = (length + (TILE - 1)) // TILE

        def look(i, best):
            b = requests - 1 - i
            return jnp.where(used[b] + tiles <= TILES, b, best)

        b = lax.fori_loop(0, requests, look, requests - 1)
        start = used[b]
        used[b] = start + tiles
        bins[q] = b
        starts[q] = start
        turn = b // rows

        @pl.when(b - turn * rows == row)
        def _():
            def note(i, carry):
                table[turn * TILES + start + i] = q * TILES + i
                return carry

            lax.fori_loop(0, tiles, note, 0)

        return jnp.maximum(top, b + 1)

    count[0] = lax.fori_loop(0, requests, put, 0)


def pack(place, lengths, rows):
    requests = lengths.shape[0]
    passes = requests // rows
    whole = lambda n: jax.ShapeDtypeStruct((n,), jnp.int32)
    return pl.pallas_call(
        functools.partial(pack_kernel, requests, rows, passes),
        out_shape=[whole(passes * TILES), whole(requests), whole(requests), whole(1)],
        in_specs=[SMEM, SMEM],
        out_specs=[SMEM] * 4,
        scratch_shapes=[pltpu.SMEM((requests,), jnp.int32)],
        compiler_params=params(),
    )(place, lengths)


def pick_kernel(rows, per_row, turn, place, table, *refs):
    pieces, out, sem = refs[:rows], refs[rows], refs[rows + 1]
    row = place[0]

    def step(i, carry):
        code = jnp.maximum(table[turn * TILES + i], 0)
        request = code // TILES
        owner = request // per_row
        tile = (request - owner * per_row) * TILES + (code - request * TILES)
        piece = lax.bitwise_xor(owner, row)
        source = pl.ds(pl.multiple_of(tile * TILE, TILE), TILE)
        target = pl.ds(pl.multiple_of(i * TILE, TILE), TILE)
        for j in range(rows):

            @pl.when(piece == j)
            def _():
                pltpu.make_async_copy(pieces[j].at[source, :], out.at[target, :], sem).start()

        return carry

    lax.fori_loop(0, TILES, step, 0)
    pltpu.make_async_copy(out, out, sem).wait()


def pick(place, table, pieces, turn):
    rows = len(pieces)
    width = pieces[0].shape[1]
    return pl.pallas_call(
        functools.partial(pick_kernel, rows, pieces[0].shape[0] // S, turn),
        out_shape=jax.ShapeDtypeStruct((S, width), jnp.bfloat16),
        in_specs=[SMEM, SMEM] + [ANY] * rows,
        out_specs=VMEM,
        scratch_shapes=[pltpu.SemaphoreType.DMA],
        compiler_params=params(),
        cost_estimate=cost(0, 4 * S * width),
    )(place, table, *pieces)


def spread_kernel(rows, per_row, total, place, lengths, bins, starts, *refs):
    pieces, out = refs[:total], refs[total]
    row = place[0]
    width = out.shape[1]
    for a in range(per_row):
        request = row * per_row + a
        length = lengths[a]
        b = bins[request]
        start = starts[request]
        turn = b // rows
        index = lax.bitwise_xor(b - turn * rows, row) + turn * rows
        tiles = (length + (TILE - 1)) // TILE

        def blank(i, carry):
            out[pl.ds(pl.multiple_of(a * S + i * TILE, TILE), TILE), :] = jnp.zeros((TILE, width), jnp.bfloat16)
            return carry

        lax.fori_loop(tiles, TILES, blank, 0)
        for j in range(total):

            @pl.when(index == j)
            def _():
                def move(i, carry):
                    values = pieces[j][pl.ds(pl.multiple_of((start + i) * TILE, TILE), TILE), :]
                    position = i * TILE + lax.broadcasted_iota(jnp.int32, (TILE, width), 0)
                    kept = jnp.where(position < length, values.astype(jnp.float32), 0.0)
                    out[pl.ds(pl.multiple_of(a * S + i * TILE, TILE), TILE), :] = kept.astype(jnp.bfloat16)
                    return carry

                lax.fori_loop(0, tiles, move, 0)


def spread(place, lengths, bins, starts, pieces, rows, per_row):
    width = pieces[0].shape[1]
    return pl.pallas_call(
        functools.partial(spread_kernel, rows, per_row, len(pieces)),
        out_shape=jax.ShapeDtypeStruct((per_row * S, width), jnp.bfloat16),
        in_specs=[SMEM] * 4 + [VMEM] * len(pieces),
        out_specs=VMEM,
        compiler_params=params(),
        cost_estimate=cost(0, 2 * S * width * (len(pieces) + per_row)),
    )(place, lengths, bins, starts, *pieces)


DOT = functools.partial(jnp.dot, preferred_element_type=jnp.float32)


def flatten(parts):
    return [part for entry in parts for part in entry], tuple(len(entry) for entry in parts)


def read_parts(refs, counts):
    at = 0
    for count in counts:
        block = refs[at][...]
        for other in refs[at + 1 : at + count]:
            block = block + other[...]
        at += count
        yield block


def silu(values):
    return values * (1.0 / (1.0 + jnp.exp(-values)))


def retain_kernel(rows, counts, heads, place, decays, cosine, sine, seg_col, seg_row, *refs):
    cols, number = len(counts), sum(counts)
    tokens, weights = refs[:number], refs[number : number + rows]
    mixed, normed, gathered, sems = refs[number + rows :]
    depth = D // rows
    width = D // cols
    parts = ((0, 2 * KEY), (2 * KEY, VAL), (2 * KEY + VAL, VAL))

    for head in range(heads):
        for i, (low, size) in enumerate(parts):
            columns = pl.ds(head * HEAD_WIDTH + low, size)
            for j in range(rows):
                where = pl.ds(pl.multiple_of(lax.bitwise_xor(place[0], j) * depth, depth), depth)
                pltpu.make_async_copy(
                    weights[j].at[:, columns], gathered.at[where, columns], sems.at[head * 3 + i]
                ).start()

    total = jnp.zeros((S, 1), jnp.float32)
    for block in read_parts(tokens, counts):
        values = block.astype(jnp.float32)
        total += jnp.sum(values * values, axis=1, keepdims=True)
    scale = lax.rsqrt(total / D + epsilon)
    for k, block in enumerate(read_parts(tokens, counts)):
        where = pl.ds(pl.multiple_of(lax.bitwise_xor(place[1], k) * width, width), width)
        normed[:, where] = (block.astype(jnp.float32) * scale).astype(jnp.bfloat16)

    def project(head, i):
        low, size = parts[i]
        columns = pl.ds(head * HEAD_WIDTH + low, size)
        view = gathered.at[:, columns]
        pltpu.make_async_copy(view, view, sems.at[head * 3 + i]).wait()
        return DOT(normed[...], gathered[:, columns]).astype(jnp.bfloat16)

    def rotate(values):
        values = values.astype(jnp.float32)
        first, second = values[:, : KEY // 2], values[:, KEY // 2 :]
        cos, sin = cosine[...], sine[...]
        return jnp.concatenate([first * cos - second * sin, first * sin + second * cos], axis=1)

    lag = lax.broadcasted_iota(jnp.int32, (S, S), 0) - lax.broadcasted_iota(jnp.int32, (S, S), 1)
    allowed = (lag >= 0) & (seg_col[...] == seg_row[...])
    span = jnp.where(allowed, lag.astype(jnp.float32), 1e6)
    for head in range(heads):
        both = project(head, 0)
        query = rotate(both[:, :KEY]).astype(jnp.bfloat16)
        keyed = (rotate(both[:, KEY:]) * (1.0 / math.sqrt(KEY))).astype(jnp.bfloat16)
        scores = lax.dot_general(query, keyed, (((1,), (1,)), ((), ())), preferred_element_type=jnp.float32)
        scores = scores * jnp.exp(span * decays[head])
        denom = jnp.sum(scores, axis=1, keepdims=True)
        value = project(head, 1)
        retained = DOT(scores.astype(jnp.bfloat16), value) / jnp.maximum(jnp.abs(denom), 1.0)
        centred = retained - jnp.mean(retained, axis=1, keepdims=True)
        spread_of = jnp.mean(centred * centred, axis=1, keepdims=True)
        grouped = centred * lax.rsqrt(spread_of + epsilon)
        gate = project(head, 2).astype(jnp.float32)
        mixed[:, head * VAL : (head + 1) * VAL] = (silu(gate) * grouped).astype(jnp.bfloat16)


def retain(place, decays, cosine, sine, seg_col, seg_row, tokens, weights):
    rows, cols = len(weights), len(tokens)
    heads = HEADS // cols
    flat, counts = flatten(tokens)
    return pl.pallas_call(
        functools.partial(retain_kernel, rows, counts, heads),
        out_shape=jax.ShapeDtypeStruct((S, heads * VAL), jnp.bfloat16),
        in_specs=[SMEM, SMEM] + [VMEM] * (4 + len(flat)) + [ANY] * rows,
        out_specs=VMEM,
        scratch_shapes=[
            pltpu.VMEM((S, D), jnp.bfloat16),
            pltpu.VMEM((D, heads * HEAD_WIDTH), jnp.bfloat16),
            pltpu.SemaphoreType.DMA((heads * 3,)),
        ],
        compiler_params=params(),
        cost_estimate=cost(2 * S * D * HEAD_WIDTH * heads * 1.3, 2 * D * HEAD_WIDTH * heads),
    )(place, decays, cosine, sine, seg_col, seg_row, *flat, *weights)


def load_terms(rows, cols, place, weights, gathered, sems):
    ratio = rows // cols
    for j in range(rows):
        owner = lax.bitwise_xor(place[0], j)
        target = owner // ratio
        slot = lax.bitwise_xor(target, place[1]) * ratio + (owner - target * ratio)
        pltpu.make_async_copy(weights[j], gathered.at[slot], sems.at[slot]).start()


def put_terms(rows, cols, left, gathered, sems, outs):
    ratio = rows // cols
    depth = D // rows
    for slot in range(rows):
        view = gathered.at[slot]
        pltpu.make_async_copy(view, view, sems.at[slot]).wait()
        k, i = slot // ratio, slot % ratio
        outs[k][:, i * depth : (i + 1) * depth] = DOT(left, view[...]).astype(jnp.bfloat16)


def mix_kernel(rows, cols, place, mixed, *refs):
    weights, outs = refs[:rows], refs[rows : rows + cols]
    gathered, sems = refs[rows + cols :]
    load_terms(rows, cols, place, weights, gathered, sems)
    put_terms(rows, cols, mixed[...], gathered, sems, outs)


def mix(place, mixed, weights, cols):
    rows = len(weights)
    width = D // cols
    return pl.pallas_call(
        functools.partial(mix_kernel, rows, cols),
        out_shape=[jax.ShapeDtypeStruct((S, width), jnp.bfloat16)] * cols,
        in_specs=[SMEM, VMEM] + [ANY] * rows,
        out_specs=[VMEM] * cols,
        scratch_shapes=[
            pltpu.VMEM((rows,) + weights[0].shape, jnp.bfloat16),
            pltpu.SemaphoreType.DMA((rows,)),
        ],
        compiler_params=params(),
        cost_estimate=cost(2 * S * D * mixed.shape[1], 2 * D * mixed.shape[1]),
    )(place, mixed, *weights)


def feed_kernel(rows, counts, tile, place, *refs):
    cols, number = len(counts), sum(counts)
    tokens = refs[:number]
    pairs = refs[number : number + rows]
    downs = refs[number + rows : number + 2 * rows]
    outs = refs[number + 2 * rows : number + 2 * rows + cols]
    ordered, hidden, gathered, gathered_down, sems, sems_down = refs[number + 2 * rows + cols :]
    depth = D // rows
    width = D // cols
    steps = gathered.shape[2] // tile

    for step in range(steps):
        columns = pl.ds(step * tile, tile)
        for j in range(rows):
            where = pl.ds(pl.multiple_of(lax.bitwise_xor(place[0], j) * depth, depth), depth)
            pltpu.make_async_copy(
                pairs[j].at[:, :, columns], gathered.at[:, where, columns], sems.at[step]
            ).start()
    load_terms(rows, cols, place, downs, gathered_down, sems_down)

    total = jnp.zeros((S, 1), jnp.float32)
    for k, block in enumerate(read_parts(tokens, counts)):
        values = block.astype(jnp.float32)
        total += jnp.sum(values * values, axis=1, keepdims=True)
        where = pl.ds(pl.multiple_of(lax.bitwise_xor(place[1], k) * width, width), width)
        ordered[:, where] = block
    scale = lax.rsqrt(total / D + epsilon)

    for step in range(steps):
        columns = pl.ds(step * tile, tile)
        view = gathered.at[:, :, columns]
        pltpu.make_async_copy(view, view, sems.at[step]).wait()
        gate = DOT(ordered[...], gathered[0, :, columns]) * scale
        up = DOT(ordered[...], gathered[1, :, columns]) * scale
        hidden[:, columns] = (silu(gate) * up).astype(jnp.bfloat16)
    put_terms(rows, cols, hidden[...], gathered_down, sems_down, outs)


def feed(place, tokens, gateups, downs):
    rows, cols = len(gateups), len(tokens)
    units = gateups[0].shape[2]
    tile = min(units, 512)
    flat, counts = flatten(tokens)
    return pl.pallas_call(
        functools.partial(feed_kernel, rows, counts, tile),
        out_shape=[jax.ShapeDtypeStruct((S, D // cols), jnp.bfloat16)] * cols,
        in_specs=[SMEM] + [VMEM] * len(flat) + [ANY] * (2 * rows),
        out_specs=[VMEM] * cols,
        scratch_shapes=[
            pltpu.VMEM((S, D), jnp.bfloat16),
            pltpu.VMEM((S, units), jnp.bfloat16),
            pltpu.VMEM((2, D, units), jnp.bfloat16),
            pltpu.VMEM((rows,) + downs[0].shape, jnp.bfloat16),
            pltpu.SemaphoreType.DMA((units // tile,)),
            pltpu.SemaphoreType.DMA((rows,)),
        ],
        compiler_params=params(),
        cost_estimate=cost(6 * S * D * units, 6 * D * units),
    )(place, *flat, *gateups, *downs)


def shards(hidden_states, lengths, qkvg_master, gateup_master, out_master, down_master):
    rows, cols = lax.axis_size("row"), lax.axis_size("col")
    per_row = lengths.shape[0]
    heads = HEADS // cols
    place = jnp.stack([lax.axis_index("row"), lax.axis_index("col")]).astype(jnp.int32)

    all_lengths = gather_lengths(lengths)
    everyone = gather_rows(hidden_states)

    depth = qkvg_master.shape[0]
    units = gateup_master.shape[2] // cols
    qkvg_cut = cut((depth, heads * HEAD_WIDTH), place, qkvg_master)
    qkvg_parts = exchange(qkvg_cut)
    (qkvg_blocks,) = join("qkvg", qkvg_parts, place)
    qkvg_pieces = gather_rows(qkvg_blocks)

    out_cut = cut((depth, units), place, out_master.T)
    out_cut = list(after(tuple(out_cut), *qkvg_parts[1:]))
    out_parts = exchange(out_cut)
    (out_blocks,) = join("out", out_parts, place)
    out_pieces = gather_rows(after(out_blocks, qkvg_pieces[2], qkvg_pieces[4]))

    table, bins, starts, count = pack(place, all_lengths, rows)

    head_ids = lax.axis_index("col") * heads + jnp.arange(heads)
    decays = jnp.log1p(-jnp.power(2.0, -5.0 - head_ids.astype(jnp.float32)))
    freq = jnp.power(10000.0, -2.0 * jnp.arange(KEY // 2).astype(jnp.float32) / KEY)

    def begin(turn):
        codes = table[turn * TILES : (turn + 1) * TILES]
        segments = jnp.where(codes < 0, -1, codes // TILES)
        seg = jnp.broadcast_to(segments[:, None], (TILES, TILE)).reshape(S)
        positions = ((jnp.maximum(codes, 0) % TILES)[:, None] * TILE + jnp.arange(TILE)[None, :]).reshape(S)
        angle = positions.astype(jnp.float32)[:, None] * freq[None, :]
        own = pick(place, table, everyone, turn)
        return own, (jnp.cos(angle), jnp.sin(angle), seg[:, None], seg[None, :])

    own, tables = begin(0)
    tokens = gather_cols(own)

    feed_cut = cut((3, depth, units), place, down_master.T, gateup_master)
    feed_cut = list(after(tuple(feed_cut), *[part for entry in tokens[1:] for part in entry]))
    gateup_blocks, down_blocks = join("feed", exchange(feed_cut), place)
    gateup_pieces = gather_rows(after(gateup_blocks, out_pieces[2], out_pieces[4]))
    down_pieces = gather_rows(after(down_blocks, gateup_pieces[2], gateup_pieces[4]))

    def layer(own, tables, tokens):
        mixed = retain(place, decays, *tables, tokens, qkvg_pieces)
        residual = own.astype(jnp.float32) + collect(mix(place, mixed, out_pieces, cols))
        terms = feed(place, gather_cols(residual.astype(jnp.bfloat16)), gateup_pieces, down_pieces)
        return gather_rows((residual + collect(terms)).astype(jnp.bfloat16), direct=True)

    first = layer(own, tables, tokens)

    def finish(pieces):
        return spread(place, lengths, bins, starts, pieces, rows, per_row)

    def more(pieces):
        for turn in range(1, per_row):
            own, tables = begin(turn)
            pieces = pieces + layer(own, tables, gather_cols(own))
        return finish(pieces)

    layer_output = lax.cond(count[0] > rows, more, finish, first)
    return (layer_output, qkvg_blocks, gateup_blocks, out_blocks, down_blocks)


def solution(mesh):
    return jax.shard_map(
        shards,
        mesh=mesh,
        in_specs=(
            P("row", "col"),
            P("row"),
            P(("row", "col"), None),
            P(None, ("row", "col"), None),
            P(None, ("row", "col")),
            P(None, ("row", "col")),
        ),
        out_specs=(
            P("row", "col"),
            P("row", "col"),
            P(None, "row", "col"),
            P("col", "row"),
            P("col", "row"),
        ),
        check_vma=False,
    )
```

```python
import functools
import math

import jax
import jax.numpy as jnp
from jax import lax
from jax.experimental import pallas as pl
from jax.experimental.pallas import tpu as pltpu
from jax.sharding import PartitionSpec as P

D = 2048
HEADS = 8
KEY = 256
VAL = 512
S = 512
TILE = 16
TILES = S // TILE
HEAD_WIDTH = 2 * KEY + 2 * VAL

epsilon = 1e-05
VMEM_LIMIT = 56 * 1024 * 1024

SMEM = pl.BlockSpec(memory_space=pltpu.SMEM)
VMEM = pl.BlockSpec(memory_space=pltpu.VMEM)
ANY = pl.BlockSpec(memory_space=pl.ANY)


def params():
    return pltpu.CompilerParams(vmem_limit_bytes=VMEM_LIMIT)


def cost(flops, moved):
    return pl.CostEstimate(flops=int(flops), bytes_accessed=int(moved), transcendentals=0)


def swap(block, axis, step):
    size = lax.axis_size(axis)
    return lax.ppermute(block, axis, [(i, i ^ step) for i in range(size)])


def after(value, *earlier):
    return lax.optimization_barrier((value,) + earlier)[0]


def gather_rows(block, direct=False, behind=()):
    size = lax.axis_size("row")
    pieces = {0: block}
    if size == 8:
        half = block.shape[0] // 2
        pieces[2] = swap(block, "row", 2)
        pieces[4] = swap(block, "row", 4)
        if direct:
            pieces[6] = swap(block, "row", 6)
        else:
            across, along = pieces[2], pieces[4]
            if behind:
                across, along = after((across, along), *behind)
            upper = swap(along[:half], "row", 2)
            lower = swap(across[half:], "row", 4)
            pieces[6] = jnp.concatenate([upper, lower], axis=0)
        bits = [1]
    else:
        bits = [1 << i for i in reversed(range(size.bit_length() - 1))]
    for bit in bits:
        for j in sorted(pieces):
            pieces[j | bit] = swap(pieces[j], "row", bit)
    return [pieces[j] for j in range(size)]


def last_parts(pieces):
    return (pieces[6], pieces[1], pieces[3], pieces[5]) if len(pieces) == 8 else (pieces[-1],)


def gather_lengths(lengths):
    size = lax.axis_size("row")
    bit = 1
    while bit < size:
        lengths = jnp.concatenate([lengths, swap(lengths, "row", bit)])
        bit *= 2
    return lengths


def exchange(blocks):
    return [blocks[0]] + [swap(blocks[k], "col", k) for k in range(1, len(blocks))]


def gather_cols(block):
    size = lax.axis_size("col")
    if size != 4:
        return [(block,)] + [(swap(block, "col", k),) for k in range(1, size)]
    near = swap(block, "col", 1)
    far = swap(block, "col", 2)
    middle = lax.ppermute(block, "col", [(1, 2), (2, 1)])
    ends = lax.ppermute(far, "col", [(2, 3), (1, 0)])
    return [(block,), (near,), (far,), (middle, ends)]


def collect(terms):
    size = lax.axis_size("col")
    if size != 4:
        parts = exchange(terms)
    else:
        ends = lax.ppermute(terms[3], "col", [(3, 2), (0, 1)])
        near = swap(terms[1], "col", 1)
        middle = lax.ppermute(terms[3], "col", [(1, 2), (2, 1)])
        both = terms[2].astype(jnp.float32) + ends.astype(jnp.float32)
        far = swap(both.astype(jnp.bfloat16), "col", 2)
        parts = [terms[0], near, far, middle]
    return sum(part.astype(jnp.float32) for part in parts)


def cut_kernel(cols, place, *refs):
    masters, outs = refs[:-cols], refs[-cols:]
    width = outs[0].shape[-1]
    for k in range(cols):
        target = lax.bitwise_xor(place[1], k)
        columns = pl.ds(pl.multiple_of(target * width, 128), width)
        if len(masters) == 1:
            outs[k][...] = masters[0][:, columns].astype(jnp.bfloat16)
        else:
            outs[k][0] = masters[0][:, columns].astype(jnp.bfloat16)
            outs[k][1] = masters[1][0, :, columns].astype(jnp.bfloat16)
            outs[k][2] = masters[1][1, :, columns].astype(jnp.bfloat16)


def cut(shape, place, *masters):
    cols = lax.axis_size("col")
    return pl.pallas_call(
        functools.partial(cut_kernel, cols),
        out_shape=[jax.ShapeDtypeStruct(shape, jnp.bfloat16)] * cols,
        in_specs=[SMEM] + [VMEM] * len(masters),
        out_specs=[VMEM] * cols,
        compiler_params=params(),
        cost_estimate=cost(0, 6 * math.prod(shape) * cols),
    )(place, *masters)


def turned(values):
    return values.astype(jnp.float32).T.astype(jnp.bfloat16)


def join_kernel(cols, kind, place, *refs):
    rows = refs[0].shape[-2]
    for k in range(cols):
        source = lax.bitwise_xor(place[1], k)
        where = pl.ds(pl.multiple_of(source * rows, 16), rows)
        if kind == "qkvg":
            refs[cols][where, :] = refs[k][...]
        elif kind == "out":
            refs[cols + 1][where, :] = refs[k][...]
        else:
            refs[cols + 2][where, :] = refs[k][0]
            refs[cols][0, where, :] = refs[k][1]
            refs[cols][1, where, :] = refs[k][2]
    if kind == "out":
        refs[cols][...] = turned(refs[cols + 1][...])
    elif kind == "feed":
        refs[cols + 1][...] = turned(refs[cols + 2][...])


def join(kind, blocks, place):
    cols = len(blocks)
    depth, width = blocks[0].shape[-2] * cols, blocks[0].shape[-1]
    shapes = {"qkvg": [(depth, width)], "out": [(width, depth)], "feed": [(2, depth, width), (width, depth)]}[kind]
    return pl.pallas_call(
        functools.partial(join_kernel, cols, kind),
        out_shape=[jax.ShapeDtypeStruct(shape, jnp.bfloat16) for shape in shapes],
        in_specs=[SMEM] + [VMEM] * cols,
        out_specs=[VMEM] * len(shapes),
        scratch_shapes=[] if kind == "qkvg" else [pltpu.VMEM((depth, width), jnp.bfloat16)],
        compiler_params=params(),
        cost_estimate=cost(0, 4 * math.prod(blocks[0].shape) * cols),
    )(place, *blocks)


def pack_kernel(requests, rows, passes, place, lengths, table, bins, starts, count, used):
    row = place[0]
    per_row = requests // rows

    def clear(i, carry):
        table[i] = -1
        return carry

    lax.fori_loop(0, passes * TILES, clear, 0)

    def clear_used(i, carry):
        used[i] = 0
        return carry

    lax.fori_loop(0, requests, clear_used, 0)

    def put(q, top):
        owner = q // per_row
        length = lengths[lax.bitwise_xor(owner, row) * per_row + (q - owner * per_row)]
        tiles = (length + (TILE - 1)) // TILE

        def look(i, best):
            b = requests - 1 - i
            return jnp.where(used[b] + tiles <= TILES, b, best)

        b = lax.fori_loop(0, requests, look, requests - 1)
        start = used[b]
        used[b] = start + tiles
        bins[q] = b
        starts[q] = start
        turn = b // rows

        @pl.when(b - turn * rows == row)
        def _():
            def note(i, carry):
                table[turn * TILES + start + i] = q * TILES + i
                return carry

            lax.fori_loop(0, tiles, note, 0)

        return jnp.maximum(top, b + 1)

    count[0] = lax.fori_loop(0, requests, put, 0)


def pack(place, lengths, rows):
    requests = lengths.shape[0]
    passes = requests // rows
    whole = lambda n: jax.ShapeDtypeStruct((n,), jnp.int32)
    return pl.pallas_call(
        functools.partial(pack_kernel, requests, rows, passes),
        out_shape=[whole(passes * TILES), whole(requests), whole(requests), whole(1)],
        in_specs=[SMEM, SMEM],
        out_specs=[SMEM] * 4,
        scratch_shapes=[pltpu.SMEM((requests,), jnp.int32)],
        compiler_params=params(),
    )(place, lengths)


def pick_kernel(rows, per_row, turn, place, table, *refs):
    pieces, out, sem = refs[:rows], refs[rows], refs[rows + 1]
    row = place[0]

    def step(i, carry):
        code = jnp.maximum(table[turn * TILES + i], 0)
        request = code // TILES
        owner = request // per_row
        tile = (request - owner * per_row) * TILES + (code - request * TILES)
        piece = lax.bitwise_xor(owner, row)
        source = pl.ds(pl.multiple_of(tile * TILE, TILE), TILE)
        target = pl.ds(pl.multiple_of(i * TILE, TILE), TILE)
        for j in range(rows):

            @pl.when(piece == j)
            def _():
                pltpu.make_async_copy(pieces[j].at[source, :], out.at[target, :], sem).start()

        return carry

    lax.fori_loop(0, TILES, step, 0)
    pltpu.make_async_copy(out, out, sem).wait()


def pick(place, table, pieces, turn):
    rows = len(pieces)
    width = pieces[0].shape[1]
    return pl.pallas_call(
        functools.partial(pick_kernel, rows, pieces[0].shape[0] // S, turn),
        out_shape=jax.ShapeDtypeStruct((S, width), jnp.bfloat16),
        in_specs=[SMEM, SMEM] + [ANY] * rows,
        out_specs=VMEM,
        scratch_shapes=[pltpu.SemaphoreType.DMA],
        compiler_params=params(),
        cost_estimate=cost(0, 4 * S * width),
    )(place, table, *pieces)


def spread_kernel(rows, per_row, total, place, lengths, bins, starts, *refs):
    pieces, out = refs[:total], refs[total]
    row = place[0]
    width = out.shape[1]
    for a in range(per_row):
        request = row * per_row + a
        length = lengths[a]
        b = bins[request]
        start = starts[request]
        turn = b // rows
        index = lax.bitwise_xor(b - turn * rows, row) + turn * rows
        tiles = (length + (TILE - 1)) // TILE

        def blank(i, carry):
            out[pl.ds(pl.multiple_of(a * S + i * TILE, TILE), TILE), :] = jnp.zeros((TILE, width), jnp.bfloat16)
            return carry

        lax.fori_loop(tiles, TILES, blank, 0)
        for j in range(total):

            @pl.when(index == j)
            def _():
                def move(i, carry):
                    values = pieces[j][pl.ds(pl.multiple_of((start + i) * TILE, TILE), TILE), :]
                    position = i * TILE + lax.broadcasted_iota(jnp.int32, (TILE, width), 0)
                    kept = jnp.where(position < length, values.astype(jnp.float32), 0.0)
                    out[pl.ds(pl.multiple_of(a * S + i * TILE, TILE), TILE), :] = kept.astype(jnp.bfloat16)
                    return carry

                lax.fori_loop(0, tiles, move, 0)


def spread(place, lengths, bins, starts, pieces, rows, per_row):
    width = pieces[0].shape[1]
    return pl.pallas_call(
        functools.partial(spread_kernel, rows, per_row, len(pieces)),
        out_shape=jax.ShapeDtypeStruct((per_row * S, width), jnp.bfloat16),
        in_specs=[SMEM] * 4 + [VMEM] * len(pieces),
        out_specs=VMEM,
        compiler_params=params(),
        cost_estimate=cost(0, 2 * S * width * (len(pieces) + per_row)),
    )(place, lengths, bins, starts, *pieces)


DOT = functools.partial(jnp.dot, preferred_element_type=jnp.float32)


def flatten(parts):
    return [part for entry in parts for part in entry], tuple(len(entry) for entry in parts)


def read_parts(refs, counts):
    at = 0
    for count in counts:
        block = refs[at][...]
        for other in refs[at + 1 : at + count]:
            block = block + other[...]
        at += count
        yield block


def silu(values):
    return values * (1.0 / (1.0 + jnp.exp(-values)))


def retain_kernel(rows, counts, heads, place, decays, cosine, sine, seg_col, seg_row, *refs):
    cols, number = len(counts), sum(counts)
    tokens, weights = refs[:number], refs[number : number + rows]
    mixed, normed, gathered, sems = refs[number + rows :]
    depth = D // rows
    width = D // cols
    parts = ((0, 2 * KEY), (2 * KEY, VAL), (2 * KEY + VAL, VAL))

    for head in range(heads):
        for i, (low, size) in enumerate(parts):
            columns = pl.ds(head * HEAD_WIDTH + low, size)
            for j in range(rows):
                where = pl.ds(pl.multiple_of(lax.bitwise_xor(place[0], j) * depth, depth), depth)
                pltpu.make_async_copy(
                    weights[j].at[:, columns], gathered.at[where, columns], sems.at[head * 3 + i]
                ).start()

    total = jnp.zeros((S, 1), jnp.float32)
    for block in read_parts(tokens, counts):
        values = block.astype(jnp.float32)
        total += jnp.sum(values * values, axis=1, keepdims=True)
    scale = lax.rsqrt(total / D + epsilon)
    for k, block in enumerate(read_parts(tokens, counts)):
        where = pl.ds(pl.multiple_of(lax.bitwise_xor(place[1], k) * width, width), width)
        normed[:, where] = (block.astype(jnp.float32) * scale).astype(jnp.bfloat16)

    def project(head, i):
        low, size = parts[i]
        columns = pl.ds(head * HEAD_WIDTH + low, size)
        view = gathered.at[:, columns]
        pltpu.make_async_copy(view, view, sems.at[head * 3 + i]).wait()
        return DOT(normed[...], gathered[:, columns]).astype(jnp.bfloat16)

    def rotate(values):
        values = values.astype(jnp.float32)
        first, second = values[:, : KEY // 2], values[:, KEY // 2 :]
        cos, sin = cosine[...], sine[...]
        return jnp.concatenate([first * cos - second * sin, first * sin + second * cos], axis=1)

    lag = lax.broadcasted_iota(jnp.int32, (S, S), 0) - lax.broadcasted_iota(jnp.int32, (S, S), 1)
    allowed = (lag >= 0) & (seg_col[...] == seg_row[...])
    span = jnp.where(allowed, lag.astype(jnp.float32), 1e6)
    for head in range(heads):
        both = project(head, 0)
        query = rotate(both[:, :KEY]).astype(jnp.bfloat16)
        keyed = (rotate(both[:, KEY:]) * (1.0 / math.sqrt(KEY))).astype(jnp.bfloat16)
        scores = lax.dot_general(query, keyed, (((1,), (1,)), ((), ())), preferred_element_type=jnp.float32)
        scores = scores * jnp.exp(span * decays[head])
        denom = jnp.sum(scores, axis=1, keepdims=True)
        value = project(head, 1)
        retained = DOT(scores.astype(jnp.bfloat16), value) / jnp.maximum(jnp.abs(denom), 1.0)
        centred = retained - jnp.mean(retained, axis=1, keepdims=True)
        spread_of = jnp.mean(centred * centred, axis=1, keepdims=True)
        grouped = centred * lax.rsqrt(spread_of + epsilon)
        gate = project(head, 2).astype(jnp.float32)
        mixed[:, head * VAL : (head + 1) * VAL] = (silu(gate) * grouped).astype(jnp.bfloat16)


def retain(place, decays, cosine, sine, seg_col, seg_row, tokens, weights):
    rows, cols = len(weights), len(tokens)
    heads = HEADS // cols
    flat, counts = flatten(tokens)
    return pl.pallas_call(
        functools.partial(retain_kernel, rows, counts, heads),
        out_shape=jax.ShapeDtypeStruct((S, heads * VAL), jnp.bfloat16),
        in_specs=[SMEM, SMEM] + [VMEM] * (4 + len(flat)) + [ANY] * rows,
        out_specs=VMEM,
        scratch_shapes=[
            pltpu.VMEM((S, D), jnp.bfloat16),
            pltpu.VMEM((D, heads * HEAD_WIDTH), jnp.bfloat16),
            pltpu.SemaphoreType.DMA((heads * 3,)),
        ],
        compiler_params=params(),
        cost_estimate=cost(2 * S * D * HEAD_WIDTH * heads * 1.3, 2 * D * HEAD_WIDTH * heads),
    )(place, decays, cosine, sine, seg_col, seg_row, *flat, *weights)


def load_terms(rows, cols, place, weights, gathered, sem):
    ratio = rows // cols
    for j in range(rows):
        owner = lax.bitwise_xor(place[0], j)
        target = owner // ratio
        slot = lax.bitwise_xor(target, place[1]) * ratio + (owner - target * ratio)
        pltpu.make_async_copy(weights[j], gathered.at[slot], sem).start()


def put_terms(rows, cols, left, gathered, sem, outs):
    ratio = rows // cols
    depth = D // rows
    pltpu.make_async_copy(gathered, gathered, sem).wait()
    for slot in range(rows):
        k, i = slot // ratio, slot % ratio
        outs[k][:, i * depth : (i + 1) * depth] = DOT(left, gathered[slot]).astype(jnp.bfloat16)


def mix_kernel(rows, cols, place, mixed, *refs):
    weights, outs = refs[:rows], refs[rows : rows + cols]
    gathered, sem = refs[rows + cols :]
    load_terms(rows, cols, place, weights, gathered, sem)
    put_terms(rows, cols, mixed[...], gathered, sem, outs)


def mix(place, mixed, weights, cols):
    rows = len(weights)
    width = D // cols
    return pl.pallas_call(
        functools.partial(mix_kernel, rows, cols),
        out_shape=[jax.ShapeDtypeStruct((S, width), jnp.bfloat16)] * cols,
        in_specs=[SMEM, VMEM] + [ANY] * rows,
        out_specs=[VMEM] * cols,
        scratch_shapes=[
            pltpu.VMEM((rows,) + weights[0].shape, jnp.bfloat16),
            pltpu.SemaphoreType.DMA,
        ],
        compiler_params=params(),
        cost_estimate=cost(2 * S * D * mixed.shape[1], 2 * D * mixed.shape[1]),
    )(place, mixed, *weights)


def feed_kernel(rows, counts, tile, place, *refs):
    cols, number = len(counts), sum(counts)
    tokens = refs[:number]
    pairs = refs[number : number + rows]
    downs = refs[number + rows : number + 2 * rows]
    outs = refs[number + 2 * rows : number + 2 * rows + cols]
    ordered, hidden, gathered, gathered_down, sems, sem_down = refs[number + 2 * rows + cols :]
    depth = D // rows
    width = D // cols
    steps = gathered.shape[2] // tile

    for step in range(steps):
        columns = pl.ds(step * tile, tile)
        for j in range(rows):
            where = pl.ds(pl.multiple_of(lax.bitwise_xor(place[0], j) * depth, depth), depth)
            pltpu.make_async_copy(
                pairs[j].at[:, :, columns], gathered.at[:, where, columns], sems.at[step]
            ).start()
    load_terms(rows, cols, place, downs, gathered_down, sem_down)

    total = jnp.zeros((S, 1), jnp.float32)
    for k, block in enumerate(read_parts(tokens, counts)):
        values = block.astype(jnp.float32)
        total += jnp.sum(values * values, axis=1, keepdims=True)
        where = pl.ds(pl.multiple_of(lax.bitwise_xor(place[1], k) * width, width), width)
        ordered[:, where] = block
    scale = lax.rsqrt(total / D + epsilon)

    for step in range(steps):
        columns = pl.ds(step * tile, tile)
        view = gathered.at[:, :, columns]
        pltpu.make_async_copy(view, view, sems.at[step]).wait()
        gate = DOT(ordered[...], gathered[0, :, columns]) * scale
        up = DOT(ordered[...], gathered[1, :, columns]) * scale
        hidden[:, columns] = (silu(gate) * up).astype(jnp.bfloat16)
    put_terms(rows, cols, hidden[...], gathered_down, sem_down, outs)


def feed(place, tokens, gateups, downs):
    rows, cols = len(gateups), len(tokens)
    units = gateups[0].shape[2]
    tile = min(units, 512)
    flat, counts = flatten(tokens)
    return pl.pallas_call(
        functools.partial(feed_kernel, rows, counts, tile),
        out_shape=[jax.ShapeDtypeStruct((S, D // cols), jnp.bfloat16)] * cols,
        in_specs=[SMEM] + [VMEM] * len(flat) + [ANY] * (2 * rows),
        out_specs=[VMEM] * cols,
        scratch_shapes=[
            pltpu.VMEM((S, D), jnp.bfloat16),
            pltpu.VMEM((S, units), jnp.bfloat16),
            pltpu.VMEM((2, D, units), jnp.bfloat16),
            pltpu.VMEM((rows,) + downs[0].shape, jnp.bfloat16),
            pltpu.SemaphoreType.DMA((units // tile,)),
            pltpu.SemaphoreType.DMA,
        ],
        compiler_params=params(),
        cost_estimate=cost(6 * S * D * units, 6 * D * units),
    )(place, *flat, *gateups, *downs)


def shards(hidden_states, lengths, qkvg_master, gateup_master, out_master, down_master):
    rows, cols = lax.axis_size("row"), lax.axis_size("col")
    per_row = lengths.shape[0]
    heads = HEADS // cols
    place = jnp.stack([lax.axis_index("row"), lax.axis_index("col")]).astype(jnp.int32)

    all_lengths = gather_lengths(lengths)
    depth = qkvg_master.shape[0]
    units = gateup_master.shape[2] // cols
    qkvg_parts = exchange(cut((depth, heads * HEAD_WIDTH), place, qkvg_master))
    everyone = gather_rows(after(hidden_states, all_lengths), behind=(qkvg_parts[1],))
    (qkvg_blocks,) = join("qkvg", qkvg_parts, place)
    out_cut = cut((depth, units), place, out_master.T)
    out_parts = exchange(list(after(tuple(out_cut), *qkvg_parts[1:])))
    (out_blocks,) = join("out", out_parts, place)

    table, bins, starts, count = pack(place, all_lengths, rows)

    head_ids = lax.axis_index("col") * heads + jnp.arange(heads)
    decays = jnp.log1p(-jnp.power(2.0, -5.0 - head_ids.astype(jnp.float32)))
    freq = jnp.power(10000.0, -2.0 * jnp.arange(KEY // 2).astype(jnp.float32) / KEY)

    def begin(turn):
        codes = table[turn * TILES : (turn + 1) * TILES]
        segments = jnp.where(codes < 0, -1, codes // TILES)
        seg = jnp.broadcast_to(segments[:, None], (TILES, TILE)).reshape(S)
        positions = ((jnp.maximum(codes, 0) % TILES)[:, None] * TILE + jnp.arange(TILE)[None, :]).reshape(S)
        angle = positions.astype(jnp.float32)[:, None] * freq[None, :]
        own = pick(place, table, everyone, turn)
        return own, (jnp.cos(angle), jnp.sin(angle), seg[:, None], seg[None, :])

    table = after(table, *out_parts[1:])
    own, tables = begin(0)
    tokens = gather_cols(own)
    qkvg_pieces = gather_rows(after(qkvg_blocks, *last_parts(everyone)), behind=[entry[0] for entry in tokens[1:]] + out_parts[1:])
    out_pieces = gather_rows(after(out_blocks, *last_parts(qkvg_pieces)), direct=True)

    feed_cut = cut((3, depth, units), place, down_master.T, gateup_master)
    behind = [part for entry in tokens[1:] for part in entry] + qkvg_pieces[1:]
    feed_parts = exchange(list(after(tuple(feed_cut), *behind)))

    mixed = retain(place, decays, *tables, tokens, qkvg_pieces)

    gateup_blocks, down_blocks = join("feed", list(after(tuple(feed_parts), mixed)), place)
    gateup_pieces = gather_rows(gateup_blocks)
    down_pieces = gather_rows(after(down_blocks, *last_parts(gateup_pieces)), direct=True)

    def layer(own, mixed):
        residual = own.astype(jnp.float32) + collect(mix(place, mixed, out_pieces, cols))
        terms = feed(place, gather_cols(residual.astype(jnp.bfloat16)), gateup_pieces, down_pieces)
        return gather_rows((residual + collect(terms)).astype(jnp.bfloat16), direct=True)

    first = layer(own, mixed)

    def finish(pieces):
        return spread(place, lengths, bins, starts, pieces, rows, per_row)

    def more(pieces):
        for turn in range(1, per_row):
            own, tables = begin(turn)
            pieces = pieces + layer(own, retain(place, decays, *tables, gather_cols(own), qkvg_pieces))
        return finish(pieces)

    layer_output = lax.cond(count[0] > rows, more, finish, first)
    return (layer_output, qkvg_blocks, gateup_blocks, out_blocks, down_blocks)


def solution(mesh):
    return jax.shard_map(
        shards,
        mesh=mesh,
        in_specs=(
            P("row", "col"),
            P("row"),
            P(("row", "col"), None),
            P(None, ("row", "col"), None),
            P(None, ("row", "col")),
            P(None, ("row", "col")),
        ),
        out_specs=(
            P("row", "col"),
            P("row", "col"),
            P(None, "row", "col"),
            P("col", "row"),
            P("col", "row"),
        ),
        check_vma=False,
    )
```

```python
import functools
import math

import jax
import jax.numpy as jnp
from jax import lax
from jax.experimental import pallas as pl
from jax.experimental.pallas import tpu as pltpu
from jax.sharding import PartitionSpec as P

D = 2048
HEADS = 8
KEY = 256
VAL = 512
S = 512
TILE = 16
TILES = S // TILE
HEAD_WIDTH = 2 * KEY + 2 * VAL

epsilon = 1e-05
VMEM_LIMIT = 56 * 1024 * 1024

SMEM = pl.BlockSpec(memory_space=pltpu.SMEM)
VMEM = pl.BlockSpec(memory_space=pltpu.VMEM)
ANY = pl.BlockSpec(memory_space=pl.ANY)


def params():
    return pltpu.CompilerParams(vmem_limit_bytes=VMEM_LIMIT)


def cost(flops, moved):
    return pl.CostEstimate(flops=int(flops), bytes_accessed=int(moved), transcendentals=0)


def swap(block, axis, step):
    size = lax.axis_size(axis)
    return lax.ppermute(block, axis, [(i, i ^ step) for i in range(size)])


def after(value, *earlier):
    return lax.optimization_barrier((value,) + earlier)[0]


def gather_rows(block, direct=False, halves=(), whole=(), core=()):
    size = lax.axis_size("row")
    pieces = {0: block}
    if size == 8:
        axis = block.ndim - 2
        half = block.shape[axis] // 2
        pieces[2] = swap(block, "row", 2)
        pieces[4] = swap(block, "row", 4)
        if direct:
            pieces[6] = swap(block, "row", 6)
        else:
            across, along = after((pieces[2], pieces[4]), *halves)
            upper = swap(lax.slice_in_dim(along, 0, half, axis=axis), "row", 2)
            lower = swap(lax.slice_in_dim(across, half, 2 * half, axis=axis), "row", 4)
            pieces[6] = jnp.concatenate(after((upper, lower), *whole), axis=axis)
        pieces[0] = after(block, pieces[2], pieces[4])
        bits = [1]
    else:
        bits = [1 << i for i in reversed(range(size.bit_length() - 1))]
    for bit in bits:
        for j in sorted(pieces):
            pieces[j | bit] = swap(after(pieces[j], *core), "row", bit)
    return [pieces[j] for j in range(size)]


def last_parts(pieces):
    return (pieces[6],) if len(pieces) == 8 else (pieces[-1],)


def gather_lengths(lengths):
    size = lax.axis_size("row")
    bit = 1
    while bit < size:
        lengths = jnp.concatenate([lengths, swap(lengths, "row", bit)])
        bit *= 2
    return lengths


def exchange(blocks):
    return [blocks[0]] + [swap(blocks[k], "col", k) for k in range(1, len(blocks))]


def gather_cols(block):
    size = lax.axis_size("col")
    if size != 4:
        return [(block,)] + [(swap(block, "col", k),) for k in range(1, size)]
    near = swap(block, "col", 1)
    far = swap(block, "col", 2)
    middle = lax.ppermute(after(block, far), "col", [(1, 2), (2, 1)])
    ends = lax.ppermute(far, "col", [(2, 3), (1, 0)])
    return [(block,), (near,), (far,), (middle, ends)]


def collect(terms):
    if lax.axis_size("col") != 4:
        return exchange(terms)
    early = lax.ppermute(terms[3], "col", [(3, 2), (0, 1)])
    middle = lax.ppermute(terms[3], "col", [(1, 2), (2, 1)])
    near = swap(after(terms[1], early), "col", 1)
    both = terms[2].astype(jnp.float32) + early.astype(jnp.float32)
    far = swap(both.astype(jnp.bfloat16), "col", 2)
    return [terms[0], near, far, middle]


def added(parts):
    return sum(part.astype(jnp.float32) for part in parts)


def cut_front_kernel(cols, place, qkvg, out, *blocks):
    units = out.shape[1] // cols
    width = blocks[0].shape[1] - units
    for k in range(cols):
        target = lax.bitwise_xor(place[1], k)
        columns = pl.ds(pl.multiple_of(target * width, 128), width)
        blocks[k][:, :width] = qkvg[:, columns].astype(jnp.bfloat16)
        columns = pl.ds(pl.multiple_of(target * units, 128), units)
        blocks[k][:, width:] = out[:, columns].astype(jnp.bfloat16)


def cut_feed_kernel(cols, place, down, gateup, *blocks):
    units = blocks[0].shape[2]
    for k in range(cols):
        target = lax.bitwise_xor(place[1], k)
        columns = pl.ds(pl.multiple_of(target * units, 128), units)
        blocks[k][0] = down[:, columns].astype(jnp.bfloat16)
        blocks[k][1] = gateup[0, :, columns].astype(jnp.bfloat16)
        blocks[k][2] = gateup[1, :, columns].astype(jnp.bfloat16)


def cut(kernel, shape, place, *masters):
    cols = lax.axis_size("col")
    return pl.pallas_call(
        functools.partial(kernel, cols),
        out_shape=[jax.ShapeDtypeStruct(shape, jnp.bfloat16)] * cols,
        in_specs=[SMEM] + [VMEM] * len(masters),
        out_specs=[VMEM] * cols,
        compiler_params=params(),
        cost_estimate=cost(0, 6 * math.prod(shape) * cols),
    )(place, *masters)


def join_kernel(cols, place, *refs):
    out = refs[cols]
    rows = refs[0].shape[-2]
    for k in range(cols):
        source = lax.bitwise_xor(place[1], k)
        where = pl.ds(pl.multiple_of(source * rows, 16), rows)
        if len(out.shape) == 2:
            out[where, :] = refs[k][...]
        else:
            out[:, where, :] = refs[k][...]


def join(blocks, place):
    cols = len(blocks)
    shape = list(blocks[0].shape)
    shape[-2] *= cols
    return pl.pallas_call(
        functools.partial(join_kernel, cols),
        out_shape=jax.ShapeDtypeStruct(tuple(shape), jnp.bfloat16),
        in_specs=[SMEM] + [VMEM] * cols,
        out_specs=VMEM,
        compiler_params=params(),
        cost_estimate=cost(0, 4 * math.prod(shape)),
    )(place, *blocks)


def pack_kernel(requests, rows, passes, place, lengths, table, bins, starts, count, used):
    row = place[0]
    per_row = requests // rows

    def clear(i, carry):
        table[i] = -1
        return carry

    lax.fori_loop(0, passes * TILES, clear, 0)

    def clear_used(i, carry):
        used[i] = 0
        return carry

    lax.fori_loop(0, requests, clear_used, 0)

    def put(q, top):
        owner = q // per_row
        length = lengths[lax.bitwise_xor(owner, row) * per_row + (q - owner * per_row)]
        tiles = (length + (TILE - 1)) // TILE

        def look(i, best):
            b = requests - 1 - i
            return jnp.where(used[b] + tiles <= TILES, b, best)

        b = lax.fori_loop(0, requests, look, requests - 1)
        start = used[b]
        used[b] = start + tiles
        bins[q] = b
        starts[q] = start
        turn = b // rows

        @pl.when(b - turn * rows == row)
        def _():
            def note(i, carry):
                table[turn * TILES + start + i] = q * TILES + i
                return carry

            lax.fori_loop(0, tiles, note, 0)

        return jnp.maximum(top, b + 1)

    count[0] = lax.fori_loop(0, requests, put, 0)


def pack(place, lengths, rows):
    requests = lengths.shape[0]
    passes = requests // rows
    whole = lambda n: jax.ShapeDtypeStruct((n,), jnp.int32)
    return pl.pallas_call(
        functools.partial(pack_kernel, requests, rows, passes),
        out_shape=[whole(passes * TILES), whole(requests), whole(requests), whole(1)],
        in_specs=[SMEM, SMEM],
        out_specs=[SMEM] * 4,
        scratch_shapes=[pltpu.SMEM((requests,), jnp.int32)],
        compiler_params=params(),
    )(place, lengths)


def pick_kernel(rows, per_row, turn, place, table, *refs):
    pieces, out, sem = refs[:rows], refs[rows], refs[rows + 1]
    row = place[0]

    def step(i, carry):
        code = jnp.maximum(table[turn * TILES + i], 0)
        request = code // TILES
        owner = request // per_row
        tile = (request - owner * per_row) * TILES + (code - request * TILES)
        piece = lax.bitwise_xor(owner, row)
        source = pl.ds(pl.multiple_of(tile * TILE, TILE), TILE)
        target = pl.ds(pl.multiple_of(i * TILE, TILE), TILE)
        for j in range(rows):

            @pl.when(piece == j)
            def _():
                pltpu.make_async_copy(pieces[j].at[source, :], out.at[target, :], sem).start()

        return carry

    lax.fori_loop(0, TILES, step, 0)
    pltpu.make_async_copy(out, out, sem).wait()


def pick(place, table, pieces, turn):
    rows = len(pieces)
    width = pieces[0].shape[1]
    return pl.pallas_call(
        functools.partial(pick_kernel, rows, pieces[0].shape[0] // S, turn),
        out_shape=jax.ShapeDtypeStruct((S, width), jnp.bfloat16),
        in_specs=[SMEM, SMEM] + [ANY] * rows,
        out_specs=VMEM,
        scratch_shapes=[pltpu.SemaphoreType.DMA],
        compiler_params=params(),
        cost_estimate=cost(0, 4 * S * width),
    )(place, table, *pieces)


def spread_kernel(rows, per_row, total, place, lengths, bins, starts, *refs):
    pieces, out = refs[:total], refs[total]
    row = place[0]
    width = out.shape[1]
    for a in range(per_row):
        request = row * per_row + a
        length = lengths[a]
        b = bins[request]
        start = starts[request]
        turn = b // rows
        index = lax.bitwise_xor(b - turn * rows, row) + turn * rows
        tiles = (length + (TILE - 1)) // TILE

        def blank(i, carry):
            out[pl.ds(pl.multiple_of(a * S + i * TILE, TILE), TILE), :] = jnp.zeros((TILE, width), jnp.bfloat16)
            return carry

        lax.fori_loop(tiles, TILES, blank, 0)
        for j in range(total):

            @pl.when(index == j)
            def _():
                def move(i, carry):
                    values = pieces[j][pl.ds(pl.multiple_of((start + i) * TILE, TILE), TILE), :]
                    position = i * TILE + lax.broadcasted_iota(jnp.int32, (TILE, width), 0)
                    kept = jnp.where(position < length, values.astype(jnp.float32), 0.0)
                    out[pl.ds(pl.multiple_of(a * S + i * TILE, TILE), TILE), :] = kept.astype(jnp.bfloat16)
                    return carry

                lax.fori_loop(0, tiles, move, 0)


def spread(place, lengths, bins, starts, pieces, rows, per_row):
    width = pieces[0].shape[1]
    return pl.pallas_call(
        functools.partial(spread_kernel, rows, per_row, len(pieces)),
        out_shape=jax.ShapeDtypeStruct((per_row * S, width), jnp.bfloat16),
        in_specs=[SMEM] * 4 + [VMEM] * len(pieces),
        out_specs=VMEM,
        compiler_params=params(),
        cost_estimate=cost(0, 2 * S * width * (len(pieces) + per_row)),
    )(place, lengths, bins, starts, *pieces)


DOT = functools.partial(jnp.dot, preferred_element_type=jnp.float32)


def DOT_T(left, right):
    return lax.dot_general(left, right, (((1,), (1,)), ((), ())), preferred_element_type=jnp.float32)


def flatten(parts):
    return [part for entry in parts for part in entry], tuple(len(entry) for entry in parts)


def read_parts(refs, counts):
    at = 0
    for count in counts:
        block = refs[at][...]
        for other in refs[at + 1 : at + count]:
            block = block + other[...]
        at += count
        yield block


def silu(values):
    return values * (1.0 / (1.0 + jnp.exp(-values)))


def retain_kernel(rows, counts, heads, place, decays, cosine, sine, seg_col, seg_row, *refs):
    cols, number = len(counts), sum(counts)
    tokens, weights = refs[:number], refs[number : number + rows]
    mixed, normed, gathered, sems = refs[number + rows :]
    depth = D // rows
    width = D // cols
    parts = ((0, 2 * KEY), (2 * KEY, VAL), (2 * KEY + VAL, VAL))

    for head in range(heads):
        for i, (low, size) in enumerate(parts):
            columns = pl.ds(head * HEAD_WIDTH + low, size)
            for j in range(rows):
                where = pl.ds(pl.multiple_of(lax.bitwise_xor(place[0], j) * depth, depth), depth)
                pltpu.make_async_copy(
                    weights[j].at[:, columns], gathered.at[where, columns], sems.at[head * 3 + i]
                ).start()

    total = jnp.zeros((S, 1), jnp.float32)
    for block in read_parts(tokens, counts):
        values = block.astype(jnp.float32)
        total += jnp.sum(values * values, axis=1, keepdims=True)
    scale = lax.rsqrt(total / D + epsilon)
    for k, block in enumerate(read_parts(tokens, counts)):
        where = pl.ds(pl.multiple_of(lax.bitwise_xor(place[1], k) * width, width), width)
        normed[:, where] = (block.astype(jnp.float32) * scale).astype(jnp.bfloat16)

    def project(head, i):
        low, size = parts[i]
        columns = pl.ds(head * HEAD_WIDTH + low, size)
        view = gathered.at[:, columns]
        pltpu.make_async_copy(view, view, sems.at[head * 3 + i]).wait()
        return DOT(normed[...], gathered[:, columns]).astype(jnp.bfloat16)

    def rotate(values):
        values = values.astype(jnp.float32)
        first, second = values[:, : KEY // 2], values[:, KEY // 2 :]
        cos, sin = cosine[...], sine[...]
        return jnp.concatenate([first * cos - second * sin, first * sin + second * cos], axis=1)

    lag = lax.broadcasted_iota(jnp.int32, (S, S), 0) - lax.broadcasted_iota(jnp.int32, (S, S), 1)
    allowed = (lag >= 0) & (seg_col[...] == seg_row[...])
    span = jnp.where(allowed, lag.astype(jnp.float32), 1e6)
    for head in range(heads):
        both = project(head, 0)
        query = rotate(both[:, :KEY]).astype(jnp.bfloat16)
        keyed = (rotate(both[:, KEY:]) * (1.0 / math.sqrt(KEY))).astype(jnp.bfloat16)
        scores = DOT_T(query, keyed)
        scores = scores * jnp.exp(span * decays[head])
        denom = jnp.sum(scores, axis=1, keepdims=True)
        value = project(head, 1)
        retained = DOT(scores.astype(jnp.bfloat16), value) / jnp.maximum(jnp.abs(denom), 1.0)
        centred = retained - jnp.mean(retained, axis=1, keepdims=True)
        spread_of = jnp.mean(centred * centred, axis=1, keepdims=True)
        grouped = centred * lax.rsqrt(spread_of + epsilon)
        gate = project(head, 2).astype(jnp.float32)
        mixed[:, head * VAL : (head + 1) * VAL] = (silu(gate) * grouped).astype(jnp.bfloat16)


def retain(place, decays, cosine, sine, seg_col, seg_row, tokens, weights):
    rows, cols = len(weights), len(tokens)
    heads = HEADS // cols
    flat, counts = flatten(tokens)
    return pl.pallas_call(
        functools.partial(retain_kernel, rows, counts, heads),
        out_shape=jax.ShapeDtypeStruct((S, heads * VAL), jnp.bfloat16),
        in_specs=[SMEM, SMEM] + [VMEM] * (4 + len(flat)) + [ANY] * rows,
        out_specs=VMEM,
        scratch_shapes=[
            pltpu.VMEM((S, D), jnp.bfloat16),
            pltpu.VMEM((D, heads * HEAD_WIDTH), jnp.bfloat16),
            pltpu.SemaphoreType.DMA((heads * 3,)),
        ],
        compiler_params=params(),
        cost_estimate=cost(2 * S * D * HEAD_WIDTH * heads * 1.3, 2 * D * HEAD_WIDTH * heads),
    )(place, decays, cosine, sine, seg_col, seg_row, *flat, *weights)


def load_terms(rows, cols, place, views, gathered, sem):
    ratio = rows // cols
    for j in range(rows):
        owner = lax.bitwise_xor(place[0], j)
        target = owner // ratio
        slot = lax.bitwise_xor(target, place[1]) * ratio + (owner - target * ratio)
        pltpu.make_async_copy(views[j], gathered.at[slot], sem).start()


def put_terms(rows, cols, left, gathered, sem, outs):
    ratio = rows // cols
    depth = D // rows
    pltpu.make_async_copy(gathered, gathered, sem).wait()
    for slot in range(rows):
        k, i = slot // ratio, slot % ratio
        outs[k][:, i * depth : (i + 1) * depth] = DOT_T(left, gathered[slot]).astype(jnp.bfloat16)


def mix_kernel(rows, cols, place, mixed, *refs):
    weights, outs = refs[:rows], refs[rows : rows + cols]
    gathered, sem = refs[rows + cols :]
    units = mixed.shape[1]
    views = [ref.at[:, pl.ds(ref.shape[1] - units, units)] for ref in weights]
    load_terms(rows, cols, place, views, gathered, sem)
    put_terms(rows, cols, mixed[...], gathered, sem, outs)


def mix(place, mixed, weights, cols):
    rows = len(weights)
    width = D // cols
    return pl.pallas_call(
        functools.partial(mix_kernel, rows, cols),
        out_shape=[jax.ShapeDtypeStruct((S, width), jnp.bfloat16)] * cols,
        in_specs=[SMEM, VMEM] + [ANY] * rows,
        out_specs=[VMEM] * cols,
        scratch_shapes=[
            pltpu.VMEM((rows, D // rows, mixed.shape[1]), jnp.bfloat16),
            pltpu.SemaphoreType.DMA,
        ],
        compiler_params=params(),
        cost_estimate=cost(2 * S * D * mixed.shape[1], 2 * D * mixed.shape[1]),
    )(place, mixed, *weights)


def feed_kernel(rows, counts, tile, place, *refs):
    cols, number = len(counts), sum(counts)
    tokens = refs[:number]
    weights = refs[number : number + rows]
    outs = refs[number + rows : number + rows + cols]
    ordered, hidden, gathered, gathered_down, sems, sem_down = refs[number + rows + cols :]
    depth = D // rows
    width = D // cols
    steps = gathered.shape[2] // tile

    for step in range(steps):
        columns = pl.ds(step * tile, tile)
        for j in range(rows):
            where = pl.ds(pl.multiple_of(lax.bitwise_xor(place[0], j) * depth, depth), depth)
            pltpu.make_async_copy(
                weights[j].at[pl.ds(1, 2), :, columns], gathered.at[:, where, columns], sems.at[step]
            ).start()
    load_terms(rows, cols, place, [ref.at[0] for ref in weights], gathered_down, sem_down)

    total = jnp.zeros((S, 1), jnp.float32)
    for k, block in enumerate(read_parts(tokens, counts)):
        values = block.astype(jnp.float32)
        total += jnp.sum(values * values, axis=1, keepdims=True)
        where = pl.ds(pl.multiple_of(lax.bitwise_xor(place[1], k) * width, width), width)
        ordered[:, where] = block
    scale = lax.rsqrt(total / D + epsilon)

    for step in range(steps):
        columns = pl.ds(step * tile, tile)
        view = gathered.at[:, :, columns]
        pltpu.make_async_copy(view, view, sems.at[step]).wait()
        gate = DOT(ordered[...], gathered[0, :, columns]) * scale
        up = DOT(ordered[...], gathered[1, :, columns]) * scale
        hidden[:, columns] = (silu(gate) * up).astype(jnp.bfloat16)
    put_terms(rows, cols, hidden[...], gathered_down, sem_down, outs)


def feed(place, tokens, weights):
    rows, cols = len(weights), len(tokens)
    units = weights[0].shape[2]
    tile = min(units, 512)
    flat, counts = flatten(tokens)
    return pl.pallas_call(
        functools.partial(feed_kernel, rows, counts, tile),
        out_shape=[jax.ShapeDtypeStruct((S, D // cols), jnp.bfloat16)] * cols,
        in_specs=[SMEM] + [VMEM] * len(flat) + [ANY] * rows,
        out_specs=[VMEM] * cols,
        scratch_shapes=[
            pltpu.VMEM((S, D), jnp.bfloat16),
            pltpu.VMEM((S, units), jnp.bfloat16),
            pltpu.VMEM((2, D, units), jnp.bfloat16),
            pltpu.VMEM((rows, D // rows, units), jnp.bfloat16),
            pltpu.SemaphoreType.DMA((units // tile,)),
            pltpu.SemaphoreType.DMA,
        ],
        compiler_params=params(),
        cost_estimate=cost(6 * S * D * units, 6 * D * units),
    )(place, *flat, *weights)


def shards(hidden_states, lengths, qkvg_master, gateup_master, out_master, down_master):
    rows, cols = lax.axis_size("row"), lax.axis_size("col")
    per_row = lengths.shape[0]
    heads = HEADS // cols
    place = jnp.stack([lax.axis_index("row"), lax.axis_index("col")]).astype(jnp.int32)

    all_lengths = gather_lengths(lengths)
    depth = qkvg_master.shape[0]
    units = gateup_master.shape[2] // cols
    width = heads * HEAD_WIDTH
    front_cut = cut(cut_front_kernel, (depth, width + units), place, qkvg_master, out_master.T)
    front_parts = exchange(front_cut)
    everyone = gather_rows(after(hidden_states, all_lengths), halves=front_parts[1:3])
    front_blocks = join(front_parts, place)

    table, bins, starts, count = pack(place, all_lengths, rows)

    head_ids = lax.axis_index("col") * heads + jnp.arange(heads)
    decays = jnp.log1p(-jnp.power(2.0, -5.0 - head_ids.astype(jnp.float32)))
    freq = jnp.power(10000.0, -2.0 * jnp.arange(KEY // 2).astype(jnp.float32) / KEY)

    def begin(turn):
        codes = table[turn * TILES : (turn + 1) * TILES]
        segments = jnp.where(codes < 0, -1, codes // TILES)
        seg = jnp.broadcast_to(segments[:, None], (TILES, TILE)).reshape(S)
        positions = ((jnp.maximum(codes, 0) % TILES)[:, None] * TILE + jnp.arange(TILE)[None, :]).reshape(S)
        angle = positions.astype(jnp.float32)[:, None] * freq[None, :]
        own = pick(place, table, everyone, turn)
        return own, (jnp.cos(angle), jnp.sin(angle), seg[:, None], seg[None, :])

    own, tables = begin(0)
    tokens = gather_cols(own)
    ahead = [tokens[1][0], tokens[2][0]]
    rest = [part for entry in tokens[3:] for part in entry]
    front_pieces = gather_rows(after(front_blocks, *last_parts(everyone)), halves=ahead, whole=rest)

    feed_cut = cut(cut_feed_kernel, (3, depth, units), place, down_master.T, gateup_master)
    feed_parts = exchange(list(after(tuple(feed_cut), *rest)))

    mixed = retain(place, decays, *tables, tokens, front_pieces)
    terms = mix(place, mixed, front_pieces, cols)
    attended = collect(terms)
    feed_blocks = join(list(after(tuple(feed_parts), terms[0])), place)
    feed_pieces = gather_rows(feed_blocks, halves=attended[1:])
    residual = own.astype(jnp.float32) + added(attended)

    def rest_of_layer(residual):
        terms = feed(place, gather_cols(residual.astype(jnp.bfloat16)), feed_pieces)
        return gather_rows((residual + added(collect(terms))).astype(jnp.bfloat16), direct=True)

    first = rest_of_layer(residual)

    def finish(pieces):
        return spread(place, lengths, bins, starts, pieces, rows, per_row)

    def more(pieces):
        for turn in range(1, per_row):
            own, tables = begin(turn)
            mixed = retain(place, decays, *tables, gather_cols(own), front_pieces)
            attended = collect(mix(place, mixed, front_pieces, cols))
            pieces = pieces + rest_of_layer(own.astype(jnp.float32) + added(attended))
        return finish(pieces)

    layer_output = lax.cond(count[0] > rows, more, finish, first)
    return (layer_output, front_blocks[:, :width], feed_blocks[1:], front_blocks[:, width:].T, feed_blocks[0].T)


def solution(mesh):
    return jax.shard_map(
        shards,
        mesh=mesh,
        in_specs=(
            P("row", "col"),
            P("row"),
            P(("row", "col"), None),
            P(None, ("row", "col"), None),
            P(None, ("row", "col")),
            P(None, ("row", "col")),
        ),
        out_specs=(
            P("row", "col"),
            P("row", "col"),
            P(None, "row", "col"),
            P("col", "row"),
            P("col", "row"),
        ),
        check_vma=False,
    )
```

```python
import functools
import math

import jax
import jax.numpy as jnp
from jax import lax
from jax.experimental import pallas as pl
from jax.experimental.pallas import tpu as pltpu
from jax.sharding import PartitionSpec as P

D = 2048
HEADS = 8
KEY = 256
VAL = 512
S = 512
TILE = 16
TILES = S // TILE
HEAD_WIDTH = 2 * KEY + 2 * VAL

epsilon = 1e-05
VMEM_LIMIT = 56 * 1024 * 1024

SMEM = pl.BlockSpec(memory_space=pltpu.SMEM)
VMEM = pl.BlockSpec(memory_space=pltpu.VMEM)
ANY = pl.BlockSpec(memory_space=pl.ANY)


def params():
    return pltpu.CompilerParams(vmem_limit_bytes=VMEM_LIMIT)


def cost(flops, moved):
    return pl.CostEstimate(flops=int(flops), bytes_accessed=int(moved), transcendentals=0)


def swap(block, axis, step):
    size = lax.axis_size(axis)
    return lax.ppermute(block, axis, [(i, i ^ step) for i in range(size)])


def after(value, *earlier):
    return lax.optimization_barrier((value,) + earlier)[0]


def gather_links(block, arrived=None, halves=(), whole=()):
    across, along = arrived or (swap(block, "row", 2), swap(block, "row", 4))
    pieces = {0: block, 2: across, 4: along}
    axis = block.ndim - 2
    half = block.shape[axis] // 2
    across, along = after((across, along), *halves)
    upper = swap(lax.slice_in_dim(along, 0, half, axis=axis), "row", 2)
    lower = swap(lax.slice_in_dim(across, half, 2 * half, axis=axis), "row", 4)
    pieces[6] = jnp.concatenate(after((upper, lower), *whole), axis=axis)
    return pieces


def gather_cores(pieces, earlier=()):
    if earlier:
        pieces[1] = swap(pieces[0], "row", 1)
        pieces[3] = swap(after(pieces[2], *earlier), "row", 1)
        pieces[5] = swap(after(pieces[4], pieces[3]), "row", 1)
        pieces[7] = swap(after(pieces[6], pieces[5]), "row", 1)
    else:
        own = after(pieces[0], pieces[2], pieces[4])
        for j in (0, 2, 4, 6):
            pieces[j | 1] = swap(pieces[j] if j else own, "row", 1)
    return [pieces[j] for j in range(8)]


def gather_rows(block, direct=False, **order):
    size = lax.axis_size("row")
    if size == 8 and not direct:
        return gather_cores(gather_links(block, **order))
    pieces = {0: block}
    if size == 8:
        for j in (2, 4, 6):
            pieces[j] = swap(block, "row", j)
        pieces[0] = after(block, pieces[2], pieces[4])
        bits = [1]
    else:
        bits = [1 << i for i in reversed(range(size.bit_length() - 1))]
    for bit in bits:
        for j in sorted(pieces):
            pieces[j | bit] = swap(pieces[j], "row", bit)
    return [pieces[j] for j in range(size)]


def last_parts(pieces):
    return (pieces[6],) if len(pieces) == 8 else (pieces[-1],)


def mark(block, lengths):
    digits = jnp.stack([lengths // TILE, lengths % TILE], axis=1).astype(jnp.bfloat16)
    rows = jnp.pad(digits, ((0, 2 * TILE - digits.shape[0]), (0, block.shape[1] - 2)))
    return jnp.concatenate([block, rows], axis=0)


def read_marks(pieces, per_row):
    rows = pieces[0].shape[0] - 2 * TILE
    digits = jnp.concatenate([piece[rows : rows + per_row, :2] for piece in pieces], axis=0).astype(jnp.int32)
    return digits[:, 0] * TILE + digits[:, 1]


def exchange(blocks):
    return [blocks[0]] + [swap(blocks[k], "col", k) for k in range(1, len(blocks))]


def gather_cols(block):
    size = lax.axis_size("col")
    if size != 4:
        return [(block,)] + [(swap(block, "col", k),) for k in range(1, size)]
    near = swap(block, "col", 1)
    far = swap(block, "col", 2)
    mine, passed = after((block, far), near)
    middle = lax.ppermute(mine, "col", [(1, 2), (2, 1)])
    ends = lax.ppermute(passed, "col", [(2, 3), (1, 0)])
    return [(block,), (near,), (far,), (middle, ends)]


def collect(terms, later=()):
    if lax.axis_size("col") != 4:
        parts = exchange(terms)
        return parts, parts[1:2]
    early = lax.ppermute(terms[3], "col", [(3, 2), (0, 1)])
    middle = lax.ppermute(terms[3], "col", [(1, 2), (2, 1)])
    term1, term2, early = after((terms[1], terms[2], early), middle, *later)
    near = swap(term1, "col", 1)
    both = term2.astype(jnp.float32) + early.astype(jnp.float32)
    far = swap(both.astype(jnp.bfloat16), "col", 2)
    return [terms[0], near, far, middle], (early, middle)


def added(parts):
    return sum(part.astype(jnp.float32) for part in parts)


def cut_front_kernel(cols, place, qkvg, out, *blocks):
    units = out.shape[1] // cols
    width = blocks[0].shape[1] - units
    for k in range(cols):
        target = lax.bitwise_xor(place[1], k)
        columns = pl.ds(pl.multiple_of(target * width, 128), width)
        blocks[k][:, :width] = qkvg[:, columns].astype(jnp.bfloat16)
        columns = pl.ds(pl.multiple_of(target * units, 128), units)
        blocks[k][:, width:] = out[:, columns].astype(jnp.bfloat16)


def cut_feed_kernel(cols, place, down, gateup, *blocks):
    units = blocks[0].shape[2]
    for k in range(cols):
        target = lax.bitwise_xor(place[1], k)
        columns = pl.ds(pl.multiple_of(target * units, 128), units)
        blocks[k][0] = down[:, columns].astype(jnp.bfloat16)
        blocks[k][1] = gateup[0, :, columns].astype(jnp.bfloat16)
        blocks[k][2] = gateup[1, :, columns].astype(jnp.bfloat16)


def cut(kernel, shape, place, *masters):
    cols = lax.axis_size("col")
    return pl.pallas_call(
        functools.partial(kernel, cols),
        out_shape=[jax.ShapeDtypeStruct(shape, jnp.bfloat16)] * cols,
        in_specs=[SMEM] + [VMEM] * len(masters),
        out_specs=[VMEM] * cols,
        compiler_params=params(),
        cost_estimate=cost(0, 6 * math.prod(shape) * cols),
    )(place, *masters)


def join_kernel(cols, place, *refs):
    out = refs[cols]
    rows = refs[0].shape[-2]
    for k in range(cols):
        source = lax.bitwise_xor(place[1], k)
        where = pl.ds(pl.multiple_of(source * rows, 16), rows)
        if len(out.shape) == 2:
            out[where, :] = refs[k][...]
        else:
            out[:, where, :] = refs[k][...]


def join(blocks, place):
    cols = len(blocks)
    shape = list(blocks[0].shape)
    shape[-2] *= cols
    return pl.pallas_call(
        functools.partial(join_kernel, cols),
        out_shape=jax.ShapeDtypeStruct(tuple(shape), jnp.bfloat16),
        in_specs=[SMEM] + [VMEM] * cols,
        out_specs=VMEM,
        compiler_params=params(),
        cost_estimate=cost(0, 4 * math.prod(shape)),
    )(place, *blocks)


def pack_kernel(requests, rows, passes, place, lengths, table, bins, starts, count, used):
    row = place[0]
    per_row = requests // rows

    def clear(i, carry):
        table[i] = -1
        return carry

    lax.fori_loop(0, passes * TILES, clear, 0)

    def clear_used(i, carry):
        used[i] = 0
        return carry

    lax.fori_loop(0, requests, clear_used, 0)

    def put(q, top):
        owner = q // per_row
        length = lengths[lax.bitwise_xor(owner, row) * per_row + (q - owner * per_row)]
        tiles = (length + (TILE - 1)) // TILE

        def look(i, best):
            b = requests - 1 - i
            return jnp.where(used[b] + tiles <= TILES, b, best)

        b = lax.fori_loop(0, requests, look, requests - 1)
        start = used[b]
        used[b] = start + tiles
        bins[q] = b
        starts[q] = start
        turn = b // rows

        @pl.when(b - turn * rows == row)
        def _():
            def note(i, carry):
                table[turn * TILES + start + i] = q * TILES + i
                return carry

            lax.fori_loop(0, tiles, note, 0)

        return jnp.maximum(top, b + 1)

    count[0] = lax.fori_loop(0, requests, put, 0)


def pack(place, lengths, rows):
    requests = lengths.shape[0]
    passes = requests // rows
    whole = lambda n: jax.ShapeDtypeStruct((n,), jnp.int32)
    return pl.pallas_call(
        functools.partial(pack_kernel, requests, rows, passes),
        out_shape=[whole(passes * TILES), whole(requests), whole(requests), whole(1)],
        in_specs=[SMEM, SMEM],
        out_specs=[SMEM] * 4,
        scratch_shapes=[pltpu.SMEM((requests,), jnp.int32)],
        compiler_params=params(),
    )(place, lengths)


def pick_kernel(rows, per_row, turn, place, table, *refs):
    pieces, out, sem = refs[:rows], refs[rows], refs[rows + 1]
    row = place[0]

    def step(i, carry):
        code = jnp.maximum(table[turn * TILES + i], 0)
        request = code // TILES
        owner = request // per_row
        tile = (request - owner * per_row) * TILES + (code - request * TILES)
        piece = lax.bitwise_xor(owner, row)
        source = pl.ds(pl.multiple_of(tile * TILE, TILE), TILE)
        target = pl.ds(pl.multiple_of(i * TILE, TILE), TILE)
        for j in range(rows):

            @pl.when(piece == j)
            def _():
                pltpu.make_async_copy(pieces[j].at[source, :], out.at[target, :], sem).start()

        return carry

    lax.fori_loop(0, TILES, step, 0)
    pltpu.make_async_copy(out, out, sem).wait()


def pick(place, table, pieces, turn):
    rows = len(pieces)
    width = pieces[0].shape[1]
    return pl.pallas_call(
        functools.partial(pick_kernel, rows, pieces[0].shape[0] // S, turn),
        out_shape=jax.ShapeDtypeStruct((S, width), jnp.bfloat16),
        in_specs=[SMEM, SMEM] + [ANY] * rows,
        out_specs=VMEM,
        scratch_shapes=[pltpu.SemaphoreType.DMA],
        compiler_params=params(),
        cost_estimate=cost(0, 4 * S * width),
    )(place, table, *pieces)


def spread_kernel(rows, per_row, total, place, lengths, bins, starts, *refs):
    pieces, out = refs[:total], refs[total]
    row = place[0]
    width = out.shape[1]
    for a in range(per_row):
        request = row * per_row + a
        length = lengths[a]
        b = bins[request]
        start = starts[request]
        turn = b // rows
        index = lax.bitwise_xor(b - turn * rows, row) + turn * rows
        tiles = (length + (TILE - 1)) // TILE

        def blank(i, carry):
            out[pl.ds(pl.multiple_of(a * S + i * TILE, TILE), TILE), :] = jnp.zeros((TILE, width), jnp.bfloat16)
            return carry

        lax.fori_loop(tiles, TILES, blank, 0)
        for j in range(total):

            @pl.when(index == j)
            def _():
                def move(i, carry):
                    values = pieces[j][pl.ds(pl.multiple_of((start + i) * TILE, TILE), TILE), :]
                    position = i * TILE + lax.broadcasted_iota(jnp.int32, (TILE, width), 0)
                    kept = jnp.where(position < length, values.astype(jnp.float32), 0.0)
                    out[pl.ds(pl.multiple_of(a * S + i * TILE, TILE), TILE), :] = kept.astype(jnp.bfloat16)
                    return carry

                lax.fori_loop(0, tiles, move, 0)


def spread(place, lengths, bins, starts, pieces, rows, per_row):
    width = pieces[0].shape[1]
    return pl.pallas_call(
        functools.partial(spread_kernel, rows, per_row, len(pieces)),
        out_shape=jax.ShapeDtypeStruct((per_row * S, width), jnp.bfloat16),
        in_specs=[SMEM] * 4 + [VMEM] * len(pieces),
        out_specs=VMEM,
        compiler_params=params(),
        cost_estimate=cost(0, 2 * S * width * (len(pieces) + per_row)),
    )(place, lengths, bins, starts, *pieces)


DOT = functools.partial(jnp.dot, preferred_element_type=jnp.float32)


def DOT_T(left, right):
    return lax.dot_general(left, right, (((1,), (1,)), ((), ())), preferred_element_type=jnp.float32)


def flatten(parts):
    return [part for entry in parts for part in entry], tuple(len(entry) for entry in parts)


def read_parts(refs, counts):
    at = 0
    for count in counts:
        block = refs[at][...]
        for other in refs[at + 1 : at + count]:
            block = block + other[...]
        at += count
        yield block


def silu(values):
    return values * (1.0 / (1.0 + jnp.exp(-values)))


def retain_kernel(rows, counts, heads, place, decays, cosine, sine, seg_col, seg_row, *refs):
    cols, number = len(counts), sum(counts)
    tokens, weights = refs[:number], refs[number : number + rows]
    mixed, normed, gathered, sems = refs[number + rows :]
    depth = D // rows
    width = D // cols
    parts = ((0, 2 * KEY), (2 * KEY, VAL), (2 * KEY + VAL, VAL))

    for head in range(heads):
        for i, (low, size) in enumerate(parts):
            columns = pl.ds(head * HEAD_WIDTH + low, size)
            for j in range(rows):
                where = pl.ds(pl.multiple_of(lax.bitwise_xor(place[0], j) * depth, depth), depth)
                pltpu.make_async_copy(
                    weights[j].at[:, columns], gathered.at[where, columns], sems.at[head * 3 + i]
                ).start()

    total = jnp.zeros((S, 1), jnp.float32)
    for block in read_parts(tokens, counts):
        values = block.astype(jnp.float32)
        total += jnp.sum(values * values, axis=1, keepdims=True)
    scale = lax.rsqrt(total / D + epsilon)
    for k, block in enumerate(read_parts(tokens, counts)):
        where = pl.ds(pl.multiple_of(lax.bitwise_xor(place[1], k) * width, width), width)
        normed[:, where] = (block.astype(jnp.float32) * scale).astype(jnp.bfloat16)

    def project(head, i):
        low, size = parts[i]
        columns = pl.ds(head * HEAD_WIDTH + low, size)
        view = gathered.at[:, columns]
        pltpu.make_async_copy(view, view, sems.at[head * 3 + i]).wait()
        return DOT(normed[...], gathered[:, columns]).astype(jnp.bfloat16)

    def rotate(values):
        values = values.astype(jnp.float32)
        first, second = values[:, : KEY // 2], values[:, KEY // 2 :]
        cos, sin = cosine[...], sine[...]
        return jnp.concatenate([first * cos - second * sin, first * sin + second * cos], axis=1)

    lag = lax.broadcasted_iota(jnp.int32, (S, S), 0) - lax.broadcasted_iota(jnp.int32, (S, S), 1)
    allowed = (lag >= 0) & (seg_col[...] == seg_row[...])
    span = jnp.where(allowed, lag.astype(jnp.float32), 1e6)
    for head in range(heads):
        both = project(head, 0)
        query = rotate(both[:, :KEY]).astype(jnp.bfloat16)
        keyed = (rotate(both[:, KEY:]) * (1.0 / math.sqrt(KEY))).astype(jnp.bfloat16)
        scores = DOT_T(query, keyed)
        scores = scores * jnp.exp(span * decays[head])
        denom = jnp.sum(scores, axis=1, keepdims=True)
        value = project(head, 1)
        retained = DOT(scores.astype(jnp.bfloat16), value) / jnp.maximum(jnp.abs(denom), 1.0)
        centred = retained - jnp.mean(retained, axis=1, keepdims=True)
        spread_of = jnp.mean(centred * centred, axis=1, keepdims=True)
        grouped = centred * lax.rsqrt(spread_of + epsilon)
        gate = project(head, 2).astype(jnp.float32)
        mixed[:, head * VAL : (head + 1) * VAL] = (silu(gate) * grouped).astype(jnp.bfloat16)


def retain(place, decays, cosine, sine, seg_col, seg_row, tokens, weights):
    rows, cols = len(weights), len(tokens)
    heads = HEADS // cols
    flat, counts = flatten(tokens)
    return pl.pallas_call(
        functools.partial(retain_kernel, rows, counts, heads),
        out_shape=jax.ShapeDtypeStruct((S, heads * VAL), jnp.bfloat16),
        in_specs=[SMEM, SMEM] + [VMEM] * (4 + len(flat)) + [ANY] * rows,
        out_specs=VMEM,
        scratch_shapes=[
            pltpu.VMEM((S, D), jnp.bfloat16),
            pltpu.VMEM((D, heads * HEAD_WIDTH), jnp.bfloat16),
            pltpu.SemaphoreType.DMA((heads * 3,)),
        ],
        compiler_params=params(),
        cost_estimate=cost(2 * S * D * HEAD_WIDTH * heads * 1.3, 2 * D * HEAD_WIDTH * heads),
    )(place, decays, cosine, sine, seg_col, seg_row, *flat, *weights)


def load_terms(rows, cols, place, views, gathered, sem):
    ratio = rows // cols
    for j in range(rows):
        owner = lax.bitwise_xor(place[0], j)
        target = owner // ratio
        slot = lax.bitwise_xor(target, place[1]) * ratio + (owner - target * ratio)
        pltpu.make_async_copy(views[j], gathered.at[slot], sem).start()


def put_terms(rows, cols, left, gathered, sem, outs):
    ratio = rows // cols
    depth = D // rows
    pltpu.make_async_copy(gathered, gathered, sem).wait()
    for slot in range(rows):
        k, i = slot // ratio, slot % ratio
        outs[k][:, i * depth : (i + 1) * depth] = DOT_T(left, gathered[slot]).astype(jnp.bfloat16)


def mix_kernel(rows, cols, place, mixed, *refs):
    weights, outs = refs[:rows], refs[rows : rows + cols]
    gathered, sem = refs[rows + cols :]
    units = mixed.shape[1]
    views = [ref.at[:, pl.ds(ref.shape[1] - units, units)] for ref in weights]
    load_terms(rows, cols, place, views, gathered, sem)
    put_terms(rows, cols, mixed[...], gathered, sem, outs)


def mix(place, mixed, weights, cols):
    rows = len(weights)
    width = D // cols
    return pl.pallas_call(
        functools.partial(mix_kernel, rows, cols),
        out_shape=[jax.ShapeDtypeStruct((S, width), jnp.bfloat16)] * cols,
        in_specs=[SMEM, VMEM] + [ANY] * rows,
        out_specs=[VMEM] * cols,
        scratch_shapes=[
            pltpu.VMEM((rows, D // rows, mixed.shape[1]), jnp.bfloat16),
            pltpu.SemaphoreType.DMA,
        ],
        compiler_params=params(),
        cost_estimate=cost(2 * S * D * mixed.shape[1], 2 * D * mixed.shape[1]),
    )(place, mixed, *weights)


def feed_kernel(rows, counts, tile, place, *refs):
    cols, number = len(counts), sum(counts)
    tokens = refs[:number]
    weights = refs[number : number + rows]
    outs = refs[number + rows : number + rows + cols]
    ordered, hidden, gathered, gathered_down, sems, sem_down = refs[number + rows + cols :]
    depth = D // rows
    width = D // cols
    steps = gathered.shape[2] // tile

    for step in range(steps):
        columns = pl.ds(step * tile, tile)
        for j in range(rows):
            where = pl.ds(pl.multiple_of(lax.bitwise_xor(place[0], j) * depth, depth), depth)
            pltpu.make_async_copy(
                weights[j].at[pl.ds(1, 2), :, columns], gathered.at[:, where, columns], sems.at[step]
            ).start()
    load_terms(rows, cols, place, [ref.at[0] for ref in weights], gathered_down, sem_down)

    total = jnp.zeros((S, 1), jnp.float32)
    for k, block in enumerate(read_parts(tokens, counts)):
        values = block.astype(jnp.float32)
        total += jnp.sum(values * values, axis=1, keepdims=True)
        where = pl.ds(pl.multiple_of(lax.bitwise_xor(place[1], k) * width, width), width)
        ordered[:, where] = block
    scale = lax.rsqrt(total / D + epsilon)

    for step in range(steps):
        columns = pl.ds(step * tile, tile)
        view = gathered.at[:, :, columns]
        pltpu.make_async_copy(view, view, sems.at[step]).wait()
        gate = DOT(ordered[...], gathered[0, :, columns]) * scale
        up = DOT(ordered[...], gathered[1, :, columns]) * scale
        hidden[:, columns] = (silu(gate) * up).astype(jnp.bfloat16)
    put_terms(rows, cols, hidden[...], gathered_down, sem_down, outs)


def feed(place, tokens, weights):
    rows, cols = len(weights), len(tokens)
    units = weights[0].shape[2]
    tile = min(units, 512)
    flat, counts = flatten(tokens)
    return pl.pallas_call(
        functools.partial(feed_kernel, rows, counts, tile),
        out_shape=[jax.ShapeDtypeStruct((S, D // cols), jnp.bfloat16)] * cols,
        in_specs=[SMEM] + [VMEM] * len(flat) + [ANY] * rows,
        out_specs=[VMEM] * cols,
        scratch_shapes=[
            pltpu.VMEM((S, D), jnp.bfloat16),
            pltpu.VMEM((S, units), jnp.bfloat16),
            pltpu.VMEM((2, D, units), jnp.bfloat16),
            pltpu.VMEM((rows, D // rows, units), jnp.bfloat16),
            pltpu.SemaphoreType.DMA((units // tile,)),
            pltpu.SemaphoreType.DMA,
        ],
        compiler_params=params(),
        cost_estimate=cost(6 * S * D * units, 6 * D * units),
    )(place, *flat, *weights)


def shards(hidden_states, lengths, qkvg_master, gateup_master, out_master, down_master):
    rows, cols = lax.axis_size("row"), lax.axis_size("col")
    per_row = lengths.shape[0]
    heads = HEADS // cols
    place = jnp.stack([lax.axis_index("row"), lax.axis_index("col")]).astype(jnp.int32)

    depth = qkvg_master.shape[0]
    units = gateup_master.shape[2] // cols
    width = heads * HEAD_WIDTH
    front_cut = cut(cut_front_kernel, (depth, width + units), place, qkvg_master, out_master.T)
    front_parts = exchange(front_cut)
    marked = mark(hidden_states, lengths)
    everyone = gather_rows(after(marked, front_cut[0]), halves=front_parts[1:3])
    front_blocks = join(front_parts, place)
    feed_cut = cut(cut_feed_kernel, (3, depth, units), place, down_master.T, gateup_master)
    feed_parts = exchange(list(after(tuple(feed_cut), *front_parts[1:])))
    all_lengths = read_marks(everyone, per_row)

    table, bins, starts, count = pack(place, all_lengths, rows)
    table = after(table, *feed_parts[1:3])

    head_ids = lax.axis_index("col") * heads + jnp.arange(heads)
    decays = jnp.log1p(-jnp.power(2.0, -5.0 - head_ids.astype(jnp.float32)))
    freq = jnp.power(10000.0, -2.0 * jnp.arange(KEY // 2).astype(jnp.float32) / KEY)

    def begin(turn):
        codes = table[turn * TILES : (turn + 1) * TILES]
        segments = jnp.where(codes < 0, -1, codes // TILES)
        seg = jnp.broadcast_to(segments[:, None], (TILES, TILE)).reshape(S)
        positions = ((jnp.maximum(codes, 0) % TILES)[:, None] * TILE + jnp.arange(TILE)[None, :]).reshape(S)
        angle = positions.astype(jnp.float32)[:, None] * freq[None, :]
        own = pick(place, table, everyone, turn)
        return own, (jnp.cos(angle), jnp.sin(angle), seg[:, None], seg[None, :])

    own, tables = begin(0)
    tokens = gather_cols(own)
    ahead = [tokens[1][0], tokens[2][0]]
    rest = [part for entry in tokens[3:] for part in entry]
    front_pieces = gather_rows(
        after(front_blocks, *last_parts(everyone)), halves=ahead, whole=(*rest, *tables, *feed_parts[3:])
    )

    mixed = retain(place, decays, *tables, tokens, front_pieces)
    terms = mix(place, mixed, front_pieces, cols)
    feed_blocks = after(join(feed_parts, place), *last_parts(front_pieces))
    whole = rows == 8
    arrived = (swap(feed_blocks, "row", 2), swap(feed_blocks, "row", 4)) if whole else ()
    attended, early = collect(terms, later=arrived)
    residual = own.astype(jnp.float32) + added(attended)
    sent = residual.astype(jnp.bfloat16)
    if whole:
        feed_pieces = gather_cores(gather_links(feed_blocks, arrived=arrived, halves=early), earlier=early)
        mid_tokens = gather_cols(after(sent, feed_pieces[5], feed_pieces[6]))
    else:
        mid_tokens = gather_cols(sent)
        feed_pieces = gather_rows(feed_blocks)

    weights = (front_blocks[:, :width], feed_blocks[1:], front_blocks[:, width:].T, feed_blocks[0].T)
    weights = lax.optimization_barrier(weights)

    def rest_of_layer(residual, tokens, feed_pieces):
        fed, _ = collect(feed(place, tokens, feed_pieces))
        return gather_rows((residual + added(fed)).astype(jnp.bfloat16), direct=True)

    first = rest_of_layer(residual, mid_tokens, [after(feed_pieces[0], *weights)] + feed_pieces[1:])

    def finish(pieces):
        return spread(place, lengths, bins, starts, pieces, rows, per_row)

    def more(pieces):
        for turn in range(1, per_row):
            own, tables = begin(turn)
            mixed = retain(place, decays, *tables, gather_cols(own), front_pieces)
            attended, _ = collect(mix(place, mixed, front_pieces, cols))
            residual = own.astype(jnp.float32) + added(attended)
            pieces = pieces + rest_of_layer(residual, gather_cols(residual.astype(jnp.bfloat16)), feed_pieces)
        return finish(pieces)

    layer_output = lax.cond(count[0] > rows, more, finish, first)
    return (layer_output,) + weights


def solution(mesh):
    return jax.shard_map(
        shards,
        mesh=mesh,
        in_specs=(
            P("row", "col"),
            P("row"),
            P(("row", "col"), None),
            P(None, ("row", "col"), None),
            P(None, ("row", "col")),
            P(None, ("row", "col")),
        ),
        out_specs=(
            P("row", "col"),
            P("row", "col"),
            P(None, "row", "col"),
            P("col", "row"),
            P("col", "row"),
        ),
        check_vma=False,
    )
```

```python
import functools
import math

import jax
import jax.numpy as jnp
from jax import lax
from jax.experimental import pallas as pl
from jax.experimental.pallas import tpu as pltpu
from jax.sharding import PartitionSpec as P

D = 2048
HEADS = 8
KEY = 256
VAL = 512
S = 512
TILE = 16
TILES = S // TILE
HEAD_WIDTH = 2 * KEY + 2 * VAL

epsilon = 1e-05
VMEM_LIMIT = 56 * 1024 * 1024

SMEM = pl.BlockSpec(memory_space=pltpu.SMEM)
VMEM = pl.BlockSpec(memory_space=pltpu.VMEM)
ANY = pl.BlockSpec(memory_space=pl.ANY)


def params():
    return pltpu.CompilerParams(vmem_limit_bytes=VMEM_LIMIT)


def cost(flops, moved):
    return pl.CostEstimate(flops=int(flops), bytes_accessed=int(moved), transcendentals=0)


def swap(block, axis, step):
    size = lax.axis_size(axis)
    return lax.ppermute(block, axis, [(i, i ^ step) for i in range(size)])


def after(value, *earlier):
    return lax.optimization_barrier((value,) + earlier)[0]


def gather_links(block, arrived=None, halves=(), whole=()):
    across, along = arrived or (swap(block, "row", 2), swap(block, "row", 4))
    pieces = {0: block, 2: across, 4: along}
    axis = block.ndim - 2
    half = block.shape[axis] // 2
    across, along = after((across, along), *halves)
    upper = swap(lax.slice_in_dim(along, 0, half, axis=axis), "row", 2)
    lower = swap(lax.slice_in_dim(across, half, 2 * half, axis=axis), "row", 4)
    pieces[6] = jnp.concatenate(after((upper, lower), *whole), axis=axis)
    return pieces


def gather_cores(pieces, earlier=()):
    own = pieces[0] if earlier else after(pieces[0], pieces[2], pieces[4])
    for j in (0, 2, 4, 6):
        pieces[j | 1] = swap(after(pieces[j], *earlier) if j else own, "row", 1)
    return [pieces[j] for j in range(8)]


def gather_rows(block, direct=False, **order):
    size = lax.axis_size("row")
    if size == 8 and not direct:
        return gather_cores(gather_links(block, **order))
    pieces = {0: block}
    if size == 8:
        for j in (2, 4, 6):
            pieces[j] = swap(block, "row", j)
        pieces[0] = after(block, pieces[2], pieces[4])
        bits = [1]
    else:
        bits = [1 << i for i in reversed(range(size.bit_length() - 1))]
    for bit in bits:
        for j in sorted(pieces):
            pieces[j | bit] = swap(pieces[j], "row", bit)
    return [pieces[j] for j in range(size)]


def last_parts(pieces):
    return (pieces[6],) if len(pieces) == 8 else (pieces[-1],)


def mark(block, lengths):
    digits = jnp.stack([lengths // TILE, lengths % TILE], axis=1).astype(jnp.bfloat16)
    rows = jnp.pad(digits, ((0, 2 * TILE - digits.shape[0]), (0, block.shape[1] - 2)))
    return jnp.concatenate([block, rows], axis=0)


def read_marks(pieces, per_row):
    rows = pieces[0].shape[0] - 2 * TILE
    digits = jnp.concatenate([piece[rows : rows + per_row, :2] for piece in pieces], axis=0).astype(jnp.int32)
    return digits[:, 0] * TILE + digits[:, 1]


def exchange(blocks):
    return [blocks[0]] + [swap(blocks[k], "col", k) for k in range(1, len(blocks))]


def gather_cols(block):
    size = lax.axis_size("col")
    if size != 4:
        return [(block,)] + [(swap(block, "col", k),) for k in range(1, size)]
    near = swap(block, "col", 1)
    far = swap(block, "col", 2)
    mine, passed = after((block, far), near)
    middle = lax.ppermute(mine, "col", [(1, 2), (2, 1)])
    ends = lax.ppermute(passed, "col", [(2, 3), (1, 0)])
    return [(block,), (near,), (far,), (middle, ends)]


def collect(terms, later=()):
    if lax.axis_size("col") != 4:
        parts = exchange(terms)
        return parts, parts[1:2]
    early = lax.ppermute(terms[3], "col", [(3, 2), (0, 1)])
    middle = lax.ppermute(terms[3], "col", [(1, 2), (2, 1)])
    term1, term2, early = after((terms[1], terms[2], early), middle, *later)
    near = swap(term1, "col", 1)
    both = term2.astype(jnp.float32) + early.astype(jnp.float32)
    far = swap(both.astype(jnp.bfloat16), "col", 2)
    return [terms[0], near, far, middle], (early, middle)


def added(parts):
    return sum(part.astype(jnp.float32) for part in parts)


def cut_front_kernel(cols, place, qkvg, out, *blocks):
    units = out.shape[1] // cols
    width = blocks[0].shape[1] - units
    for k in range(cols):
        target = lax.bitwise_xor(place[1], k)
        columns = pl.ds(pl.multiple_of(target * width, 128), width)
        blocks[k][:, :width] = qkvg[:, columns].astype(jnp.bfloat16)
        columns = pl.ds(pl.multiple_of(target * units, 128), units)
        blocks[k][:, width:] = out[:, columns].astype(jnp.bfloat16)


def cut_feed_kernel(cols, place, down, gateup, *blocks):
    units = blocks[0].shape[2]
    for k in range(cols):
        target = lax.bitwise_xor(place[1], k)
        columns = pl.ds(pl.multiple_of(target * units, 128), units)
        blocks[k][0] = down[:, columns].astype(jnp.bfloat16)
        blocks[k][1] = gateup[0, :, columns].astype(jnp.bfloat16)
        blocks[k][2] = gateup[1, :, columns].astype(jnp.bfloat16)


def cut(kernel, shape, place, *masters):
    cols = lax.axis_size("col")
    return pl.pallas_call(
        functools.partial(kernel, cols),
        out_shape=[jax.ShapeDtypeStruct(shape, jnp.bfloat16)] * cols,
        in_specs=[SMEM] + [VMEM] * len(masters),
        out_specs=[VMEM] * cols,
        compiler_params=params(),
        cost_estimate=cost(0, 6 * math.prod(shape) * cols),
    )(place, *masters)


def join_kernel(cols, place, *refs):
    out = refs[cols]
    rows = refs[0].shape[-2]
    for k in range(cols):
        source = lax.bitwise_xor(place[1], k)
        where = pl.ds(pl.multiple_of(source * rows, 16), rows)
        if len(out.shape) == 2:
            out[where, :] = refs[k][...]
        else:
            out[:, where, :] = refs[k][...]


def join(blocks, place):
    cols = len(blocks)
    shape = list(blocks[0].shape)
    shape[-2] *= cols
    return pl.pallas_call(
        functools.partial(join_kernel, cols),
        out_shape=jax.ShapeDtypeStruct(tuple(shape), jnp.bfloat16),
        in_specs=[SMEM] + [VMEM] * cols,
        out_specs=VMEM,
        compiler_params=params(),
        cost_estimate=cost(0, 4 * math.prod(shape)),
    )(place, *blocks)


def pack_kernel(requests, rows, passes, place, lengths, table, bins, starts, count, used):
    row = place[0]
    per_row = requests // rows

    def clear(i, carry):
        table[i] = -1
        return carry

    lax.fori_loop(0, passes * TILES, clear, 0)

    def clear_used(i, carry):
        used[i] = 0
        return carry

    lax.fori_loop(0, requests, clear_used, 0)

    def put(q, top):
        owner = q // per_row
        length = lengths[lax.bitwise_xor(owner, row) * per_row + (q - owner * per_row)]
        tiles = (length + (TILE - 1)) // TILE

        def look(i, best):
            b = requests - 1 - i
            return jnp.where(used[b] + tiles <= TILES, b, best)

        b = lax.fori_loop(0, requests, look, requests - 1)
        start = used[b]
        used[b] = start + tiles
        bins[q] = b
        starts[q] = start
        turn = b // rows

        @pl.when(b - turn * rows == row)
        def _():
            def note(i, carry):
                table[turn * TILES + start + i] = q * TILES + i
                return carry

            lax.fori_loop(0, tiles, note, 0)

        return jnp.maximum(top, b + 1)

    count[0] = lax.fori_loop(0, requests, put, 0)


def pack(place, lengths, rows):
    requests = lengths.shape[0]
    passes = requests // rows
    whole = lambda n: jax.ShapeDtypeStruct((n,), jnp.int32)
    return pl.pallas_call(
        functools.partial(pack_kernel, requests, rows, passes),
        out_shape=[whole(passes * TILES), whole(requests), whole(requests), whole(1)],
        in_specs=[SMEM, SMEM],
        out_specs=[SMEM] * 4,
        scratch_shapes=[pltpu.SMEM((requests,), jnp.int32)],
        compiler_params=params(),
    )(place, lengths)


def pick_kernel(rows, per_row, turn, place, table, *refs):
    pieces, out, sem = refs[:rows], refs[rows], refs[rows + 1]
    row = place[0]

    def step(i, carry):
        code = jnp.maximum(table[turn * TILES + i], 0)
        request = code // TILES
        owner = request // per_row
        tile = (request - owner * per_row) * TILES + (code - request * TILES)
        piece = lax.bitwise_xor(owner, row)
        source = pl.ds(pl.multiple_of(tile * TILE, TILE), TILE)
        target = pl.ds(pl.multiple_of(i * TILE, TILE), TILE)
        for j in range(rows):

            @pl.when(piece == j)
            def _():
                pltpu.make_async_copy(pieces[j].at[source, :], out.at[target, :], sem).start()

        return carry

    lax.fori_loop(0, TILES, step, 0)
    pltpu.make_async_copy(out, out, sem).wait()


def pick(place, table, pieces, turn):
    rows = len(pieces)
    width = pieces[0].shape[1]
    return pl.pallas_call(
        functools.partial(pick_kernel, rows, pieces[0].shape[0] // S, turn),
        out_shape=jax.ShapeDtypeStruct((S, width), jnp.bfloat16),
        in_specs=[SMEM, SMEM] + [ANY] * rows,
        out_specs=VMEM,
        scratch_shapes=[pltpu.SemaphoreType.DMA],
        compiler_params=params(),
        cost_estimate=cost(0, 4 * S * width),
    )(place, table, *pieces)


def spread_kernel(rows, per_row, total, place, lengths, bins, starts, *refs):
    pieces, out = refs[:total], refs[total]
    row = place[0]
    width = out.shape[1]
    for a in range(per_row):
        request = row * per_row + a
        length = lengths[a]
        b = bins[request]
        start = starts[request]
        turn = b // rows
        index = lax.bitwise_xor(b - turn * rows, row) + turn * rows
        tiles = (length + (TILE - 1)) // TILE

        def blank(i, carry):
            out[pl.ds(pl.multiple_of(a * S + i * TILE, TILE), TILE), :] = jnp.zeros((TILE, width), jnp.bfloat16)
            return carry

        lax.fori_loop(tiles, TILES, blank, 0)
        for j in range(total):

            @pl.when(index == j)
            def _():
                def move(i, carry):
                    values = pieces[j][pl.ds(pl.multiple_of((start + i) * TILE, TILE), TILE), :]
                    position = i * TILE + lax.broadcasted_iota(jnp.int32, (TILE, width), 0)
                    kept = jnp.where(position < length, values.astype(jnp.float32), 0.0)
                    out[pl.ds(pl.multiple_of(a * S + i * TILE, TILE), TILE), :] = kept.astype(jnp.bfloat16)
                    return carry

                lax.fori_loop(0, tiles, move, 0)


def spread(place, lengths, bins, starts, pieces, rows, per_row):
    width = pieces[0].shape[1]
    return pl.pallas_call(
        functools.partial(spread_kernel, rows, per_row, len(pieces)),
        out_shape=jax.ShapeDtypeStruct((per_row * S, width), jnp.bfloat16),
        in_specs=[SMEM] * 4 + [VMEM] * len(pieces),
        out_specs=VMEM,
        compiler_params=params(),
        cost_estimate=cost(0, 2 * S * width * (len(pieces) + per_row)),
    )(place, lengths, bins, starts, *pieces)


DOT = functools.partial(jnp.dot, preferred_element_type=jnp.float32)


def DOT_T(left, right):
    return lax.dot_general(left, right, (((1,), (1,)), ((), ())), preferred_element_type=jnp.float32)


def flatten(parts):
    return [part for entry in parts for part in entry], tuple(len(entry) for entry in parts)


def read_parts(refs, counts):
    at = 0
    for count in counts:
        block = refs[at][...]
        for other in refs[at + 1 : at + count]:
            block = block + other[...]
        at += count
        yield block


def silu(values):
    return values * (1.0 / (1.0 + jnp.exp(-values)))


def retain_kernel(rows, counts, heads, place, decays, cosine, sine, seg_col, seg_row, *refs):
    cols, number = len(counts), sum(counts)
    tokens, weights = refs[:number], refs[number : number + rows]
    mixed, normed, gathered, sems = refs[number + rows :]
    depth = D // rows
    width = D // cols
    parts = ((0, 2 * KEY), (2 * KEY, VAL), (2 * KEY + VAL, VAL))

    for head in range(heads):
        for i, (low, size) in enumerate(parts):
            columns = pl.ds(head * HEAD_WIDTH + low, size)
            for j in range(rows):
                where = pl.ds(pl.multiple_of(lax.bitwise_xor(place[0], j) * depth, depth), depth)
                pltpu.make_async_copy(
                    weights[j].at[:, columns], gathered.at[where, columns], sems.at[head * 3 + i]
                ).start()

    total = jnp.zeros((S, 1), jnp.float32)
    for block in read_parts(tokens, counts):
        values = block.astype(jnp.float32)
        total += jnp.sum(values * values, axis=1, keepdims=True)
    scale = lax.rsqrt(total / D + epsilon)
    for k, block in enumerate(read_parts(tokens, counts)):
        where = pl.ds(pl.multiple_of(lax.bitwise_xor(place[1], k) * width, width), width)
        normed[:, where] = (block.astype(jnp.float32) * scale).astype(jnp.bfloat16)

    def project(head, i):
        low, size = parts[i]
        columns = pl.ds(head * HEAD_WIDTH + low, size)
        view = gathered.at[:, columns]
        pltpu.make_async_copy(view, view, sems.at[head * 3 + i]).wait()
        return DOT(normed[...], gathered[:, columns]).astype(jnp.bfloat16)

    def rotate(values):
        values = values.astype(jnp.float32)
        first, second = values[:, : KEY // 2], values[:, KEY // 2 :]
        cos, sin = cosine[...], sine[...]
        return jnp.concatenate([first * cos - second * sin, first * sin + second * cos], axis=1)

    lag = lax.broadcasted_iota(jnp.int32, (S, S), 0) - lax.broadcasted_iota(jnp.int32, (S, S), 1)
    allowed = (lag >= 0) & (seg_col[...] == seg_row[...])
    span = jnp.where(allowed, lag.astype(jnp.float32), 1e6)
    for head in range(heads):
        both = project(head, 0)
        query = rotate(both[:, :KEY]).astype(jnp.bfloat16)
        keyed = (rotate(both[:, KEY:]) * (1.0 / math.sqrt(KEY))).astype(jnp.bfloat16)
        scores = DOT_T(query, keyed)
        scores = scores * jnp.exp(span * decays[head])
        denom = jnp.sum(scores, axis=1, keepdims=True)
        value = project(head, 1)
        retained = DOT(scores.astype(jnp.bfloat16), value) / jnp.maximum(jnp.abs(denom), 1.0)
        centred = retained - jnp.mean(retained, axis=1, keepdims=True)
        spread_of = jnp.mean(centred * centred, axis=1, keepdims=True)
        grouped = centred * lax.rsqrt(spread_of + epsilon)
        gate = project(head, 2).astype(jnp.float32)
        mixed[:, head * VAL : (head + 1) * VAL] = (silu(gate) * grouped).astype(jnp.bfloat16)


def retain(place, decays, cosine, sine, seg_col, seg_row, tokens, weights):
    rows, cols = len(weights), len(tokens)
    heads = HEADS // cols
    flat, counts = flatten(tokens)
    return pl.pallas_call(
        functools.partial(retain_kernel, rows, counts, heads),
        out_shape=jax.ShapeDtypeStruct((S, heads * VAL), jnp.bfloat16),
        in_specs=[SMEM, SMEM] + [VMEM] * (4 + len(flat)) + [ANY] * rows,
        out_specs=VMEM,
        scratch_shapes=[
            pltpu.VMEM((S, D), jnp.bfloat16),
            pltpu.VMEM((D, heads * HEAD_WIDTH), jnp.bfloat16),
            pltpu.SemaphoreType.DMA((heads * 3,)),
        ],
        compiler_params=params(),
        cost_estimate=cost(2 * S * D * HEAD_WIDTH * heads * 1.3, 2 * D * HEAD_WIDTH * heads),
    )(place, decays, cosine, sine, seg_col, seg_row, *flat, *weights)


def load_terms(rows, cols, place, views, gathered, sem):
    ratio = rows // cols
    for j in range(rows):
        owner = lax.bitwise_xor(place[0], j)
        target = owner // ratio
        slot = lax.bitwise_xor(target, place[1]) * ratio + (owner - target * ratio)
        pltpu.make_async_copy(views[j], gathered.at[slot], sem).start()


def put_terms(rows, cols, left, gathered, sem, outs):
    ratio = rows // cols
    depth = D // rows
    pltpu.make_async_copy(gathered, gathered, sem).wait()
    for slot in range(rows):
        k, i = slot // ratio, slot % ratio
        outs[k][:, i * depth : (i + 1) * depth] = DOT_T(left, gathered[slot]).astype(jnp.bfloat16)


def mix_kernel(rows, cols, place, mixed, *refs):
    weights, outs = refs[:rows], refs[rows : rows + cols]
    gathered, sem = refs[rows + cols :]
    units = mixed.shape[1]
    views = [ref.at[:, pl.ds(ref.shape[1] - units, units)] for ref in weights]
    load_terms(rows, cols, place, views, gathered, sem)
    put_terms(rows, cols, mixed[...], gathered, sem, outs)


def mix(place, mixed, weights, cols):
    rows = len(weights)
    width = D // cols
    return pl.pallas_call(
        functools.partial(mix_kernel, rows, cols),
        out_shape=[jax.ShapeDtypeStruct((S, width), jnp.bfloat16)] * cols,
        in_specs=[SMEM, VMEM] + [ANY] * rows,
        out_specs=[VMEM] * cols,
        scratch_shapes=[
            pltpu.VMEM((rows, D // rows, mixed.shape[1]), jnp.bfloat16),
            pltpu.SemaphoreType.DMA,
        ],
        compiler_params=params(),
        cost_estimate=cost(2 * S * D * mixed.shape[1], 2 * D * mixed.shape[1]),
    )(place, mixed, *weights)


def feed_kernel(rows, counts, tile, place, *refs):
    cols, number = len(counts), sum(counts)
    tokens = refs[:number]
    weights = refs[number : number + rows]
    outs = refs[number + rows : number + rows + cols]
    ordered, hidden, gathered, gathered_down, sems, sem_down = refs[number + rows + cols :]
    depth = D // rows
    width = D // cols
    steps = gathered.shape[2] // tile

    for step in range(steps):
        columns = pl.ds(step * tile, tile)
        for j in range(rows):
            where = pl.ds(pl.multiple_of(lax.bitwise_xor(place[0], j) * depth, depth), depth)
            pltpu.make_async_copy(
                weights[j].at[pl.ds(1, 2), :, columns], gathered.at[:, where, columns], sems.at[step]
            ).start()
    load_terms(rows, cols, place, [ref.at[0] for ref in weights], gathered_down, sem_down)

    total = jnp.zeros((S, 1), jnp.float32)
    for k, block in enumerate(read_parts(tokens, counts)):
        values = block.astype(jnp.float32)
        total += jnp.sum(values * values, axis=1, keepdims=True)
        where = pl.ds(pl.multiple_of(lax.bitwise_xor(place[1], k) * width, width), width)
        ordered[:, where] = block
    scale = lax.rsqrt(total / D + epsilon)

    for step in range(steps):
        columns = pl.ds(step * tile, tile)
        view = gathered.at[:, :, columns]
        pltpu.make_async_copy(view, view, sems.at[step]).wait()
        gate = DOT(ordered[...], gathered[0, :, columns]) * scale
        up = DOT(ordered[...], gathered[1, :, columns]) * scale
        hidden[:, columns] = (silu(gate) * up).astype(jnp.bfloat16)
    put_terms(rows, cols, hidden[...], gathered_down, sem_down, outs)


def feed(place, tokens, weights):
    rows, cols = len(weights), len(tokens)
    units = weights[0].shape[2]
    tile = min(units, 512)
    flat, counts = flatten(tokens)
    return pl.pallas_call(
        functools.partial(feed_kernel, rows, counts, tile),
        out_shape=[jax.ShapeDtypeStruct((S, D // cols), jnp.bfloat16)] * cols,
        in_specs=[SMEM] + [VMEM] * len(flat) + [ANY] * rows,
        out_specs=[VMEM] * cols,
        scratch_shapes=[
            pltpu.VMEM((S, D), jnp.bfloat16),
            pltpu.VMEM((S, units), jnp.bfloat16),
            pltpu.VMEM((2, D, units), jnp.bfloat16),
            pltpu.VMEM((rows, D // rows, units), jnp.bfloat16),
            pltpu.SemaphoreType.DMA((units // tile,)),
            pltpu.SemaphoreType.DMA,
        ],
        compiler_params=params(),
        cost_estimate=cost(6 * S * D * units, 6 * D * units),
    )(place, *flat, *weights)


def shards(hidden_states, lengths, qkvg_master, gateup_master, out_master, down_master):
    rows, cols = lax.axis_size("row"), lax.axis_size("col")
    per_row = lengths.shape[0]
    heads = HEADS // cols
    place = jnp.stack([lax.axis_index("row"), lax.axis_index("col")]).astype(jnp.int32)

    depth = qkvg_master.shape[0]
    units = gateup_master.shape[2] // cols
    width = heads * HEAD_WIDTH
    front_cut = cut(cut_front_kernel, (depth, width + units), place, qkvg_master, out_master.T)
    front_parts = exchange(front_cut)
    marked = mark(hidden_states, lengths)
    everyone = gather_rows(after(marked, front_cut[0]), halves=front_parts[1:3])
    front_blocks = join(front_parts, place)
    feed_cut = cut(cut_feed_kernel, (3, depth, units), place, down_master.T, gateup_master)
    all_lengths = read_marks(everyone, per_row)

    table, bins, starts, count = pack(place, all_lengths, rows)

    head_ids = lax.axis_index("col") * heads + jnp.arange(heads)
    decays = jnp.log1p(-jnp.power(2.0, -5.0 - head_ids.astype(jnp.float32)))
    freq = jnp.power(10000.0, -2.0 * jnp.arange(KEY // 2).astype(jnp.float32) / KEY)

    def begin(turn):
        codes = table[turn * TILES : (turn + 1) * TILES]
        segments = jnp.where(codes < 0, -1, codes // TILES)
        seg = jnp.broadcast_to(segments[:, None], (TILES, TILE)).reshape(S)
        positions = ((jnp.maximum(codes, 0) % TILES)[:, None] * TILE + jnp.arange(TILE)[None, :]).reshape(S)
        angle = positions.astype(jnp.float32)[:, None] * freq[None, :]
        own = pick(place, table, everyone, turn)
        return own, (jnp.cos(angle), jnp.sin(angle), seg[:, None], seg[None, :])

    own, tables = begin(0)
    tokens = gather_cols(own)
    ahead = [tokens[1][0], tokens[2][0]]
    rest = [part for entry in tokens[3:] for part in entry]
    feed_parts = exchange(list(after(tuple(feed_cut), *rest)))
    front_pieces = gather_rows(
        after(front_blocks, *last_parts(everyone)), halves=ahead, whole=(*rest, *tables, *feed_parts[1:])
    )

    mixed = retain(place, decays, *tables, tokens, front_pieces)
    terms = mix(place, mixed, front_pieces, cols)
    feed_blocks = after(join(feed_parts, place), *last_parts(front_pieces))
    whole = rows == 8
    arrived = (swap(feed_blocks, "row", 2), swap(feed_blocks, "row", 4)) if whole else ()
    attended, early = collect(terms, later=arrived)
    residual = own.astype(jnp.float32) + added(attended)
    sent = residual.astype(jnp.bfloat16)
    if whole:
        links = gather_links(feed_blocks, arrived=arrived, halves=early)
        mid_tokens = gather_cols(after(sent, links[6]))
        feed_pieces = gather_cores(links, earlier=(mid_tokens[1][0], mid_tokens[2][0]))
    else:
        mid_tokens = gather_cols(sent)
        feed_pieces = gather_rows(feed_blocks)

    weights = (front_blocks[:, :width], feed_blocks[1:], front_blocks[:, width:].T, feed_blocks[0].T)
    weights = lax.optimization_barrier(weights)

    def rest_of_layer(residual, tokens, feed_pieces):
        fed, _ = collect(feed(place, tokens, feed_pieces))
        return gather_rows((residual + added(fed)).astype(jnp.bfloat16), direct=True)

    first = rest_of_layer(residual, mid_tokens, [after(feed_pieces[0], *weights)] + feed_pieces[1:])

    def finish(pieces):
        return spread(place, lengths, bins, starts, pieces, rows, per_row)

    def more(pieces):
        for turn in range(1, per_row):
            own, tables = begin(turn)
            mixed = retain(place, decays, *tables, gather_cols(own), front_pieces)
            attended, _ = collect(mix(place, mixed, front_pieces, cols))
            residual = own.astype(jnp.float32) + added(attended)
            pieces = pieces + rest_of_layer(residual, gather_cols(residual.astype(jnp.bfloat16)), feed_pieces)
        return finish(pieces)

    layer_output = lax.cond(count[0] > rows, more, finish, first)
    return (layer_output,) + weights


def solution(mesh):
    return jax.shard_map(
        shards,
        mesh=mesh,
        in_specs=(
            P("row", "col"),
            P("row"),
            P(("row", "col"), None),
            P(None, ("row", "col"), None),
            P(None, ("row", "col")),
            P(None, ("row", "col")),
        ),
        out_specs=(
            P("row", "col"),
            P("row", "col"),
            P(None, "row", "col"),
            P("col", "row"),
            P("col", "row"),
        ),
        check_vma=False,
    )
```

```python
import functools
import math

import jax
import jax.numpy as jnp
from jax import lax
from jax.experimental import pallas as pl
from jax.experimental.pallas import tpu as pltpu
from jax.sharding import PartitionSpec as P

D = 2048
HEADS = 8
KEY = 256
VAL = 512
S = 512
TILE = 16
TILES = S // TILE
HEAD_WIDTH = 2 * KEY + 2 * VAL

epsilon = 1e-05
VMEM_LIMIT = 56 * 1024 * 1024

SMEM = pl.BlockSpec(memory_space=pltpu.SMEM)
VMEM = pl.BlockSpec(memory_space=pltpu.VMEM)
ANY = pl.BlockSpec(memory_space=pl.ANY)


def params():
    return pltpu.CompilerParams(vmem_limit_bytes=VMEM_LIMIT)


def cost(flops, moved):
    return pl.CostEstimate(flops=int(flops), bytes_accessed=int(moved), transcendentals=0)


def swap(block, axis, step):
    size = lax.axis_size(axis)
    return lax.ppermute(block, axis, [(i, i ^ step) for i in range(size)])


def after(value, *earlier):
    return lax.optimization_barrier((value,) + earlier)[0]


def gather_links(block, halves=()):
    across, along = swap(block, "row", 2), swap(block, "row", 4)
    pieces = {0: (block,), 2: (across,), 4: (along,)}
    axis = block.ndim - 2
    half = block.shape[axis] // 2
    across, along = after((across, along), *halves)
    upper = swap(lax.slice_in_dim(along, 0, half, axis=axis), "row", 2)
    lower = swap(lax.slice_in_dim(across, half, 2 * half, axis=axis), "row", 4)
    pieces[6] = (upper, lower)
    return pieces


def gather_cores(pieces, earlier=(), whole=()):
    if not earlier:
        pieces[0] = (after(pieces[0][0], pieces[2][0], pieces[4][0]),)
    for j in (0, 2, 4, 6):
        wait = (*earlier, *whole) if j == 6 else earlier if j else ()
        pieces[j | 1] = tuple(swap(after(part, *wait), "row", 1) for part in pieces[j])
    return [pieces[j] for j in range(8)]


def gather_rows(block, direct=False, halves=(), core=(), whole=()):
    size = lax.axis_size("row")
    if size == 8 and not direct:
        return gather_cores(gather_links(block, halves=halves), earlier=core, whole=whole)
    pieces = {0: block}
    if size == 8:
        for j in (2, 4, 6):
            pieces[j] = swap(block, "row", j)
        pieces[0] = after(block, pieces[2], pieces[4])
        bits = [1]
    else:
        bits = [1 << i for i in reversed(range(size.bit_length() - 1))]
    for bit in bits:
        for j in sorted(pieces):
            pieces[j | bit] = swap(pieces[j], "row", bit)
    return [(pieces[j],) for j in range(size)]


def last_parts(pieces):
    return pieces[6] if len(pieces) == 8 else pieces[-1]


def mark(block, lengths):
    digits = jnp.stack([lengths // TILE, lengths % TILE], axis=1).astype(jnp.bfloat16)
    rows = jnp.pad(digits, ((0, 2 * TILE - digits.shape[0]), (0, block.shape[1] - 2)))
    return jnp.concatenate([block, rows], axis=0)


def read_marks(pieces, per_row):
    last = [piece[-1] for piece in pieces]
    digits = jnp.concatenate(
        [block[block.shape[0] - 2 * TILE :][:per_row, :2] for block in last], axis=0
    ).astype(jnp.int32)
    return digits[:, 0] * TILE + digits[:, 1]


def exchange(blocks):
    return [blocks[0]] + [swap(blocks[k], "col", k) for k in range(1, len(blocks))]


def gather_cols(block):
    size = lax.axis_size("col")
    if size != 4:
        return [(block,)] + [(swap(block, "col", k),) for k in range(1, size)]
    near = swap(block, "col", 1)
    far = swap(block, "col", 2)
    mine, passed = after((block, far), near)
    middle = lax.ppermute(mine, "col", [(1, 2), (2, 1)])
    ends = lax.ppermute(passed, "col", [(2, 3), (1, 0)])
    return [(block,), (near,), (far,), (middle, ends)]


def collect(terms):
    if lax.axis_size("col") != 4:
        return exchange(terms)
    early = lax.ppermute(terms[3], "col", [(3, 2), (0, 1)])
    middle = lax.ppermute(terms[3], "col", [(1, 2), (2, 1)])
    term1, term2, early = after((terms[1], terms[2], early), middle)
    near = swap(term1, "col", 1)
    both = term2.astype(jnp.float32) + early.astype(jnp.float32)
    far = swap(both.astype(jnp.bfloat16), "col", 2)
    return [terms[0], near, far, middle]


def added(parts):
    return sum(part.astype(jnp.float32) for part in parts)


def cut_front_kernel(cols, place, qkvg, out, *blocks):
    units = out.shape[1] // cols
    width = blocks[0].shape[1] - units
    for k in range(cols):
        target = lax.bitwise_xor(place[1], k)
        columns = pl.ds(pl.multiple_of(target * width, 128), width)
        blocks[k][:, :width] = qkvg[:, columns].astype(jnp.bfloat16)
        columns = pl.ds(pl.multiple_of(target * units, 128), units)
        blocks[k][:, width:] = out[:, columns].astype(jnp.bfloat16)


def cut_feed_kernel(cols, place, down, gateup, *blocks):
    units = blocks[0].shape[2]
    for k in range(cols):
        target = lax.bitwise_xor(place[1], k)
        columns = pl.ds(pl.multiple_of(target * units, 128), units)
        blocks[k][0] = down[:, columns].astype(jnp.bfloat16)
        blocks[k][1] = gateup[0, :, columns].astype(jnp.bfloat16)
        blocks[k][2] = gateup[1, :, columns].astype(jnp.bfloat16)


def cut(kernel, shape, place, *masters):
    cols = lax.axis_size("col")
    return pl.pallas_call(
        functools.partial(kernel, cols),
        out_shape=[jax.ShapeDtypeStruct(shape, jnp.bfloat16)] * cols,
        in_specs=[SMEM] + [VMEM] * len(masters),
        out_specs=[VMEM] * cols,
        compiler_params=params(),
        cost_estimate=cost(0, 6 * math.prod(shape) * cols),
    )(place, *masters)


def join_kernel(cols, place, *refs):
    out = refs[cols]
    rows = refs[0].shape[-2]
    for k in range(cols):
        source = lax.bitwise_xor(place[1], k)
        where = pl.ds(pl.multiple_of(source * rows, 16), rows)
        if len(out.shape) == 2:
            out[where, :] = refs[k][...]
        else:
            out[:, where, :] = refs[k][...]


def join(blocks, place):
    cols = len(blocks)
    shape = list(blocks[0].shape)
    shape[-2] *= cols
    return pl.pallas_call(
        functools.partial(join_kernel, cols),
        out_shape=jax.ShapeDtypeStruct(tuple(shape), jnp.bfloat16),
        in_specs=[SMEM] + [VMEM] * cols,
        out_specs=VMEM,
        compiler_params=params(),
        cost_estimate=cost(0, 4 * math.prod(shape)),
    )(place, *blocks)


def pack_kernel(requests, rows, passes, place, lengths, table, bins, starts, count, used):
    row = place[0]
    per_row = requests // rows

    def clear(i, carry):
        table[i] = -1
        return carry

    lax.fori_loop(0, passes * TILES, clear, 0)

    def clear_used(i, carry):
        used[i] = 0
        return carry

    lax.fori_loop(0, requests, clear_used, 0)

    def put(q, top):
        owner = q // per_row
        length = lengths[lax.bitwise_xor(owner, row) * per_row + (q - owner * per_row)]
        tiles = (length + (TILE - 1)) // TILE

        def look(i, best):
            b = requests - 1 - i
            return jnp.where(used[b] + tiles <= TILES, b, best)

        b = lax.fori_loop(0, requests, look, requests - 1)
        start = used[b]
        used[b] = start + tiles
        bins[q] = b
        starts[q] = start
        turn = b // rows

        @pl.when(b - turn * rows == row)
        def _():
            def note(i, carry):
                table[turn * TILES + start + i] = q * TILES + i
                return carry

            lax.fori_loop(0, tiles, note, 0)

        return jnp.maximum(top, b + 1)

    count[0] = lax.fori_loop(0, requests, put, 0)


def pack(place, lengths, rows):
    requests = lengths.shape[0]
    passes = requests // rows
    whole = lambda n: jax.ShapeDtypeStruct((n,), jnp.int32)
    return pl.pallas_call(
        functools.partial(pack_kernel, requests, rows, passes),
        out_shape=[whole(passes * TILES), whole(requests), whole(requests), whole(1)],
        in_specs=[SMEM, SMEM],
        out_specs=[SMEM] * 4,
        scratch_shapes=[pltpu.SMEM((requests,), jnp.int32)],
        compiler_params=params(),
    )(place, lengths)


def pick_kernel(counts, per_row, turn, place, table, *refs):
    number = sum(counts)
    pieces, out, sem = split(refs[:number], counts), refs[number], refs[number + 1]
    row = place[0]

    def step(i, carry):
        code = jnp.maximum(table[turn * TILES + i], 0)
        request = code // TILES
        owner = request // per_row
        tile = (request - owner * per_row) * TILES + (code - request * TILES)
        piece = lax.bitwise_xor(owner, row)
        target = pl.ds(pl.multiple_of(i * TILE, TILE), TILE)
        for j, parts in enumerate(pieces):
            tiles = parts[0].shape[0] // TILE
            for k, part in enumerate(parts):

                @pl.when((piece == j) & (tile // tiles == k))
                def _():
                    source = pl.ds(pl.multiple_of((tile - k * tiles) * TILE, TILE), TILE)
                    pltpu.make_async_copy(part.at[source, :], out.at[target, :], sem).start()

        return carry

    lax.fori_loop(0, TILES, step, 0)
    pltpu.make_async_copy(out, out, sem).wait()


def pick(place, table, pieces, turn, per_row):
    flat, counts = flatten(pieces)
    width = flat[0].shape[1]
    return pl.pallas_call(
        functools.partial(pick_kernel, counts, per_row, turn),
        out_shape=jax.ShapeDtypeStruct((S, width), jnp.bfloat16),
        in_specs=[SMEM, SMEM] + [ANY] * len(flat),
        out_specs=VMEM,
        scratch_shapes=[pltpu.SemaphoreType.DMA],
        compiler_params=params(),
        cost_estimate=cost(0, 4 * S * width),
    )(place, table, *flat)


def spread_kernel(rows, per_row, total, place, lengths, bins, starts, *refs):
    pieces, out = refs[:total], refs[total]
    row = place[0]
    width = out.shape[1]
    for a in range(per_row):
        request = row * per_row + a
        length = lengths[a]
        b = bins[request]
        start = starts[request]
        turn = b // rows
        index = lax.bitwise_xor(b - turn * rows, row) + turn * rows
        tiles = (length + (TILE - 1)) // TILE

        def blank(i, carry):
            out[pl.ds(pl.multiple_of(a * S + i * TILE, TILE), TILE), :] = jnp.zeros((TILE, width), jnp.bfloat16)
            return carry

        lax.fori_loop(tiles, TILES, blank, 0)
        for j in range(total):

            @pl.when(index == j)
            def _():
                def move(i, carry):
                    values = pieces[j][pl.ds(pl.multiple_of((start + i) * TILE, TILE), TILE), :]
                    position = i * TILE + lax.broadcasted_iota(jnp.int32, (TILE, width), 0)
                    kept = jnp.where(position < length, values.astype(jnp.float32), 0.0)
                    out[pl.ds(pl.multiple_of(a * S + i * TILE, TILE), TILE), :] = kept.astype(jnp.bfloat16)
                    return carry

                lax.fori_loop(0, tiles, move, 0)


def spread(place, lengths, bins, starts, pieces, rows, per_row):
    pieces = [block for (block,) in pieces]
    width = pieces[0].shape[1]
    return pl.pallas_call(
        functools.partial(spread_kernel, rows, per_row, len(pieces)),
        out_shape=jax.ShapeDtypeStruct((per_row * S, width), jnp.bfloat16),
        in_specs=[SMEM] * 4 + [VMEM] * len(pieces),
        out_specs=VMEM,
        compiler_params=params(),
        cost_estimate=cost(0, 2 * S * width * (len(pieces) + per_row)),
    )(place, lengths, bins, starts, *pieces)


DOT = functools.partial(jnp.dot, preferred_element_type=jnp.float32)


def DOT_T(left, right):
    return lax.dot_general(left, right, (((1,), (1,)), ((), ())), preferred_element_type=jnp.float32)


def flatten(parts):
    return [part for entry in parts for part in entry], tuple(len(entry) for entry in parts)


def split(refs, counts):
    refs = list(refs)
    return [tuple(refs.pop(0) for _ in range(count)) for count in counts]


def read_parts(refs, counts):
    at = 0
    for count in counts:
        block = refs[at][...]
        for other in refs[at + 1 : at + count]:
            block = block + other[...]
        at += count
        yield block


def silu(values):
    return values * (1.0 / (1.0 + jnp.exp(-values)))


def row_parts(weights, axis):
    for j, parts in enumerate(weights):
        size = parts[0].shape[axis]
        for k, part in enumerate(parts):
            yield j, part, k * size, size


def retain_kernel(weight_counts, counts, heads, place, decays, cosine, sine, seg_col, seg_row, *refs):
    cols, number = len(counts), sum(counts)
    rows, total_weights = len(weight_counts), sum(weight_counts)
    tokens, weights = refs[:number], split(refs[number : number + total_weights], weight_counts)
    mixed, normed, gathered, sems = refs[number + total_weights :]
    depth = D // rows
    width = D // cols
    parts = ((0, 2 * KEY), (2 * KEY, VAL), (2 * KEY + VAL, VAL))

    for head in range(heads):
        for i, (low, span) in enumerate(parts):
            columns = pl.ds(head * HEAD_WIDTH + low, span)
            for j, part, start, size in row_parts(weights, 0):
                where = pl.ds(pl.multiple_of(lax.bitwise_xor(place[0], j) * depth + start, size), size)
                pltpu.make_async_copy(
                    part.at[:, columns], gathered.at[where, columns], sems.at[head * 3 + i]
                ).start()

    total = jnp.zeros((S, 1), jnp.float32)
    for block in read_parts(tokens, counts):
        values = block.astype(jnp.float32)
        total += jnp.sum(values * values, axis=1, keepdims=True)
    scale = lax.rsqrt(total / D + epsilon)
    for k, block in enumerate(read_parts(tokens, counts)):
        where = pl.ds(pl.multiple_of(lax.bitwise_xor(place[1], k) * width, width), width)
        normed[:, where] = (block.astype(jnp.float32) * scale).astype(jnp.bfloat16)

    def project(head, i):
        low, size = parts[i]
        columns = pl.ds(head * HEAD_WIDTH + low, size)
        view = gathered.at[:, columns]
        pltpu.make_async_copy(view, view, sems.at[head * 3 + i]).wait()
        return DOT(normed[...], gathered[:, columns]).astype(jnp.bfloat16)

    def rotate(values):
        values = values.astype(jnp.float32)
        first, second = values[:, : KEY // 2], values[:, KEY // 2 :]
        cos, sin = cosine[...], sine[...]
        return jnp.concatenate([first * cos - second * sin, first * sin + second * cos], axis=1)

    lag = lax.broadcasted_iota(jnp.int32, (S, S), 0) - lax.broadcasted_iota(jnp.int32, (S, S), 1)
    allowed = (lag >= 0) & (seg_col[...] == seg_row[...])
    span = jnp.where(allowed, lag.astype(jnp.float32), 1e6)
    for head in range(heads):
        both = project(head, 0)
        query = rotate(both[:, :KEY]).astype(jnp.bfloat16)
        keyed = (rotate(both[:, KEY:]) * (1.0 / math.sqrt(KEY))).astype(jnp.bfloat16)
        scores = DOT_T(query, keyed)
        scores = scores * jnp.exp(span * decays[head])
        denom = jnp.sum(scores, axis=1, keepdims=True)
        value = project(head, 1)
        retained = DOT(scores.astype(jnp.bfloat16), value) / jnp.maximum(jnp.abs(denom), 1.0)
        centred = retained - jnp.mean(retained, axis=1, keepdims=True)
        spread_of = jnp.mean(centred * centred, axis=1, keepdims=True)
        grouped = centred * lax.rsqrt(spread_of + epsilon)
        gate = project(head, 2).astype(jnp.float32)
        mixed[:, head * VAL : (head + 1) * VAL] = (silu(gate) * grouped).astype(jnp.bfloat16)


def retain(place, decays, cosine, sine, seg_col, seg_row, tokens, weights):
    rows, cols = len(weights), len(tokens)
    heads = HEADS // cols
    flat, counts = flatten(tokens)
    flat_weights, weight_counts = flatten(weights)
    return pl.pallas_call(
        functools.partial(retain_kernel, weight_counts, counts, heads),
        out_shape=jax.ShapeDtypeStruct((S, heads * VAL), jnp.bfloat16),
        in_specs=[SMEM, SMEM] + [VMEM] * (4 + len(flat)) + [ANY] * len(flat_weights),
        out_specs=VMEM,
        scratch_shapes=[
            pltpu.VMEM((S, D), jnp.bfloat16),
            pltpu.VMEM((D, heads * HEAD_WIDTH), jnp.bfloat16),
            pltpu.SemaphoreType.DMA((heads * 3,)),
        ],
        compiler_params=params(),
        cost_estimate=cost(2 * S * D * HEAD_WIDTH * heads * 1.3, 2 * D * HEAD_WIDTH * heads),
    )(place, decays, cosine, sine, seg_col, seg_row, *flat, *flat_weights)


def load_terms(rows, cols, place, views, gathered, sem):
    ratio = rows // cols
    for j, view, start, size in views:
        owner = lax.bitwise_xor(place[0], j)
        target = owner // ratio
        slot = lax.bitwise_xor(target, place[1]) * ratio + (owner - target * ratio)
        pltpu.make_async_copy(view, gathered.at[slot, pl.ds(start, size), :], sem).start()


def put_terms(rows, cols, left, gathered, sem, outs):
    ratio = rows // cols
    depth = D // rows
    pltpu.make_async_copy(gathered, gathered, sem).wait()
    for slot in range(rows):
        k, i = slot // ratio, slot % ratio
        outs[k][:, i * depth : (i + 1) * depth] = DOT_T(left, gathered[slot]).astype(jnp.bfloat16)


def mix_kernel(weight_counts, cols, place, mixed, *refs):
    rows, number = len(weight_counts), sum(weight_counts)
    weights, outs = split(refs[:number], weight_counts), refs[number : number + cols]
    gathered, sem = refs[number + cols :]
    units = mixed.shape[1]
    views = [
        (j, part.at[:, pl.ds(part.shape[1] - units, units)], start, size)
        for j, part, start, size in row_parts(weights, 0)
    ]
    load_terms(rows, cols, place, views, gathered, sem)
    put_terms(rows, cols, mixed[...], gathered, sem, outs)


def mix(place, mixed, weights, cols):
    rows = len(weights)
    width = D // cols
    flat, weight_counts = flatten(weights)
    return pl.pallas_call(
        functools.partial(mix_kernel, weight_counts, cols),
        out_shape=[jax.ShapeDtypeStruct((S, width), jnp.bfloat16)] * cols,
        in_specs=[SMEM, VMEM] + [ANY] * len(flat),
        out_specs=[VMEM] * cols,
        scratch_shapes=[
            pltpu.VMEM((rows, D // rows, mixed.shape[1]), jnp.bfloat16),
            pltpu.SemaphoreType.DMA,
        ],
        compiler_params=params(),
        cost_estimate=cost(2 * S * D * mixed.shape[1], 2 * D * mixed.shape[1]),
    )(place, mixed, *flat)


def feed_kernel(weight_counts, counts, tile, place, *refs):
    cols, number = len(counts), sum(counts)
    rows, last = len(weight_counts), sum(counts) + sum(weight_counts)
    tokens = refs[:number]
    weights = split(refs[number:last], weight_counts)
    outs = refs[last : last + cols]
    ordered, hidden, gathered, gathered_down, sems, sem_down = refs[last + cols :]
    depth = D // rows
    width = D // cols
    steps = gathered.shape[2] // tile

    for step in range(steps):
        columns = pl.ds(step * tile, tile)
        for j, part, start, size in row_parts(weights, 1):
            where = pl.ds(pl.multiple_of(lax.bitwise_xor(place[0], j) * depth + start, size), size)
            pltpu.make_async_copy(
                part.at[pl.ds(1, 2), :, columns], gathered.at[:, where, columns], sems.at[step]
            ).start()
    views = [(j, part.at[0], start, size) for j, part, start, size in row_parts(weights, 1)]
    load_terms(rows, cols, place, views, gathered_down, sem_down)

    total = jnp.zeros((S, 1), jnp.float32)
    for k, block in enumerate(read_parts(tokens, counts)):
        values = block.astype(jnp.float32)
        total += jnp.sum(values * values, axis=1, keepdims=True)
        where = pl.ds(pl.multiple_of(lax.bitwise_xor(place[1], k) * width, width), width)
        ordered[:, where] = block
    scale = lax.rsqrt(total / D + epsilon)

    for step in range(steps):
        columns = pl.ds(step * tile, tile)
        view = gathered.at[:, :, columns]
        pltpu.make_async_copy(view, view, sems.at[step]).wait()
        gate = DOT(ordered[...], gathered[0, :, columns]) * scale
        up = DOT(ordered[...], gathered[1, :, columns]) * scale
        hidden[:, columns] = (silu(gate) * up).astype(jnp.bfloat16)
    put_terms(rows, cols, hidden[...], gathered_down, sem_down, outs)


def feed(place, tokens, weights):
    rows, cols = len(weights), len(tokens)
    units = weights[0][0].shape[2]
    tile = min(units, 512)
    flat, counts = flatten(tokens)
    flat_weights, weight_counts = flatten(weights)
    return pl.pallas_call(
        functools.partial(feed_kernel, weight_counts, counts, tile),
        out_shape=[jax.ShapeDtypeStruct((S, D // cols), jnp.bfloat16)] * cols,
        in_specs=[SMEM] + [VMEM] * len(flat) + [ANY] * len(flat_weights),
        out_specs=[VMEM] * cols,
        scratch_shapes=[
            pltpu.VMEM((S, D), jnp.bfloat16),
            pltpu.VMEM((S, units), jnp.bfloat16),
            pltpu.VMEM((2, D, units), jnp.bfloat16),
            pltpu.VMEM((rows, D // rows, units), jnp.bfloat16),
            pltpu.SemaphoreType.DMA((units // tile,)),
            pltpu.SemaphoreType.DMA,
        ],
        compiler_params=params(),
        cost_estimate=cost(6 * S * D * units, 6 * D * units),
    )(place, *flat, *flat_weights)


def shards(hidden_states, lengths, qkvg_master, gateup_master, out_master, down_master):
    rows, cols = lax.axis_size("row"), lax.axis_size("col")
    per_row = lengths.shape[0]
    heads = HEADS // cols
    place = jnp.stack([lax.axis_index("row"), lax.axis_index("col")]).astype(jnp.int32)

    depth = qkvg_master.shape[0]
    units = gateup_master.shape[2] // cols
    width = heads * HEAD_WIDTH
    front_cut = cut(cut_front_kernel, (depth, width + units), place, qkvg_master, out_master.T)
    front_parts = exchange(front_cut)
    marked = mark(hidden_states, lengths)
    everyone = gather_rows(after(marked, front_cut[0]), halves=front_parts[1:3])
    front_blocks = join(front_parts, place)
    feed_cut = cut(cut_feed_kernel, (3, depth, units), place, down_master.T, gateup_master)
    all_lengths = read_marks(everyone, per_row)

    table, bins, starts, count = pack(place, all_lengths, rows)

    head_ids = lax.axis_index("col") * heads + jnp.arange(heads)
    decays = jnp.log1p(-jnp.power(2.0, -5.0 - head_ids.astype(jnp.float32)))
    freq = jnp.power(10000.0, -2.0 * jnp.arange(KEY // 2).astype(jnp.float32) / KEY)

    def begin(turn):
        codes = table[turn * TILES : (turn + 1) * TILES]
        segments = jnp.where(codes < 0, -1, codes // TILES)
        seg = jnp.broadcast_to(segments[:, None], (TILES, TILE)).reshape(S)
        positions = ((jnp.maximum(codes, 0) % TILES)[:, None] * TILE + jnp.arange(TILE)[None, :]).reshape(S)
        angle = positions.astype(jnp.float32)[:, None] * freq[None, :]
        own = pick(place, table, everyone, turn, per_row)
        return own, (jnp.cos(angle), jnp.sin(angle), seg[:, None], seg[None, :])

    own, tables = begin(0)
    tokens = gather_cols(own)
    ahead = [tokens[1][0], tokens[2][0]]
    rest = [part for entry in tokens[3:] for part in entry]
    feed_parts = exchange(list(after(tuple(feed_cut), *rest)))
    front_pieces = gather_rows(
        after(front_blocks, *last_parts(everyone)), halves=ahead, core=rest, whole=(*tables, feed_cut[0])
    )

    mixed = retain(place, decays, *tables, tokens, front_pieces)
    terms = mix(place, mixed, front_pieces, cols)
    feed_blocks = join(list(after(tuple(feed_parts), terms[0])), place)
    attended = collect(list(after(tuple(terms), feed_blocks)))
    residual = own.astype(jnp.float32) + added(attended)
    mid_tokens = gather_cols(residual.astype(jnp.bfloat16))
    if rows == 8:
        links = gather_links(feed_blocks, halves=attended[1:])
        feed_pieces = gather_cores(links, earlier=links[6], whole=mid_tokens[3][:1])
    else:
        feed_pieces = gather_rows(feed_blocks)

    weights = (front_blocks[:, :width], feed_blocks[1:], front_blocks[:, width:].T, feed_blocks[0].T)
    weights = lax.optimization_barrier(weights)

    def rest_of_layer(residual, tokens, feed_pieces):
        fed = collect(feed(place, tokens, feed_pieces))
        return gather_rows((residual + added(fed)).astype(jnp.bfloat16), direct=True)

    first = rest_of_layer(residual, mid_tokens, [after(feed_pieces[0], *weights)] + feed_pieces[1:])

    def finish(pieces):
        return spread(place, lengths, bins, starts, pieces, rows, per_row)

    def more(pieces):
        for turn in range(1, per_row):
            own, tables = begin(turn)
            mixed = retain(place, decays, *tables, gather_cols(own), front_pieces)
            attended = collect(mix(place, mixed, front_pieces, cols))
            residual = own.astype(jnp.float32) + added(attended)
            pieces = pieces + rest_of_layer(residual, gather_cols(residual.astype(jnp.bfloat16)), feed_pieces)
        return finish(pieces)

    layer_output = lax.cond(count[0] > rows, more, finish, first)
    return (layer_output,) + weights


def solution(mesh):
    return jax.shard_map(
        shards,
        mesh=mesh,
        in_specs=(
            P("row", "col"),
            P("row"),
            P(("row", "col"), None),
            P(None, ("row", "col"), None),
            P(None, ("row", "col")),
            P(None, ("row", "col")),
        ),
        out_specs=(
            P("row", "col"),
            P("row", "col"),
            P(None, "row", "col"),
            P("col", "row"),
            P("col", "row"),
        ),
        check_vma=False,
    )
```

```python
import functools
import math

import jax
import jax.numpy as jnp
from jax import lax
from jax.experimental import pallas as pl
from jax.experimental.pallas import tpu as pltpu
from jax.sharding import PartitionSpec as P

D = 2048
HEADS = 8
KEY = 256
VAL = 512
S = 512
TILE = 16
TILES = S // TILE
HEAD_WIDTH = 2 * KEY + 2 * VAL

epsilon = 1e-05
VMEM_LIMIT = 56 * 1024 * 1024

SMEM = pl.BlockSpec(memory_space=pltpu.SMEM)
VMEM = pl.BlockSpec(memory_space=pltpu.VMEM)
ANY = pl.BlockSpec(memory_space=pl.ANY)


def params():
    return pltpu.CompilerParams(vmem_limit_bytes=VMEM_LIMIT)


def cost(flops, moved):
    return pl.CostEstimate(flops=int(flops), bytes_accessed=int(moved), transcendentals=0)


def swap(block, axis, step):
    size = lax.axis_size(axis)
    return lax.ppermute(block, axis, [(i, i ^ step) for i in range(size)])


def after(value, *earlier):
    return lax.optimization_barrier((value,) + earlier)[0]


def gather_rows(block, direct=False, halves=(), whole=(), core=()):
    size = lax.axis_size("row")
    pieces = {0: block}
    if size == 8:
        axis = block.ndim - 2
        half = block.shape[axis] // 2
        pieces[2] = swap(block, "row", 2)
        pieces[4] = swap(block, "row", 4)
        if direct:
            pieces[6] = swap(block, "row", 6)
        else:
            across, along = after((pieces[2], pieces[4]), *halves)
            upper = swap(lax.slice_in_dim(along, 0, half, axis=axis), "row", 2)
            lower = swap(lax.slice_in_dim(across, half, 2 * half, axis=axis), "row", 4)
            pieces[6] = jnp.concatenate(after((upper, lower), *whole), axis=axis)
        pieces[0] = after(block, pieces[2], pieces[4])
        bits = [1]
    else:
        bits = [1 << i for i in reversed(range(size.bit_length() - 1))]
    for bit in bits:
        for j in sorted(pieces):
            pieces[j | bit] = swap(after(pieces[j], *core), "row", bit)
    return [pieces[j] for j in range(size)]


def last_parts(pieces):
    return (pieces[6],) if len(pieces) == 8 else (pieces[-1],)


def gather_lengths(lengths):
    size = lax.axis_size("row")
    bit = 1
    while bit < size:
        lengths = jnp.concatenate([lengths, swap(lengths, "row", bit)])
        bit *= 2
    return lengths


def exchange(blocks):
    return [blocks[0]] + [swap(blocks[k], "col", k) for k in range(1, len(blocks))]


def gather_cols(block, between=None):
    size = lax.axis_size("col")
    if size != 4:
        return [(block,)] + [(swap(block, "col", k),) for k in range(1, size)]
    near = swap(block, "col", 1)
    far = swap(block, "col", 2)
    later = between((near, far)) if between else ()
    mine, passed = after((block, far), near, *later)
    middle = lax.ppermute(mine, "col", [(1, 2), (2, 1)])
    ends = lax.ppermute(passed, "col", [(2, 3), (1, 0)])
    return [(block,), (near,), (far,), (middle, ends)]


def collect(terms):
    if lax.axis_size("col") != 4:
        return exchange(terms)
    early = lax.ppermute(terms[3], "col", [(3, 2), (0, 1)])
    middle = lax.ppermute(terms[3], "col", [(1, 2), (2, 1)])
    near = swap(after(terms[1], early), "col", 1)
    both = terms[2].astype(jnp.float32) + early.astype(jnp.float32)
    far = swap(both.astype(jnp.bfloat16), "col", 2)
    return [terms[0], near, far, middle]


def added(parts):
    return sum(part.astype(jnp.float32) for part in parts)


def cut_front_kernel(cols, place, qkvg, out, *blocks):
    units = out.shape[1] // cols
    width = blocks[0].shape[1] - units
    for k in range(cols):
        target = lax.bitwise_xor(place[1], k)
        columns = pl.ds(pl.multiple_of(target * width, 128), width)
        blocks[k][:, :width] = qkvg[:, columns].astype(jnp.bfloat16)
        columns = pl.ds(pl.multiple_of(target * units, 128), units)
        blocks[k][:, width:] = out[:, columns].astype(jnp.bfloat16)


def cut_feed_kernel(cols, place, down, gateup, *blocks):
    units = blocks[0].shape[2]
    for k in range(cols):
        target = lax.bitwise_xor(place[1], k)
        columns = pl.ds(pl.multiple_of(target * units, 128), units)
        blocks[k][0] = down[:, columns].astype(jnp.bfloat16)
        blocks[k][1] = gateup[0, :, columns].astype(jnp.bfloat16)
        blocks[k][2] = gateup[1, :, columns].astype(jnp.bfloat16)


def cut(kernel, shape, place, *masters):
    cols = lax.axis_size("col")
    return pl.pallas_call(
        functools.partial(kernel, cols),
        out_shape=[jax.ShapeDtypeStruct(shape, jnp.bfloat16)] * cols,
        in_specs=[SMEM] + [VMEM] * len(masters),
        out_specs=[VMEM] * cols,
        compiler_params=params(),
        cost_estimate=cost(0, 6 * math.prod(shape) * cols),
    )(place, *masters)


def join_kernel(cols, place, *refs):
    out = refs[cols]
    rows = refs[0].shape[-2]
    for k in range(cols):
        source = lax.bitwise_xor(place[1], k)
        where = pl.ds(pl.multiple_of(source * rows, 16), rows)
        if len(out.shape) == 2:
            out[where, :] = refs[k][...]
        else:
            out[:, where, :] = refs[k][...]


def join(blocks, place):
    cols = len(blocks)
    shape = list(blocks[0].shape)
    shape[-2] *= cols
    return pl.pallas_call(
        functools.partial(join_kernel, cols),
        out_shape=jax.ShapeDtypeStruct(tuple(shape), jnp.bfloat16),
        in_specs=[SMEM] + [VMEM] * cols,
        out_specs=VMEM,
        compiler_params=params(),
        cost_estimate=cost(0, 4 * math.prod(shape)),
    )(place, *blocks)


def pack_kernel(requests, rows, passes, place, lengths, table, bins, starts, count, used):
    row = place[0]
    per_row = requests // rows

    def clear(i, carry):
        table[i] = -1
        return carry

    lax.fori_loop(0, passes * TILES, clear, 0)

    def clear_used(i, carry):
        used[i] = 0
        return carry

    lax.fori_loop(0, requests, clear_used, 0)

    def put(q, top):
        owner = q // per_row
        length = lengths[lax.bitwise_xor(owner, row) * per_row + (q - owner * per_row)]
        tiles = (length + (TILE - 1)) // TILE

        def look(i, best):
            b = requests - 1 - i
            return jnp.where(used[b] + tiles <= TILES, b, best)

        b = lax.fori_loop(0, requests, look, requests - 1)
        start = used[b]
        used[b] = start + tiles
        bins[q] = b
        starts[q] = start
        turn = b // rows

        @pl.when(b - turn * rows == row)
        def _():
            def note(i, carry):
                table[turn * TILES + start + i] = q * TILES + i
                return carry

            lax.fori_loop(0, tiles, note, 0)

        return jnp.maximum(top, b + 1)

    count[0] = lax.fori_loop(0, requests, put, 0)


def pack(place, lengths, rows):
    requests = lengths.shape[0]
    passes = requests // rows
    whole = lambda n: jax.ShapeDtypeStruct((n,), jnp.int32)
    return pl.pallas_call(
        functools.partial(pack_kernel, requests, rows, passes),
        out_shape=[whole(passes * TILES), whole(requests), whole(requests), whole(1)],
        in_specs=[SMEM, SMEM],
        out_specs=[SMEM] * 4,
        scratch_shapes=[pltpu.SMEM((requests,), jnp.int32)],
        compiler_params=params(),
    )(place, lengths)


def pick_kernel(rows, per_row, turn, place, table, *refs):
    pieces, out, sem = refs[:rows], refs[rows], refs[rows + 1]
    row = place[0]

    def step(i, carry):
        code = jnp.maximum(table[turn * TILES + i], 0)
        request = code // TILES
        owner = request // per_row
        tile = (request - owner * per_row) * TILES + (code - request * TILES)
        piece = lax.bitwise_xor(owner, row)
        source = pl.ds(pl.multiple_of(tile * TILE, TILE), TILE)
        target = pl.ds(pl.multiple_of(i * TILE, TILE), TILE)
        for j in range(rows):

            @pl.when(piece == j)
            def _():
                pltpu.make_async_copy(pieces[j].at[source, :], out.at[target, :], sem).start()

        return carry

    lax.fori_loop(0, TILES, step, 0)
    pltpu.make_async_copy(out, out, sem).wait()


def pick(place, table, pieces, turn):
    rows = len(pieces)
    width = pieces[0].shape[1]
    return pl.pallas_call(
        functools.partial(pick_kernel, rows, pieces[0].shape[0] // S, turn),
        out_shape=jax.ShapeDtypeStruct((S, width), jnp.bfloat16),
        in_specs=[SMEM, SMEM] + [ANY] * rows,
        out_specs=VMEM,
        scratch_shapes=[pltpu.SemaphoreType.DMA],
        compiler_params=params(),
        cost_estimate=cost(0, 4 * S * width),
    )(place, table, *pieces)


def spread_kernel(rows, per_row, total, place, lengths, bins, starts, *refs):
    pieces, out = refs[:total], refs[total]
    row = place[0]
    width = out.shape[1]
    for a in range(per_row):
        request = row * per_row + a
        length = lengths[a]
        b = bins[request]
        start = starts[request]
        turn = b // rows
        index = lax.bitwise_xor(b - turn * rows, row) + turn * rows
        tiles = (length + (TILE - 1)) // TILE

        def blank(i, carry):
            out[pl.ds(pl.multiple_of(a * S + i * TILE, TILE), TILE), :] = jnp.zeros((TILE, width), jnp.bfloat16)
            return carry

        lax.fori_loop(tiles, TILES, blank, 0)
        for j in range(total):

            @pl.when(index == j)
            def _():
                def move(i, carry):
                    values = pieces[j][pl.ds(pl.multiple_of((start + i) * TILE, TILE), TILE), :]
                    position = i * TILE + lax.broadcasted_iota(jnp.int32, (TILE, width), 0)
                    kept = jnp.where(position < length, values.astype(jnp.float32), 0.0)
                    out[pl.ds(pl.multiple_of(a * S + i * TILE, TILE), TILE), :] = kept.astype(jnp.bfloat16)
                    return carry

                lax.fori_loop(0, tiles, move, 0)


def spread(place, lengths, bins, starts, pieces, rows, per_row):
    width = pieces[0].shape[1]
    return pl.pallas_call(
        functools.partial(spread_kernel, rows, per_row, len(pieces)),
        out_shape=jax.ShapeDtypeStruct((per_row * S, width), jnp.bfloat16),
        in_specs=[SMEM] * 4 + [VMEM] * len(pieces),
        out_specs=VMEM,
        compiler_params=params(),
        cost_estimate=cost(0, 2 * S * width * (len(pieces) + per_row)),
    )(place, lengths, bins, starts, *pieces)


DOT = functools.partial(jnp.dot, preferred_element_type=jnp.float32)


def DOT_T(left, right):
    return lax.dot_general(left, right, (((1,), (1,)), ((), ())), preferred_element_type=jnp.float32)


def flatten(parts):
    return [part for entry in parts for part in entry], tuple(len(entry) for entry in parts)


def read_parts(refs, counts):
    at = 0
    for count in counts:
        block = refs[at][...]
        for other in refs[at + 1 : at + count]:
            block = block + other[...]
        at += count
        yield block


def silu(values):
    return values * (1.0 / (1.0 + jnp.exp(-values)))


def retain_kernel(rows, counts, heads, place, decays, cosine, sine, seg_col, seg_row, *refs):
    cols, number = len(counts), sum(counts)
    tokens, weights = refs[:number], refs[number : number + rows]
    mixed, normed, gathered, sems = refs[number + rows :]
    depth = D // rows
    width = D // cols
    parts = ((0, 2 * KEY), (2 * KEY, VAL), (2 * KEY + VAL, VAL))

    for head in range(heads):
        for i, (low, size) in enumerate(parts):
            columns = pl.ds(head * HEAD_WIDTH + low, size)
            for j in range(rows):
                where = pl.ds(pl.multiple_of(lax.bitwise_xor(place[0], j) * depth, depth), depth)
                pltpu.make_async_copy(
                    weights[j].at[:, columns], gathered.at[where, columns], sems.at[head * 3 + i]
                ).start()

    total = jnp.zeros((S, 1), jnp.float32)
    for block in read_parts(tokens, counts):
        values = block.astype(jnp.float32)
        total += jnp.sum(values * values, axis=1, keepdims=True)
    scale = lax.rsqrt(total / D + epsilon)
    for k, block in enumerate(read_parts(tokens, counts)):
        where = pl.ds(pl.multiple_of(lax.bitwise_xor(place[1], k) * width, width), width)
        normed[:, where] = (block.astype(jnp.float32) * scale).astype(jnp.bfloat16)

    def project(head, i):
        low, size = parts[i]
        columns = pl.ds(head * HEAD_WIDTH + low, size)
        view = gathered.at[:, columns]
        pltpu.make_async_copy(view, view, sems.at[head * 3 + i]).wait()
        return DOT(normed[...], gathered[:, columns]).astype(jnp.bfloat16)

    def rotate(values):
        values = values.astype(jnp.float32)
        first, second = values[:, : KEY // 2], values[:, KEY // 2 :]
        cos, sin = cosine[...], sine[...]
        return jnp.concatenate([first * cos - second * sin, first * sin + second * cos], axis=1)

    lag = lax.broadcasted_iota(jnp.int32, (S, S), 0) - lax.broadcasted_iota(jnp.int32, (S, S), 1)
    allowed = (lag >= 0) & (seg_col[...] == seg_row[...])
    span = jnp.where(allowed, lag.astype(jnp.float32), 1e6)
    for head in range(heads):
        both = project(head, 0)
        query = rotate(both[:, :KEY]).astype(jnp.bfloat16)
        keyed = (rotate(both[:, KEY:]) * (1.0 / math.sqrt(KEY))).astype(jnp.bfloat16)
        scores = DOT_T(query, keyed)
        scores = scores * jnp.exp(span * decays[head])
        denom = jnp.sum(scores, axis=1, keepdims=True)
        value = project(head, 1)
        retained = DOT(scores.astype(jnp.bfloat16), value) / jnp.maximum(jnp.abs(denom), 1.0)
        centred = retained - jnp.mean(retained, axis=1, keepdims=True)
        spread_of = jnp.mean(centred * centred, axis=1, keepdims=True)
        grouped = centred * lax.rsqrt(spread_of + epsilon)
        gate = project(head, 2).astype(jnp.float32)
        mixed[:, head * VAL : (head + 1) * VAL] = (silu(gate) * grouped).astype(jnp.bfloat16)


def retain(place, decays, cosine, sine, seg_col, seg_row, tokens, weights):
    rows, cols = len(weights), len(tokens)
    heads = HEADS // cols
    flat, counts = flatten(tokens)
    return pl.pallas_call(
        functools.partial(retain_kernel, rows, counts, heads),
        out_shape=jax.ShapeDtypeStruct((S, heads * VAL), jnp.bfloat16),
        in_specs=[SMEM, SMEM] + [VMEM] * (4 + len(flat)) + [ANY] * rows,
        out_specs=VMEM,
        scratch_shapes=[
            pltpu.VMEM((S, D), jnp.bfloat16),
            pltpu.VMEM((D, heads * HEAD_WIDTH), jnp.bfloat16),
            pltpu.SemaphoreType.DMA((heads * 3,)),
        ],
        compiler_params=params(),
        cost_estimate=cost(2 * S * D * HEAD_WIDTH * heads * 1.3, 2 * D * HEAD_WIDTH * heads),
    )(place, decays, cosine, sine, seg_col, seg_row, *flat, *weights)


def load_terms(rows, cols, place, views, gathered, sem):
    ratio = rows // cols
    for j in range(rows):
        owner = lax.bitwise_xor(place[0], j)
        target = owner // ratio
        slot = lax.bitwise_xor(target, place[1]) * ratio + (owner - target * ratio)
        pltpu.make_async_copy(views[j], gathered.at[slot], sem).start()


def put_terms(rows, cols, left, gathered, sem, outs):
    ratio = rows // cols
    depth = D // rows
    pltpu.make_async_copy(gathered, gathered, sem).wait()
    for slot in range(rows):
        k, i = slot // ratio, slot % ratio
        outs[k][:, i * depth : (i + 1) * depth] = DOT_T(left, gathered[slot]).astype(jnp.bfloat16)


def mix_kernel(rows, cols, place, mixed, *refs):
    weights, outs = refs[:rows], refs[rows : rows + cols]
    gathered, sem = refs[rows + cols :]
    units = mixed.shape[1]
    views = [ref.at[:, pl.ds(ref.shape[1] - units, units)] for ref in weights]
    load_terms(rows, cols, place, views, gathered, sem)
    put_terms(rows, cols, mixed[...], gathered, sem, outs)


def mix(place, mixed, weights, cols):
    rows = len(weights)
    width = D // cols
    return pl.pallas_call(
        functools.partial(mix_kernel, rows, cols),
        out_shape=[jax.ShapeDtypeStruct((S, width), jnp.bfloat16)] * cols,
        in_specs=[SMEM, VMEM] + [ANY] * rows,
        out_specs=[VMEM] * cols,
        scratch_shapes=[
            pltpu.VMEM((rows, D // rows, mixed.shape[1]), jnp.bfloat16),
            pltpu.SemaphoreType.DMA,
        ],
        compiler_params=params(),
        cost_estimate=cost(2 * S * D * mixed.shape[1], 2 * D * mixed.shape[1]),
    )(place, mixed, *weights)


def feed_kernel(rows, counts, tile, place, *refs):
    cols, number = len(counts), sum(counts)
    tokens = refs[:number]
    weights = refs[number : number + rows]
    outs = refs[number + rows : number + rows + cols]
    ordered, hidden, gathered, gathered_down, sems, sem_down = refs[number + rows + cols :]
    depth = D // rows
    width = D // cols
    steps = gathered.shape[2] // tile

    for step in range(steps):
        columns = pl.ds(step * tile, tile)
        for j in range(rows):
            where = pl.ds(pl.multiple_of(lax.bitwise_xor(place[0], j) * depth, depth), depth)
            pltpu.make_async_copy(
                weights[j].at[pl.ds(1, 2), :, columns], gathered.at[:, where, columns], sems.at[step]
            ).start()
    load_terms(rows, cols, place, [ref.at[0] for ref in weights], gathered_down, sem_down)

    total = jnp.zeros((S, 1), jnp.float32)
    for k, block in enumerate(read_parts(tokens, counts)):
        values = block.astype(jnp.float32)
        total += jnp.sum(values * values, axis=1, keepdims=True)
        where = pl.ds(pl.multiple_of(lax.bitwise_xor(place[1], k) * width, width), width)
        ordered[:, where] = block
    scale = lax.rsqrt(total / D + epsilon)

    for step in range(steps):
        columns = pl.ds(step * tile, tile)
        view = gathered.at[:, :, columns]
        pltpu.make_async_copy(view, view, sems.at[step]).wait()
        gate = DOT(ordered[...], gathered[0, :, columns]) * scale
        up = DOT(ordered[...], gathered[1, :, columns]) * scale
        hidden[:, columns] = (silu(gate) * up).astype(jnp.bfloat16)
    put_terms(rows, cols, hidden[...], gathered_down, sem_down, outs)


def feed(place, tokens, weights):
    rows, cols = len(weights), len(tokens)
    units = weights[0].shape[2]
    tile = min(units, 512)
    flat, counts = flatten(tokens)
    return pl.pallas_call(
        functools.partial(feed_kernel, rows, counts, tile),
        out_shape=[jax.ShapeDtypeStruct((S, D // cols), jnp.bfloat16)] * cols,
        in_specs=[SMEM] + [VMEM] * len(flat) + [ANY] * rows,
        out_specs=[VMEM] * cols,
        scratch_shapes=[
            pltpu.VMEM((S, D), jnp.bfloat16),
            pltpu.VMEM((S, units), jnp.bfloat16),
            pltpu.VMEM((2, D, units), jnp.bfloat16),
            pltpu.VMEM((rows, D // rows, units), jnp.bfloat16),
            pltpu.SemaphoreType.DMA((units // tile,)),
            pltpu.SemaphoreType.DMA,
        ],
        compiler_params=params(),
        cost_estimate=cost(6 * S * D * units, 6 * D * units),
    )(place, *flat, *weights)


def shards(hidden_states, lengths, qkvg_master, gateup_master, out_master, down_master):
    rows, cols = lax.axis_size("row"), lax.axis_size("col")
    per_row = lengths.shape[0]
    heads = HEADS // cols
    place = jnp.stack([lax.axis_index("row"), lax.axis_index("col")]).astype(jnp.int32)

    all_lengths = gather_lengths(lengths)
    depth = qkvg_master.shape[0]
    units = gateup_master.shape[2] // cols
    width = heads * HEAD_WIDTH
    front_cut = cut(cut_front_kernel, (depth, width + units), place, qkvg_master, out_master.T)
    front_parts = exchange(front_cut)
    everyone = gather_rows(after(hidden_states, all_lengths), halves=front_parts[1:3])
    front_blocks = join(front_parts, place)

    table, bins, starts, count = pack(place, all_lengths, rows)

    head_ids = lax.axis_index("col") * heads + jnp.arange(heads)
    decays = jnp.log1p(-jnp.power(2.0, -5.0 - head_ids.astype(jnp.float32)))
    freq = jnp.power(10000.0, -2.0 * jnp.arange(KEY // 2).astype(jnp.float32) / KEY)

    def begin(turn):
        codes = table[turn * TILES : (turn + 1) * TILES]
        segments = jnp.where(codes < 0, -1, codes // TILES)
        seg = jnp.broadcast_to(segments[:, None], (TILES, TILE)).reshape(S)
        positions = ((jnp.maximum(codes, 0) % TILES)[:, None] * TILE + jnp.arange(TILE)[None, :]).reshape(S)
        angle = positions.astype(jnp.float32)[:, None] * freq[None, :]
        own = pick(place, table, everyone, turn)
        return own, (jnp.cos(angle), jnp.sin(angle), seg[:, None], seg[None, :])

    own, tables = begin(0)
    tokens = gather_cols(own)
    ahead = [tokens[1][0], tokens[2][0]]
    rest = [part for entry in tokens[3:] for part in entry]
    feed_cut = cut(cut_feed_kernel, (3, depth, units), place, down_master.T, gateup_master)
    front_pieces = gather_rows(
        after(front_blocks, *last_parts(everyone)), halves=ahead, whole=(*rest, *tables, feed_cut[0])
    )
    feed_parts = exchange(list(after(tuple(feed_cut), *rest)))

    mixed = retain(place, decays, *tables, tokens, front_pieces)
    terms = mix(place, mixed, front_pieces, cols)
    attended = collect(terms)
    feed_blocks = join(list(after(tuple(feed_parts), terms[0])), place)
    residual = own.astype(jnp.float32) + added(attended)
    feed_pieces = []

    def between(first):
        feed_pieces.extend(gather_rows(feed_blocks, halves=attended[1:], whole=first))
        return feed_pieces[1:6:2]

    mid_tokens = gather_cols(residual.astype(jnp.bfloat16), between)
    if not feed_pieces:
        feed_pieces = gather_rows(feed_blocks)

    weights = (front_blocks[:, :width], feed_blocks[1:], front_blocks[:, width:].T, feed_blocks[0].T)
    weights = lax.optimization_barrier(weights)

    def rest_of_layer(residual, tokens, feed_pieces):
        terms = feed(place, tokens, feed_pieces)
        return gather_rows((residual + added(collect(terms))).astype(jnp.bfloat16), direct=True)

    first = rest_of_layer(residual, mid_tokens, [after(feed_pieces[0], *weights)] + feed_pieces[1:])

    def finish(pieces):
        return spread(place, lengths, bins, starts, pieces, rows, per_row)

    def more(pieces):
        for turn in range(1, per_row):
            own, tables = begin(turn)
            mixed = retain(place, decays, *tables, gather_cols(own), front_pieces)
            attended = collect(mix(place, mixed, front_pieces, cols))
            residual = own.astype(jnp.float32) + added(attended)
            pieces = pieces + rest_of_layer(residual, gather_cols(residual.astype(jnp.bfloat16)), feed_pieces)
        return finish(pieces)

    layer_output = lax.cond(count[0] > rows, more, finish, first)
    return (layer_output,) + weights


def solution(mesh):
    return jax.shard_map(
        shards,
        mesh=mesh,
        in_specs=(
            P("row", "col"),
            P("row"),
            P(("row", "col"), None),
            P(None, ("row", "col"), None),
            P(None, ("row", "col")),
            P(None, ("row", "col")),
        ),
        out_specs=(
            P("row", "col"),
            P("row", "col"),
            P(None, "row", "col"),
            P("col", "row"),
            P("col", "row"),
        ),
        check_vma=False,
    )
```

```python
import functools
import math

import jax
import jax.numpy as jnp
from jax import lax
from jax.experimental import pallas as pl
from jax.experimental.pallas import tpu as pltpu
from jax.sharding import PartitionSpec as P

D = 2048
HEADS = 8
KEY = 256
VAL = 512
S = 512
TILE = 16
TILES = S // TILE
HEAD_WIDTH = 2 * KEY + 2 * VAL

epsilon = 1e-05
VMEM_LIMIT = 56 * 1024 * 1024

SMEM = pl.BlockSpec(memory_space=pltpu.SMEM)
VMEM = pl.BlockSpec(memory_space=pltpu.VMEM)
ANY = pl.BlockSpec(memory_space=pl.ANY)


def params():
    return pltpu.CompilerParams(vmem_limit_bytes=VMEM_LIMIT)


def cost(flops, moved):
    return pl.CostEstimate(flops=int(flops), bytes_accessed=int(moved), transcendentals=0)


def swap(block, axis, step):
    size = lax.axis_size(axis)
    return lax.ppermute(block, axis, [(i, i ^ step) for i in range(size)])


def along_col(block, pairs, even):
    if not even:
        return lax.ppermute(block, "col", pairs)
    rows, cols = lax.axis_size("row"), lax.axis_size("col")
    pairs = [(row * cols + a, row * cols + b) for row in range(0, rows, 2) for a, b in pairs]
    return lax.ppermute(block, ("row", "col"), pairs)


def after(value, *earlier):
    return lax.optimization_barrier((value,) + earlier)[0]


def gather_rows(block, direct=False, halves=(), whole=(), core=()):
    size = lax.axis_size("row")
    pieces = {0: block}
    if size == 8:
        axis = block.ndim - 2
        half = block.shape[axis] // 2
        pieces[2] = swap(block, "row", 2)
        pieces[4] = swap(block, "row", 4)
        if direct:
            pieces[6] = swap(block, "row", 6)
        else:
            across, along = after((pieces[2], pieces[4]), *halves)
            upper = swap(lax.slice_in_dim(along, 0, half, axis=axis), "row", 2)
            lower = swap(lax.slice_in_dim(across, half, 2 * half, axis=axis), "row", 4)
            pieces[6] = jnp.concatenate(after((upper, lower), *whole), axis=axis)
        pieces[0] = after(block, pieces[2], pieces[4])
        bits = [1]
    else:
        bits = [1 << i for i in reversed(range(size.bit_length() - 1))]
    for bit in bits:
        for j in sorted(pieces):
            pieces[j | bit] = swap(after(pieces[j], *core), "row", bit)
    return [pieces[j] for j in range(size)]


def last_parts(pieces):
    return (pieces[6],) if len(pieces) == 8 else (pieces[-1],)


def gather_lengths(lengths):
    size = lax.axis_size("row")
    bit = 1
    while bit < size:
        lengths = jnp.concatenate([lengths, swap(lengths, "row", bit)])
        bit *= 2
    return lengths


def exchange(blocks):
    return [blocks[0]] + [swap(blocks[k], "col", k) for k in range(1, len(blocks))]


def gather_cols(block, between=None, even=False):
    size = lax.axis_size("col")
    if size != 4:
        return [(block,)] + [(swap(block, "col", k),) for k in range(1, size)]
    near = along_col(block, [(0, 1), (1, 0), (2, 3), (3, 2)], even)
    far = along_col(block, [(0, 2), (2, 0), (1, 3), (3, 1)], even)
    later = between((near, far)) if between else ()
    mine, passed = after((block, far), near, *later)
    middle = along_col(mine, [(1, 2), (2, 1)], even)
    ends = along_col(passed, [(2, 3), (1, 0)], even)
    return [(block,), (near,), (far,), (middle, ends)]


def collect(terms, even=False):
    if lax.axis_size("col") != 4:
        return exchange(terms)
    early = along_col(terms[3], [(3, 2), (0, 1)], even)
    middle = along_col(terms[3], [(1, 2), (2, 1)], even)
    near = along_col(after(terms[1], early), [(0, 1), (1, 0), (2, 3), (3, 2)], even)
    both = terms[2].astype(jnp.float32) + early.astype(jnp.float32)
    far = along_col(both.astype(jnp.bfloat16), [(0, 2), (2, 0), (1, 3), (3, 1)], even)
    return [terms[0], near, far, middle]


def gather_even(block):
    rows = lax.axis_size("row")
    pieces = [block]
    for j in (2, 4, 6):
        pieces.append(lax.ppermute(block, "row", [(i, i ^ j) for i in range(0, rows, 2)]))
    return pieces + [lax.ppermute(piece, "row", [(i, i + 1) for i in range(0, rows, 2)]) for piece in pieces]


def added(parts):
    return sum(part.astype(jnp.float32) for part in parts)


def cut_front_kernel(cols, place, qkvg, out, *blocks):
    units = out.shape[1] // cols
    width = blocks[0].shape[1] - units
    for k in range(cols):
        target = lax.bitwise_xor(place[1], k)
        columns = pl.ds(pl.multiple_of(target * width, 128), width)
        blocks[k][:, :width] = qkvg[:, columns].astype(jnp.bfloat16)
        columns = pl.ds(pl.multiple_of(target * units, 128), units)
        blocks[k][:, width:] = out[:, columns].astype(jnp.bfloat16)


def cut_feed_kernel(cols, place, down, gateup, *blocks):
    units = blocks[0].shape[2]
    for k in range(cols):
        target = lax.bitwise_xor(place[1], k)
        columns = pl.ds(pl.multiple_of(target * units, 128), units)
        blocks[k][0] = down[:, columns].astype(jnp.bfloat16)
        blocks[k][1] = gateup[0, :, columns].astype(jnp.bfloat16)
        blocks[k][2] = gateup[1, :, columns].astype(jnp.bfloat16)


def cut(kernel, shape, place, *masters):
    cols = lax.axis_size("col")
    return pl.pallas_call(
        functools.partial(kernel, cols),
        out_shape=[jax.ShapeDtypeStruct(shape, jnp.bfloat16)] * cols,
        in_specs=[SMEM] + [VMEM] * len(masters),
        out_specs=[VMEM] * cols,
        compiler_params=params(),
        cost_estimate=cost(0, 6 * math.prod(shape) * cols),
    )(place, *masters)


def join_kernel(cols, place, *refs):
    out = refs[cols]
    rows = refs[0].shape[-2]
    for k in range(cols):
        source = lax.bitwise_xor(place[1], k)
        where = pl.ds(pl.multiple_of(source * rows, 16), rows)
        if len(out.shape) == 2:
            out[where, :] = refs[k][...]
        else:
            out[:, where, :] = refs[k][...]


def join(blocks, place):
    cols = len(blocks)
    shape = list(blocks[0].shape)
    shape[-2] *= cols
    return pl.pallas_call(
        functools.partial(join_kernel, cols),
        out_shape=jax.ShapeDtypeStruct(tuple(shape), jnp.bfloat16),
        in_specs=[SMEM] + [VMEM] * cols,
        out_specs=VMEM,
        compiler_params=params(),
        cost_estimate=cost(0, 4 * math.prod(shape)),
    )(place, *blocks)


def deliver_kernel(front, feed, qkvg, gateup, out, down):
    width = qkvg.shape[1]
    turned = lambda values: values.astype(jnp.float32).T.astype(jnp.bfloat16)
    qkvg[...] = front[:, :width]
    gateup[...] = feed[1:]
    out[...] = turned(front[:, width:])
    down[...] = turned(feed[0])


def deliver(front, feed, width):
    depth, units = feed.shape[1:]
    shapes = [(depth, width), (2, depth, units), (units, depth), (units, depth)]
    return tuple(
        pl.pallas_call(
            deliver_kernel,
            out_shape=[jax.ShapeDtypeStruct(shape, jnp.bfloat16) for shape in shapes],
            in_specs=[VMEM] * 2,
            out_specs=[VMEM] * 4,
            compiler_params=params(),
            cost_estimate=cost(0, 4 * depth * (width + 4 * units)),
        )(front, feed)
    )


def pack_kernel(requests, rows, passes, place, lengths, table, bins, starts, count, used):
    row = place[0]
    per_row = requests // rows

    def clear(i, carry):
        table[i] = -1
        return carry

    lax.fori_loop(0, (passes + 1) * TILES, clear, 0)

    def clear_used(i, carry):
        used[i] = 0
        return carry

    lax.fori_loop(0, requests, clear_used, 0)

    def put(q, top):
        owner = q // per_row
        length = lengths[lax.bitwise_xor(owner, row) * per_row + (q - owner * per_row)]
        tiles = (length + (TILE - 1)) // TILE

        def look(i, best):
            b = requests - 1 - i
            return jnp.where(used[b] + tiles <= TILES, b, best)

        b = lax.fori_loop(0, requests, look, requests - 1)
        start = used[b]
        used[b] = start + tiles
        bins[q] = b
        starts[q] = start
        turn = b // rows

        @pl.when(b - turn * rows == row)
        def _():
            def note(i, carry):
                table[turn * TILES + start + i] = q * TILES + i
                return carry

            lax.fori_loop(0, tiles, note, 0)

        @pl.when((turn == 1) & ((b - rows) * 2 == row))
        def _():
            def note(i, carry):
                table[passes * TILES + start + i] = q * TILES + i
                return carry

            lax.fori_loop(0, tiles, note, 0)

        return jnp.maximum(top, b + 1)

    count[0] = lax.fori_loop(0, requests, put, 0)


def pack(place, lengths, rows):
    requests = lengths.shape[0]
    passes = requests // rows
    whole = lambda n: jax.ShapeDtypeStruct((n,), jnp.int32)
    return pl.pallas_call(
        functools.partial(pack_kernel, requests, rows, passes),
        out_shape=[whole((passes + 1) * TILES), whole(requests), whole(requests), whole(1)],
        in_specs=[SMEM, SMEM],
        out_specs=[SMEM] * 4,
        scratch_shapes=[pltpu.SMEM((requests,), jnp.int32)],
        compiler_params=params(),
    )(place, lengths)


def pick_kernel(rows, per_row, turn, place, table, *refs):
    pieces, out, sem = refs[:rows], refs[rows], refs[rows + 1]
    row = place[0]

    def step(i, carry):
        code = jnp.maximum(table[turn * TILES + i], 0)
        request = code // TILES
        owner = request // per_row
        tile = (request - owner * per_row) * TILES + (code - request * TILES)
        piece = lax.bitwise_xor(owner, row)
        source = pl.ds(pl.multiple_of(tile * TILE, TILE), TILE)
        target = pl.ds(pl.multiple_of(i * TILE, TILE), TILE)
        for j in range(rows):

            @pl.when(piece == j)
            def _():
                pltpu.make_async_copy(pieces[j].at[source, :], out.at[target, :], sem).start()

        return carry

    lax.fori_loop(0, TILES, step, 0)
    pltpu.make_async_copy(out, out, sem).wait()


def pick(place, table, pieces, turn):
    rows = len(pieces)
    width = pieces[0].shape[1]
    return pl.pallas_call(
        functools.partial(pick_kernel, rows, pieces[0].shape[0] // S, turn),
        out_shape=jax.ShapeDtypeStruct((S, width), jnp.bfloat16),
        in_specs=[SMEM, SMEM] + [ANY] * rows,
        out_specs=VMEM,
        scratch_shapes=[pltpu.SemaphoreType.DMA],
        compiler_params=params(),
        cost_estimate=cost(0, 4 * S * width),
    )(place, table, *pieces)


def spread_kernel(rows, per_row, total, few, place, lengths, bins, starts, *refs):
    pieces, out = refs[:total], refs[total]
    row = place[0]
    width = out.shape[1]
    for a in range(per_row):
        request = row * per_row + a
        length = lengths[a]
        b = bins[request]
        start = starts[request]
        turn = b // rows
        index = lax.bitwise_xor(b - turn * rows, row) + turn * rows
        if few:
            chip = row // 2
            other = rows + lax.bitwise_xor(b - rows, chip) + 4 * (row - 2 * chip)
            index = jnp.where(turn == 1, other, index)
        tiles = (length + (TILE - 1)) // TILE

        def blank(i, carry):
            out[pl.ds(pl.multiple_of(a * S + i * TILE, TILE), TILE), :] = jnp.zeros((TILE, width), jnp.bfloat16)
            return carry

        lax.fori_loop(tiles, TILES, blank, 0)
        for j in range(total):

            @pl.when(index == j)
            def _():
                def move(i, carry):
                    values = pieces[j][pl.ds(pl.multiple_of((start + i) * TILE, TILE), TILE), :]
                    position = i * TILE + lax.broadcasted_iota(jnp.int32, (TILE, width), 0)
                    kept = jnp.where(position < length, values.astype(jnp.float32), 0.0)
                    out[pl.ds(pl.multiple_of(a * S + i * TILE, TILE), TILE), :] = kept.astype(jnp.bfloat16)
                    return carry

                lax.fori_loop(0, tiles, move, 0)


def spread(place, lengths, bins, starts, pieces, rows, per_row, few=False):
    width = pieces[0].shape[1]
    return pl.pallas_call(
        functools.partial(spread_kernel, rows, per_row, len(pieces), few),
        out_shape=jax.ShapeDtypeStruct((per_row * S, width), jnp.bfloat16),
        in_specs=[SMEM] * 4 + [VMEM] * len(pieces),
        out_specs=VMEM,
        compiler_params=params(),
        cost_estimate=cost(0, 2 * S * width * (len(pieces) + per_row)),
    )(place, lengths, bins, starts, *pieces)


DOT = functools.partial(jnp.dot, preferred_element_type=jnp.float32)


def DOT_T(left, right):
    return lax.dot_general(left, right, (((1,), (1,)), ((), ())), preferred_element_type=jnp.float32)


def flatten(parts):
    return [part for entry in parts for part in entry], tuple(len(entry) for entry in parts)


def read_parts(refs, counts):
    at = 0
    for count in counts:
        block = refs[at][...]
        for other in refs[at + 1 : at + count]:
            block = block + other[...]
        at += count
        yield block


def silu(values):
    return values * (1.0 / (1.0 + jnp.exp(-values)))


def retain_kernel(rows, counts, heads, place, decays, cosine, sine, seg_col, seg_row, *refs):
    cols, number = len(counts), sum(counts)
    tokens, weights = refs[:number], refs[number : number + rows]
    mixed, normed, gathered, sems = refs[number + rows :]
    depth = D // rows
    width = D // cols
    parts = ((0, 2 * KEY), (2 * KEY, VAL), (2 * KEY + VAL, VAL))

    for head in range(heads):
        for i, (low, size) in enumerate(parts):
            columns = pl.ds(head * HEAD_WIDTH + low, size)
            for j in range(rows):
                where = pl.ds(pl.multiple_of(lax.bitwise_xor(place[0], j) * depth, depth), depth)
                pltpu.make_async_copy(
                    weights[j].at[:, columns], gathered.at[where, columns], sems.at[head * 3 + i]
                ).start()

    total = jnp.zeros((S, 1), jnp.float32)
    for block in read_parts(tokens, counts):
        values = block.astype(jnp.float32)
        total += jnp.sum(values * values, axis=1, keepdims=True)
    scale = lax.rsqrt(total / D + epsilon)
    for k, block in enumerate(read_parts(tokens, counts)):
        where = pl.ds(pl.multiple_of(lax.bitwise_xor(place[1], k) * width, width), width)
        normed[:, where] = (block.astype(jnp.float32) * scale).astype(jnp.bfloat16)

    def project(head, i):
        low, size = parts[i]
        columns = pl.ds(head * HEAD_WIDTH + low, size)
        view = gathered.at[:, columns]
        pltpu.make_async_copy(view, view, sems.at[head * 3 + i]).wait()
        return DOT(normed[...], gathered[:, columns]).astype(jnp.bfloat16)

    def rotate(values):
        values = values.astype(jnp.float32)
        first, second = values[:, : KEY // 2], values[:, KEY // 2 :]
        cos, sin = cosine[...], sine[...]
        return jnp.concatenate([first * cos - second * sin, first * sin + second * cos], axis=1)

    lag = lax.broadcasted_iota(jnp.int32, (S, S), 0) - lax.broadcasted_iota(jnp.int32, (S, S), 1)
    allowed = (lag >= 0) & (seg_col[...] == seg_row[...])
    span = jnp.where(allowed, lag.astype(jnp.float32), 1e6)
    for head in range(heads):
        both = project(head, 0)
        query = rotate(both[:, :KEY]).astype(jnp.bfloat16)
        keyed = (rotate(both[:, KEY:]) * (1.0 / math.sqrt(KEY))).astype(jnp.bfloat16)
        scores = DOT_T(query, keyed)
        scores = scores * jnp.exp(span * decays[head])
        denom = jnp.sum(scores, axis=1, keepdims=True)
        value = project(head, 1)
        retained = DOT(scores.astype(jnp.bfloat16), value) / jnp.maximum(jnp.abs(denom), 1.0)
        centred = retained - jnp.mean(retained, axis=1, keepdims=True)
        spread_of = jnp.mean(centred * centred, axis=1, keepdims=True)
        grouped = centred * lax.rsqrt(spread_of + epsilon)
        gate = project(head, 2).astype(jnp.float32)
        mixed[:, head * VAL : (head + 1) * VAL] = (silu(gate) * grouped).astype(jnp.bfloat16)


def retain(place, decays, cosine, sine, seg_col, seg_row, tokens, weights):
    rows, cols = len(weights), len(tokens)
    heads = HEADS // cols
    flat, counts = flatten(tokens)
    return pl.pallas_call(
        functools.partial(retain_kernel, rows, counts, heads),
        out_shape=jax.ShapeDtypeStruct((S, heads * VAL), jnp.bfloat16),
        in_specs=[SMEM, SMEM] + [VMEM] * (4 + len(flat)) + [ANY] * rows,
        out_specs=VMEM,
        scratch_shapes=[
            pltpu.VMEM((S, D), jnp.bfloat16),
            pltpu.VMEM((D, heads * HEAD_WIDTH), jnp.bfloat16),
            pltpu.SemaphoreType.DMA((heads * 3,)),
        ],
        compiler_params=params(),
        cost_estimate=cost(2 * S * D * HEAD_WIDTH * heads * 1.3, 2 * D * HEAD_WIDTH * heads),
    )(place, decays, cosine, sine, seg_col, seg_row, *flat, *weights)


def load_terms(rows, cols, place, views, gathered, sem):
    ratio = rows // cols
    for j in range(rows):
        owner = lax.bitwise_xor(place[0], j)
        target = owner // ratio
        slot = lax.bitwise_xor(target, place[1]) * ratio + (owner - target * ratio)
        pltpu.make_async_copy(views[j], gathered.at[slot], sem).start()


def put_terms(rows, cols, left, gathered, sem, outs):
    ratio = rows // cols
    depth = D // rows
    pltpu.make_async_copy(gathered, gathered, sem).wait()
    for slot in range(rows):
        k, i = slot // ratio, slot % ratio
        outs[k][:, i * depth : (i + 1) * depth] = DOT_T(left, gathered[slot]).astype(jnp.bfloat16)


def mix_kernel(rows, cols, place, mixed, *refs):
    weights, outs = refs[:rows], refs[rows : rows + cols]
    gathered, sem = refs[rows + cols :]
    units = mixed.shape[1]
    views = [ref.at[:, pl.ds(ref.shape[1] - units, units)] for ref in weights]
    load_terms(rows, cols, place, views, gathered, sem)
    put_terms(rows, cols, mixed[...], gathered, sem, outs)


def mix(place, mixed, weights, cols):
    rows = len(weights)
    width = D // cols
    return pl.pallas_call(
        functools.partial(mix_kernel, rows, cols),
        out_shape=[jax.ShapeDtypeStruct((S, width), jnp.bfloat16)] * cols,
        in_specs=[SMEM, VMEM] + [ANY] * rows,
        out_specs=[VMEM] * cols,
        scratch_shapes=[
            pltpu.VMEM((rows, D // rows, mixed.shape[1]), jnp.bfloat16),
            pltpu.SemaphoreType.DMA,
        ],
        compiler_params=params(),
        cost_estimate=cost(2 * S * D * mixed.shape[1], 2 * D * mixed.shape[1]),
    )(place, mixed, *weights)


def feed_kernel(rows, counts, tile, place, *refs):
    cols, number = len(counts), sum(counts)
    tokens = refs[:number]
    weights = refs[number : number + rows]
    outs = refs[number + rows : number + rows + cols]
    ordered, hidden, gathered, gathered_down, sems, sem_down = refs[number + rows + cols :]
    depth = D // rows
    width = D // cols
    steps = gathered.shape[2] // tile

    for step in range(steps):
        columns = pl.ds(step * tile, tile)
        for j in range(rows):
            where = pl.ds(pl.multiple_of(lax.bitwise_xor(place[0], j) * depth, depth), depth)
            pltpu.make_async_copy(
                weights[j].at[pl.ds(1, 2), :, columns], gathered.at[:, where, columns], sems.at[step]
            ).start()
    load_terms(rows, cols, place, [ref.at[0] for ref in weights], gathered_down, sem_down)

    total = jnp.zeros((S, 1), jnp.float32)
    for k, block in enumerate(read_parts(tokens, counts)):
        values = block.astype(jnp.float32)
        total += jnp.sum(values * values, axis=1, keepdims=True)
        where = pl.ds(pl.multiple_of(lax.bitwise_xor(place[1], k) * width, width), width)
        ordered[:, where] = block
    scale = lax.rsqrt(total / D + epsilon)

    for step in range(steps):
        columns = pl.ds(step * tile, tile)
        view = gathered.at[:, :, columns]
        pltpu.make_async_copy(view, view, sems.at[step]).wait()
        gate = DOT(ordered[...], gathered[0, :, columns]) * scale
        up = DOT(ordered[...], gathered[1, :, columns]) * scale
        hidden[:, columns] = (silu(gate) * up).astype(jnp.bfloat16)
    put_terms(rows, cols, hidden[...], gathered_down, sem_down, outs)


def feed(place, tokens, weights):
    rows, cols = len(weights), len(tokens)
    units = weights[0].shape[2]
    tile = min(units, 512)
    flat, counts = flatten(tokens)
    return pl.pallas_call(
        functools.partial(feed_kernel, rows, counts, tile),
        out_shape=[jax.ShapeDtypeStruct((S, D // cols), jnp.bfloat16)] * cols,
        in_specs=[SMEM] + [VMEM] * len(flat) + [ANY] * rows,
        out_specs=[VMEM] * cols,
        scratch_shapes=[
            pltpu.VMEM((S, D), jnp.bfloat16),
            pltpu.VMEM((S, units), jnp.bfloat16),
            pltpu.VMEM((2, D, units), jnp.bfloat16),
            pltpu.VMEM((rows, D // rows, units), jnp.bfloat16),
            pltpu.SemaphoreType.DMA((units // tile,)),
            pltpu.SemaphoreType.DMA,
        ],
        compiler_params=params(),
        cost_estimate=cost(6 * S * D * units, 6 * D * units),
    )(place, *flat, *weights)


def shards(hidden_states, lengths, qkvg_master, gateup_master, out_master, down_master):
    rows, cols = lax.axis_size("row"), lax.axis_size("col")
    per_row = lengths.shape[0]
    heads = HEADS // cols
    place = jnp.stack([lax.axis_index("row"), lax.axis_index("col")]).astype(jnp.int32)

    all_lengths = gather_lengths(lengths)
    depth = qkvg_master.shape[0]
    units = gateup_master.shape[2] // cols
    width = heads * HEAD_WIDTH
    front_cut = cut(cut_front_kernel, (depth, width + units), place, qkvg_master, out_master.T)
    front_parts = exchange(front_cut)
    everyone = gather_rows(after(hidden_states, all_lengths), halves=front_parts[1:3])
    front_blocks = join(front_parts, place)

    table, bins, starts, count = pack(place, all_lengths, rows)

    head_ids = lax.axis_index("col") * heads + jnp.arange(heads)
    decays = jnp.log1p(-jnp.power(2.0, -5.0 - head_ids.astype(jnp.float32)))
    freq = jnp.power(10000.0, -2.0 * jnp.arange(KEY // 2).astype(jnp.float32) / KEY)

    def begin(turn):
        codes = table[turn * TILES : (turn + 1) * TILES]
        segments = jnp.where(codes < 0, -1, codes // TILES)
        seg = jnp.broadcast_to(segments[:, None], (TILES, TILE)).reshape(S)
        positions = ((jnp.maximum(codes, 0) % TILES)[:, None] * TILE + jnp.arange(TILE)[None, :]).reshape(S)
        angle = positions.astype(jnp.float32)[:, None] * freq[None, :]
        own = pick(place, table, everyone, turn)
        return own, (jnp.cos(angle), jnp.sin(angle), seg[:, None], seg[None, :])

    own, tables = begin(0)
    tokens = gather_cols(own)
    ahead = [tokens[1][0], tokens[2][0]]
    rest = [part for entry in tokens[3:] for part in entry]
    feed_cut = cut(cut_feed_kernel, (3, depth, units), place, down_master.T, gateup_master)
    front_pieces = gather_rows(
        after(front_blocks, *last_parts(everyone)), halves=ahead, whole=(*rest, *tables, feed_cut[0])
    )
    feed_parts = exchange(list(after(tuple(feed_cut), *rest)))

    mixed = retain(place, decays, *tables, tokens, front_pieces)
    terms = mix(place, mixed, front_pieces, cols)
    attended = collect(terms)
    feed_blocks = join(list(after(tuple(feed_parts), terms[0])), place)
    residual = own.astype(jnp.float32) + added(attended)
    feed_pieces = []

    def between(first):
        feed_pieces.extend(gather_rows(feed_blocks, halves=attended[1:], whole=first))
        return feed_pieces[1:6:2]

    mid_tokens = gather_cols(residual.astype(jnp.bfloat16), between)
    if not feed_pieces:
        feed_pieces = gather_rows(feed_blocks)

    weights = deliver(front_blocks, feed_blocks, width)

    terms = feed(place, mid_tokens, [after(feed_pieces[0], *weights)] + feed_pieces[1:])
    first = gather_rows((residual + added(collect(terms))).astype(jnp.bfloat16), direct=True)

    def again(turn, even):
        own, tables = begin(turn)
        mixed = retain(place, decays, *tables, gather_cols(own, even=even), front_pieces)
        attended = collect(mix(place, mixed, front_pieces, cols), even)
        residual = own.astype(jnp.float32) + added(attended)
        mid_tokens = gather_cols(residual.astype(jnp.bfloat16), even=even)
        fed = collect(feed(place, mid_tokens, feed_pieces), even)
        block = (residual + added(fed)).astype(jnp.bfloat16)
        return gather_even(block) if even else gather_rows(block, direct=True)

    def finish(pieces, few=False):
        return spread(place, lengths, bins, starts, pieces, rows, per_row, few)

    def more(pieces):
        for turn in range(1, per_row):
            pieces = pieces + again(turn, False)
        return finish(pieces)

    def some(pieces):
        return finish(pieces + again(per_row, True), True)

    if rows == 8 and cols == 4:
        case = (count[0] > rows).astype(jnp.int32) + (count[0] > rows + rows // 2).astype(jnp.int32)
        layer_output = lax.switch(case, [finish, some, more], first)
    else:
        layer_output = lax.cond(count[0] > rows, more, finish, first)
    return (layer_output,) + weights


def solution(mesh):
    return jax.shard_map(
        shards,
        mesh=mesh,
        in_specs=(
            P("row", "col"),
            P("row"),
            P(("row", "col"), None),
            P(None, ("row", "col"), None),
            P(None, ("row", "col")),
            P(None, ("row", "col")),
        ),
        out_specs=(
            P("row", "col"),
            P("row", "col"),
            P(None, "row", "col"),
            P("col", "row"),
            P("col", "row"),
        ),
        check_vma=False,
    )
```

```python
import functools
import math

import jax
import jax.numpy as jnp
from jax import lax
from jax.experimental import pallas as pl
from jax.experimental.pallas import tpu as pltpu
from jax.sharding import PartitionSpec as P

D = 2048
HEADS = 8
KEY = 256
VAL = 512
S = 512
TILE = 16
TILES = S // TILE
HEAD_WIDTH = 2 * KEY + 2 * VAL

epsilon = 1e-05
VMEM_LIMIT = 56 * 1024 * 1024

SMEM = pl.BlockSpec(memory_space=pltpu.SMEM)
VMEM = pl.BlockSpec(memory_space=pltpu.VMEM)
ANY = pl.BlockSpec(memory_space=pl.ANY)


def params():
    return pltpu.CompilerParams(vmem_limit_bytes=VMEM_LIMIT)


def cost(flops, moved):
    return pl.CostEstimate(flops=int(flops), bytes_accessed=int(moved), transcendentals=0)


def swap(block, axis, step):
    size = lax.axis_size(axis)
    return lax.ppermute(block, axis, [(i, i ^ step) for i in range(size)])


def along_col(block, pairs, even):
    if not even:
        return lax.ppermute(block, "col", pairs)
    rows, cols = lax.axis_size("row"), lax.axis_size("col")
    pairs = [(row * cols + a, row * cols + b) for row in range(0, rows, 2) for a, b in pairs]
    return lax.ppermute(block, ("row", "col"), pairs)


def after(value, *earlier):
    return lax.optimization_barrier((value,) + earlier)[0]


def glue_kernel(upper, lower, out):
    half = upper.shape[-2]
    out[..., :half, :] = upper[...]
    out[..., half:, :] = lower[...]


def glue(upper, lower):
    shape = list(upper.shape)
    shape[-2] *= 2
    return pl.pallas_call(
        glue_kernel,
        out_shape=jax.ShapeDtypeStruct(tuple(shape), upper.dtype),
        in_specs=[VMEM] * 2,
        out_specs=VMEM,
        compiler_params=params(),
        cost_estimate=cost(0, 4 * math.prod(shape)),
    )(upper, lower)


def gather_rows(block, direct=False, halves=(), whole=(), core=()):
    size = lax.axis_size("row")
    pieces = {0: block}
    if size == 8:
        axis = block.ndim - 2
        half = block.shape[axis] // 2
        pieces[2] = swap(block, "row", 2)
        pieces[4] = swap(block, "row", 4)
        if direct:
            pieces[6] = swap(block, "row", 6)
        else:
            across, along = after((pieces[2], pieces[4]), *halves)
            upper = swap(lax.slice_in_dim(along, 0, half, axis=axis), "row", 2)
            lower = swap(lax.slice_in_dim(across, half, 2 * half, axis=axis), "row", 4)
            pieces[6] = glue(*after((upper, lower), *whole))
        pieces[0] = after(block, pieces[2], pieces[4])
        bits = [1]
    else:
        bits = [1 << i for i in reversed(range(size.bit_length() - 1))]
    for bit in bits:
        for j in sorted(pieces):
            pieces[j | bit] = swap(after(pieces[j], *core), "row", bit)
    return [pieces[j] for j in range(size)]


def last_parts(pieces):
    return (pieces[6],) if len(pieces) == 8 else (pieces[-1],)


def gather_lengths(lengths):
    size = lax.axis_size("row")
    bit = 1
    while bit < size:
        lengths = jnp.concatenate([lengths, swap(lengths, "row", bit)])
        bit *= 2
    return lengths


def exchange(blocks):
    return [blocks[0]] + [swap(blocks[k], "col", k) for k in range(1, len(blocks))]


def gather_cols(block, between=None, even=False):
    size = lax.axis_size("col")
    if size != 4:
        return [(block,)] + [(swap(block, "col", k),) for k in range(1, size)]
    near = along_col(block, [(0, 1), (1, 0), (2, 3), (3, 2)], even)
    far = along_col(block, [(0, 2), (2, 0), (1, 3), (3, 1)], even)
    later = between((near, far)) if between else ()
    mine, passed = after((block, far), near, *later)
    middle = along_col(mine, [(1, 2), (2, 1)], even)
    ends = along_col(passed, [(2, 3), (1, 0)], even)
    return [(block,), (near,), (far,), (middle, ends)]


def collect(terms, even=False):
    if lax.axis_size("col") != 4:
        return exchange(terms)
    early = along_col(terms[3], [(3, 2), (0, 1)], even)
    middle = along_col(terms[3], [(1, 2), (2, 1)], even)
    near = along_col(after(terms[1], early), [(0, 1), (1, 0), (2, 3), (3, 2)], even)
    both = terms[2].astype(jnp.float32) + early.astype(jnp.float32)
    far = along_col(both.astype(jnp.bfloat16), [(0, 2), (2, 0), (1, 3), (3, 1)], even)
    return [terms[0], near, far, middle]


def gather_even(block):
    rows = lax.axis_size("row")
    pieces = [block]
    for j in (2, 4, 6):
        pieces.append(lax.ppermute(block, "row", [(i, i ^ j) for i in range(0, rows, 2)]))
    return pieces + [lax.ppermute(piece, "row", [(i, i + 1) for i in range(0, rows, 2)]) for piece in pieces]


def added(parts):
    return sum(part.astype(jnp.float32) for part in parts)


def cut_front_kernel(cols, place, qkvg, out, *blocks):
    units = out.shape[1] // cols
    width = blocks[0].shape[1] - units
    for k in range(cols):
        target = lax.bitwise_xor(place[1], k)
        columns = pl.ds(pl.multiple_of(target * width, 128), width)
        blocks[k][:, :width] = qkvg[:, columns].astype(jnp.bfloat16)
        columns = pl.ds(pl.multiple_of(target * units, 128), units)
        blocks[k][:, width:] = out[:, columns].astype(jnp.bfloat16)


def cut_feed_kernel(cols, place, down, gateup, *blocks):
    units = blocks[0].shape[2]
    for k in range(cols):
        target = lax.bitwise_xor(place[1], k)
        columns = pl.ds(pl.multiple_of(target * units, 128), units)
        blocks[k][0] = down[:, columns].astype(jnp.bfloat16)
        blocks[k][1] = gateup[0, :, columns].astype(jnp.bfloat16)
        blocks[k][2] = gateup[1, :, columns].astype(jnp.bfloat16)


def cut(kernel, shape, place, *masters):
    cols = lax.axis_size("col")
    return pl.pallas_call(
        functools.partial(kernel, cols),
        out_shape=[jax.ShapeDtypeStruct(shape, jnp.bfloat16)] * cols,
        in_specs=[SMEM] + [VMEM] * len(masters),
        out_specs=[VMEM] * cols,
        compiler_params=params(),
        cost_estimate=cost(0, 6 * math.prod(shape) * cols),
    )(place, *masters)


def join_kernel(cols, place, *refs):
    out = refs[cols]
    rows = refs[0].shape[-2]
    for k in range(cols):
        source = lax.bitwise_xor(place[1], k)
        where = pl.ds(pl.multiple_of(source * rows, 16), rows)
        if len(out.shape) == 2:
            out[where, :] = refs[k][...]
        else:
            out[:, where, :] = refs[k][...]


def join(blocks, place):
    cols = len(blocks)
    shape = list(blocks[0].shape)
    shape[-2] *= cols
    return pl.pallas_call(
        functools.partial(join_kernel, cols),
        out_shape=jax.ShapeDtypeStruct(tuple(shape), jnp.bfloat16),
        in_specs=[SMEM] + [VMEM] * cols,
        out_specs=VMEM,
        compiler_params=params(),
        cost_estimate=cost(0, 4 * math.prod(shape)),
    )(place, *blocks)


def deliver_kernel(front, feed, qkvg, gateup, out, down):
    width = qkvg.shape[1]
    turned = lambda values: values.astype(jnp.float32).T.astype(jnp.bfloat16)
    qkvg[...] = front[:, :width]
    gateup[...] = feed[1:]
    out[...] = turned(front[:, width:])
    down[...] = turned(feed[0])


def deliver(front, feed, width):
    depth, units = feed.shape[1:]
    shapes = [(depth, width), (2, depth, units), (units, depth), (units, depth)]
    return tuple(
        pl.pallas_call(
            deliver_kernel,
            out_shape=[jax.ShapeDtypeStruct(shape, jnp.bfloat16) for shape in shapes],
            in_specs=[VMEM] * 2,
            out_specs=[VMEM] * 4,
            compiler_params=params(),
            cost_estimate=cost(0, 4 * depth * (width + 4 * units)),
        )(front, feed)
    )


def pack_kernel(requests, rows, passes, place, lengths, table, bins, starts, count, used):
    row = place[0]
    per_row = requests // rows

    def clear(i, carry):
        table[i] = -1
        return carry

    lax.fori_loop(0, (passes + 1) * TILES, clear, 0)

    def clear_used(i, carry):
        used[i] = 0
        return carry

    lax.fori_loop(0, requests, clear_used, 0)

    def put(q, top):
        owner = q // per_row
        length = lengths[lax.bitwise_xor(owner, row) * per_row + (q - owner * per_row)]
        tiles = (length + (TILE - 1)) // TILE

        def look(i, best):
            b = requests - 1 - i
            return jnp.where(used[b] + tiles <= TILES, b, best)

        b = lax.fori_loop(0, requests, look, requests - 1)
        start = used[b]
        used[b] = start + tiles
        bins[q] = b
        starts[q] = start
        turn = b // rows

        @pl.when(b - turn * rows == row)
        def _():
            def note(i, carry):
                table[turn * TILES + start + i] = q * TILES + i
                return carry

            lax.fori_loop(0, tiles, note, 0)

        @pl.when((turn == 1) & ((b - rows) * 2 == row))
        def _():
            def note(i, carry):
                table[passes * TILES + start + i] = q * TILES + i
                return carry

            lax.fori_loop(0, tiles, note, 0)

        return jnp.maximum(top, b + 1)

    count[0] = lax.fori_loop(0, requests, put, 0)


def pack(place, lengths, rows):
    requests = lengths.shape[0]
    passes = requests // rows
    whole = lambda n: jax.ShapeDtypeStruct((n,), jnp.int32)
    return pl.pallas_call(
        functools.partial(pack_kernel, requests, rows, passes),
        out_shape=[whole((passes + 1) * TILES), whole(requests), whole(requests), whole(1)],
        in_specs=[SMEM, SMEM],
        out_specs=[SMEM] * 4,
        scratch_shapes=[pltpu.SMEM((requests,), jnp.int32)],
        compiler_params=params(),
    )(place, lengths)


def pick_kernel(rows, per_row, turn, place, table, *refs):
    pieces, out, sem = refs[:rows], refs[rows], refs[rows + 1]
    row = place[0]

    def step(i, carry):
        code = jnp.maximum(table[turn * TILES + i], 0)
        request = code // TILES
        owner = request // per_row
        tile = (request - owner * per_row) * TILES + (code - request * TILES)
        piece = lax.bitwise_xor(owner, row)
        source = pl.ds(pl.multiple_of(tile * TILE, TILE), TILE)
        target = pl.ds(pl.multiple_of(i * TILE, TILE), TILE)
        for j in range(rows):

            @pl.when(piece == j)
            def _():
                pltpu.make_async_copy(pieces[j].at[source, :], out.at[target, :], sem).start()

        return carry

    lax.fori_loop(0, TILES, step, 0)
    pltpu.make_async_copy(out, out, sem).wait()


def pick(place, table, pieces, turn):
    rows = len(pieces)
    width = pieces[0].shape[1]
    return pl.pallas_call(
        functools.partial(pick_kernel, rows, pieces[0].shape[0] // S, turn),
        out_shape=jax.ShapeDtypeStruct((S, width), jnp.bfloat16),
        in_specs=[SMEM, SMEM] + [ANY] * rows,
        out_specs=VMEM,
        scratch_shapes=[pltpu.SemaphoreType.DMA],
        compiler_params=params(),
        cost_estimate=cost(0, 4 * S * width),
    )(place, table, *pieces)


def spread_kernel(rows, per_row, total, few, place, lengths, bins, starts, *refs):
    pieces, out = refs[:total], refs[total]
    row = place[0]
    width = out.shape[1]
    for a in range(per_row):
        request = row * per_row + a
        length = lengths[a]
        b = bins[request]
        start = starts[request]
        turn = b // rows
        index = lax.bitwise_xor(b - turn * rows, row) + turn * rows
        if few:
            chip = row // 2
            other = rows + lax.bitwise_xor(b - rows, chip) + 4 * (row - 2 * chip)
            index = jnp.where(turn == 1, other, index)
        tiles = (length + (TILE - 1)) // TILE

        def blank(i, carry):
            out[pl.ds(pl.multiple_of(a * S + i * TILE, TILE), TILE), :] = jnp.zeros((TILE, width), jnp.bfloat16)
            return carry

        lax.fori_loop(tiles, TILES, blank, 0)
        for j in range(total):

            @pl.when(index == j)
            def _():
                def move(i, carry):
                    values = pieces[j][pl.ds(pl.multiple_of((start + i) * TILE, TILE), TILE), :]
                    position = i * TILE + lax.broadcasted_iota(jnp.int32, (TILE, width), 0)
                    kept = jnp.where(position < length, values.astype(jnp.float32), 0.0)
                    out[pl.ds(pl.multiple_of(a * S + i * TILE, TILE), TILE), :] = kept.astype(jnp.bfloat16)
                    return carry

                lax.fori_loop(0, tiles, move, 0)


def spread(place, lengths, bins, starts, pieces, rows, per_row, few=False):
    width = pieces[0].shape[1]
    return pl.pallas_call(
        functools.partial(spread_kernel, rows, per_row, len(pieces), few),
        out_shape=jax.ShapeDtypeStruct((per_row * S, width), jnp.bfloat16),
        in_specs=[SMEM] * 4 + [VMEM] * len(pieces),
        out_specs=VMEM,
        compiler_params=params(),
        cost_estimate=cost(0, 2 * S * width * (len(pieces) + per_row)),
    )(place, lengths, bins, starts, *pieces)


DOT = functools.partial(jnp.dot, preferred_element_type=jnp.float32)


def DOT_T(left, right):
    return lax.dot_general(left, right, (((1,), (1,)), ((), ())), preferred_element_type=jnp.float32)


def flatten(parts):
    return [part for entry in parts for part in entry], tuple(len(entry) for entry in parts)


def read_parts(refs, counts):
    at = 0
    for count in counts:
        block = refs[at][...]
        for other in refs[at + 1 : at + count]:
            block = block + other[...]
        at += count
        yield block


def silu(values):
    return values * (1.0 / (1.0 + jnp.exp(-values)))


def retain_kernel(rows, counts, heads, place, decays, cosine, sine, seg_col, seg_row, *refs):
    cols, number = len(counts), sum(counts)
    tokens, weights = refs[:number], refs[number : number + rows]
    mixed, normed, gathered, sems = refs[number + rows :]
    depth = D // rows
    width = D // cols
    parts = ((0, 2 * KEY), (2 * KEY, VAL), (2 * KEY + VAL, VAL))

    for head in range(heads):
        for i, (low, size) in enumerate(parts):
            columns = pl.ds(head * HEAD_WIDTH + low, size)
            for j in range(rows):
                where = pl.ds(pl.multiple_of(lax.bitwise_xor(place[0], j) * depth, depth), depth)
                pltpu.make_async_copy(
                    weights[j].at[:, columns], gathered.at[where, columns], sems.at[head * 3 + i]
                ).start()

    total = jnp.zeros((S, 1), jnp.float32)
    for block in read_parts(tokens, counts):
        values = block.astype(jnp.float32)
        total += jnp.sum(values * values, axis=1, keepdims=True)
    scale = lax.rsqrt(total / D + epsilon)
    for k, block in enumerate(read_parts(tokens, counts)):
        where = pl.ds(pl.multiple_of(lax.bitwise_xor(place[1], k) * width, width), width)
        normed[:, where] = (block.astype(jnp.float32) * scale).astype(jnp.bfloat16)

    def arrive(head, i):
        low, size = parts[i]
        view = gathered.at[:, pl.ds(head * HEAD_WIDTH + low, size)]
        pltpu.make_async_copy(view, view, sems.at[head * 3 + i]).wait()

    def project(head, i):
        low, size = parts[i]
        return DOT(normed[...], gathered[:, pl.ds(head * HEAD_WIDTH + low, size)]).astype(jnp.bfloat16)

    def rotate(values):
        values = values.astype(jnp.float32)
        first, second = values[:, : KEY // 2], values[:, KEY // 2 :]
        cos, sin = cosine[...], sine[...]
        return jnp.concatenate([first * cos - second * sin, first * sin + second * cos], axis=1)

    lag = lax.broadcasted_iota(jnp.int32, (S, S), 0) - lax.broadcasted_iota(jnp.int32, (S, S), 1)
    allowed = (lag >= 0) & (seg_col[...] == seg_row[...])
    span = jnp.where(allowed, lag.astype(jnp.float32), 1e6)
    for head in range(heads):
        arrive(head, 0)
        if head:
            arrive(head, 1)
            arrive(head, 2)
        both = project(head, 0)
        if not head:
            arrive(head, 1)
            arrive(head, 2)
        value = project(head, 1)
        gate = project(head, 2).astype(jnp.float32)
        query = rotate(both[:, :KEY]).astype(jnp.bfloat16)
        keyed = (rotate(both[:, KEY:]) * (1.0 / math.sqrt(KEY))).astype(jnp.bfloat16)
        scores = DOT_T(query, keyed)
        scores = scores * jnp.exp(span * decays[head])
        denom = jnp.sum(scores, axis=1, keepdims=True)
        retained = DOT(scores.astype(jnp.bfloat16), value) / jnp.maximum(jnp.abs(denom), 1.0)
        centred = retained - jnp.mean(retained, axis=1, keepdims=True)
        spread_of = jnp.mean(centred * centred, axis=1, keepdims=True)
        grouped = centred * lax.rsqrt(spread_of + epsilon)
        mixed[:, head * VAL : (head + 1) * VAL] = (silu(gate) * grouped).astype(jnp.bfloat16)


def retain(place, decays, cosine, sine, seg_col, seg_row, tokens, weights):
    rows, cols = len(weights), len(tokens)
    heads = HEADS // cols
    flat, counts = flatten(tokens)
    return pl.pallas_call(
        functools.partial(retain_kernel, rows, counts, heads),
        out_shape=jax.ShapeDtypeStruct((S, heads * VAL), jnp.bfloat16),
        in_specs=[SMEM, SMEM] + [VMEM] * (4 + len(flat)) + [ANY] * rows,
        out_specs=VMEM,
        scratch_shapes=[
            pltpu.VMEM((S, D), jnp.bfloat16),
            pltpu.VMEM((D, heads * HEAD_WIDTH), jnp.bfloat16),
            pltpu.SemaphoreType.DMA((heads * 3,)),
        ],
        compiler_params=params(),
        cost_estimate=cost(2 * S * D * HEAD_WIDTH * heads * 1.3, 2 * D * HEAD_WIDTH * heads),
    )(place, decays, cosine, sine, seg_col, seg_row, *flat, *weights)


def load_terms(rows, cols, place, views, gathered, sem):
    ratio = rows // cols
    for j in range(rows):
        owner = lax.bitwise_xor(place[0], j)
        target = owner // ratio
        slot = lax.bitwise_xor(target, place[1]) * ratio + (owner - target * ratio)
        pltpu.make_async_copy(views[j], gathered.at[slot], sem).start()


def put_terms(rows, cols, left, gathered, sem, outs):
    ratio = rows // cols
    depth = D // rows
    pltpu.make_async_copy(gathered, gathered, sem).wait()
    for slot in range(rows):
        k, i = slot // ratio, slot % ratio
        outs[k][:, i * depth : (i + 1) * depth] = DOT_T(left, gathered[slot]).astype(jnp.bfloat16)


def mix_kernel(rows, cols, place, mixed, *refs):
    weights, outs = refs[:rows], refs[rows : rows + cols]
    gathered, sem = refs[rows + cols :]
    units = mixed.shape[1]
    views = [ref.at[:, pl.ds(ref.shape[1] - units, units)] for ref in weights]
    load_terms(rows, cols, place, views, gathered, sem)
    put_terms(rows, cols, mixed[...], gathered, sem, outs)


def mix(place, mixed, weights, cols):
    rows = len(weights)
    width = D // cols
    return pl.pallas_call(
        functools.partial(mix_kernel, rows, cols),
        out_shape=[jax.ShapeDtypeStruct((S, width), jnp.bfloat16)] * cols,
        in_specs=[SMEM, VMEM] + [ANY] * rows,
        out_specs=[VMEM] * cols,
        scratch_shapes=[
            pltpu.VMEM((rows, D // rows, mixed.shape[1]), jnp.bfloat16),
            pltpu.SemaphoreType.DMA,
        ],
        compiler_params=params(),
        cost_estimate=cost(2 * S * D * mixed.shape[1], 2 * D * mixed.shape[1]),
    )(place, mixed, *weights)


def feed_kernel(rows, counts, tile, place, *refs):
    cols, number = len(counts), sum(counts)
    tokens = refs[:number]
    weights = refs[number : number + rows]
    outs = refs[number + rows : number + rows + cols]
    ordered, hidden, gathered, gathered_down, sems, sem_down = refs[number + rows + cols :]
    depth = D // rows
    width = D // cols
    steps = gathered.shape[2] // tile

    for step in range(steps):
        columns = pl.ds(step * tile, tile)
        for j in range(rows):
            where = pl.ds(pl.multiple_of(lax.bitwise_xor(place[0], j) * depth, depth), depth)
            pltpu.make_async_copy(
                weights[j].at[pl.ds(1, 2), :, columns], gathered.at[:, where, columns], sems.at[step]
            ).start()
    load_terms(rows, cols, place, [ref.at[0] for ref in weights], gathered_down, sem_down)

    total = jnp.zeros((S, 1), jnp.float32)
    for k, block in enumerate(read_parts(tokens, counts)):
        values = block.astype(jnp.float32)
        total += jnp.sum(values * values, axis=1, keepdims=True)
        where = pl.ds(pl.multiple_of(lax.bitwise_xor(place[1], k) * width, width), width)
        ordered[:, where] = block
    scale = lax.rsqrt(total / D + epsilon)

    for step in range(steps):
        columns = pl.ds(step * tile, tile)
        view = gathered.at[:, :, columns]
        pltpu.make_async_copy(view, view, sems.at[step]).wait()
        gate = DOT(ordered[...], gathered[0, :, columns]) * scale
        up = DOT(ordered[...], gathered[1, :, columns]) * scale
        hidden[:, columns] = (silu(gate) * up).astype(jnp.bfloat16)
    put_terms(rows, cols, hidden[...], gathered_down, sem_down, outs)


def feed(place, tokens, weights):
    rows, cols = len(weights), len(tokens)
    units = weights[0].shape[2]
    tile = min(units, 512)
    flat, counts = flatten(tokens)
    return pl.pallas_call(
        functools.partial(feed_kernel, rows, counts, tile),
        out_shape=[jax.ShapeDtypeStruct((S, D // cols), jnp.bfloat16)] * cols,
        in_specs=[SMEM] + [VMEM] * len(flat) + [ANY] * rows,
        out_specs=[VMEM] * cols,
        scratch_shapes=[
            pltpu.VMEM((S, D), jnp.bfloat16),
            pltpu.VMEM((S, units), jnp.bfloat16),
            pltpu.VMEM((2, D, units), jnp.bfloat16),
            pltpu.VMEM((rows, D // rows, units), jnp.bfloat16),
            pltpu.SemaphoreType.DMA((units // tile,)),
            pltpu.SemaphoreType.DMA,
        ],
        compiler_params=params(),
        cost_estimate=cost(6 * S * D * units, 6 * D * units),
    )(place, *flat, *weights)


def shards(hidden_states, lengths, qkvg_master, gateup_master, out_master, down_master):
    rows, cols = lax.axis_size("row"), lax.axis_size("col")
    per_row = lengths.shape[0]
    heads = HEADS // cols
    place = jnp.stack([lax.axis_index("row"), lax.axis_index("col")]).astype(jnp.int32)

    all_lengths = gather_lengths(lengths)
    depth = qkvg_master.shape[0]
    units = gateup_master.shape[2] // cols
    width = heads * HEAD_WIDTH
    front_cut = cut(cut_front_kernel, (depth, width + units), place, qkvg_master, out_master.T)
    front_parts = exchange(front_cut)
    everyone = gather_rows(after(hidden_states, all_lengths), halves=front_parts[1:3])
    front_blocks = join(front_parts, place)

    table, bins, starts, count = pack(place, all_lengths, rows)

    head_ids = lax.axis_index("col") * heads + jnp.arange(heads)
    decays = jnp.log1p(-jnp.power(2.0, -5.0 - head_ids.astype(jnp.float32)))
    freq = jnp.power(10000.0, -2.0 * jnp.arange(KEY // 2).astype(jnp.float32) / KEY)

    def begin(turn):
        codes = table[turn * TILES : (turn + 1) * TILES]
        segments = jnp.where(codes < 0, -1, codes // TILES)
        seg = jnp.broadcast_to(segments[:, None], (TILES, TILE)).reshape(S)
        positions = ((jnp.maximum(codes, 0) % TILES)[:, None] * TILE + jnp.arange(TILE)[None, :]).reshape(S)
        angle = positions.astype(jnp.float32)[:, None] * freq[None, :]
        own = pick(place, table, everyone, turn)
        return own, (jnp.cos(angle), jnp.sin(angle), seg[:, None], seg[None, :])

    own, tables = begin(0)
    tokens = gather_cols(own)
    ahead = [tokens[1][0], tokens[2][0]]
    rest = [part for entry in tokens[3:] for part in entry]
    feed_cut = cut(cut_feed_kernel, (3, depth, units), place, down_master.T, gateup_master)
    front_pieces = gather_rows(
        after(front_blocks, *last_parts(everyone)), halves=ahead, whole=(*rest, *tables, feed_cut[0])
    )
    feed_parts = exchange(list(after(tuple(feed_cut), *rest)))

    mixed = retain(place, decays, *tables, tokens, front_pieces)
    terms = mix(place, mixed, front_pieces, cols)
    attended = collect(terms)
    feed_blocks = join(list(after(tuple(feed_parts), terms[0])), place)
    residual = own.astype(jnp.float32) + added(attended)
    feed_pieces = []

    def between(first):
        feed_pieces.extend(gather_rows(feed_blocks, halves=attended[1:], whole=first))
        return feed_pieces[1:6:2]

    mid_tokens = gather_cols(residual.astype(jnp.bfloat16), between)
    if not feed_pieces:
        feed_pieces = gather_rows(feed_blocks)

    weights = deliver(front_blocks, feed_blocks, width)

    terms = feed(place, mid_tokens, [after(feed_pieces[0], *weights)] + feed_pieces[1:])
    first = gather_rows((residual + added(collect(terms))).astype(jnp.bfloat16), direct=True)

    def again(turn, even):
        own, tables = begin(turn)
        mixed = retain(place, decays, *tables, gather_cols(own, even=even), front_pieces)
        attended = collect(mix(place, mixed, front_pieces, cols), even)
        residual = own.astype(jnp.float32) + added(attended)
        mid_tokens = gather_cols(residual.astype(jnp.bfloat16), even=even)
        fed = collect(feed(place, mid_tokens, feed_pieces), even)
        block = (residual + added(fed)).astype(jnp.bfloat16)
        return gather_even(block) if even else gather_rows(block, direct=True)

    def finish(pieces, few=False):
        return spread(place, lengths, bins, starts, pieces, rows, per_row, few)

    def more(pieces):
        for turn in range(1, per_row):
            pieces = pieces + again(turn, False)
        return finish(pieces)

    def some(pieces):
        return finish(pieces + again(per_row, True), True)

    if rows == 8 and cols == 4:
        case = (count[0] > rows).astype(jnp.int32) + (count[0] > rows + rows // 2).astype(jnp.int32)
        layer_output = lax.switch(case, [finish, some, more], first)
    else:
        layer_output = lax.cond(count[0] > rows, more, finish, first)
    return (layer_output,) + weights


def solution(mesh):
    return jax.shard_map(
        shards,
        mesh=mesh,
        in_specs=(
            P("row", "col"),
            P("row"),
            P(("row", "col"), None),
            P(None, ("row", "col"), None),
            P(None, ("row", "col")),
            P(None, ("row", "col")),
        ),
        out_specs=(
            P("row", "col"),
            P("row", "col"),
            P(None, "row", "col"),
            P("col", "row"),
            P("col", "row"),
        ),
        check_vma=False,
    )
```

```python
import functools
import math

import jax
import jax.numpy as jnp
from jax import lax
from jax.experimental import pallas as pl
from jax.experimental.pallas import tpu as pltpu
from jax.sharding import PartitionSpec as P

D = 2048
HEADS = 8
KEY = 256
VAL = 512
S = 512
TILE = 16
TILES = S // TILE
HEAD_WIDTH = 2 * KEY + 2 * VAL

epsilon = 1e-05
VMEM_LIMIT = 56 * 1024 * 1024

SMEM = pl.BlockSpec(memory_space=pltpu.SMEM)
VMEM = pl.BlockSpec(memory_space=pltpu.VMEM)
ANY = pl.BlockSpec(memory_space=pl.ANY)


def params():
    return pltpu.CompilerParams(vmem_limit_bytes=VMEM_LIMIT)


def cost(flops, moved):
    return pl.CostEstimate(flops=int(flops), bytes_accessed=int(moved), transcendentals=0)


def swap(block, axis, step):
    size = lax.axis_size(axis)
    return lax.ppermute(block, axis, [(i, i ^ step) for i in range(size)])


def along_col(block, pairs, even):
    if not even:
        return lax.ppermute(block, "col", pairs)
    rows, cols = lax.axis_size("row"), lax.axis_size("col")
    pairs = [(row * cols + a, row * cols + b) for row in range(0, rows, 2) for a, b in pairs]
    return lax.ppermute(block, ("row", "col"), pairs)


def after(value, *earlier):
    return lax.optimization_barrier((value,) + earlier)[0]


def glue_kernel(upper, lower, out):
    half = upper.shape[-2]
    out[..., :half, :] = upper[...]
    out[..., half:, :] = lower[...]


def glue(upper, lower):
    shape = list(upper.shape)
    shape[-2] *= 2
    return pl.pallas_call(
        glue_kernel,
        out_shape=jax.ShapeDtypeStruct(tuple(shape), upper.dtype),
        in_specs=[VMEM] * 2,
        out_specs=VMEM,
        compiler_params=params(),
        cost_estimate=cost(0, 4 * math.prod(shape)),
    )(upper, lower)


def gather_rows(block, direct=False, halves=(), whole=(), core=()):
    size = lax.axis_size("row")
    pieces = {0: block}
    if size == 8:
        axis = block.ndim - 2
        half = block.shape[axis] // 2
        pieces[2] = swap(block, "row", 2)
        pieces[4] = swap(block, "row", 4)
        if direct:
            pieces[6] = swap(block, "row", 6)
        else:
            across, along = after((pieces[2], pieces[4]), *halves)
            upper = swap(lax.slice_in_dim(along, 0, half, axis=axis), "row", 2)
            lower = swap(lax.slice_in_dim(across, half, 2 * half, axis=axis), "row", 4)
            pieces[6] = glue(*after((upper, lower), *whole))
        pieces[0] = after(block, pieces[2], pieces[4])
        bits = [1]
    else:
        bits = [1 << i for i in reversed(range(size.bit_length() - 1))]
    for bit in bits:
        for j in sorted(pieces):
            pieces[j | bit] = swap(after(pieces[j], *core), "row", bit)
    return [pieces[j] for j in range(size)]


def last_parts(pieces):
    return (pieces[6],) if len(pieces) == 8 else (pieces[-1],)


def gather_lengths(lengths):
    size = lax.axis_size("row")
    bit = 1
    while bit < size:
        lengths = jnp.concatenate([lengths, swap(lengths, "row", bit)])
        bit *= 2
    return lengths


def exchange(blocks):
    return [blocks[0]] + [swap(blocks[k], "col", k) for k in range(1, len(blocks))]


def gather_cols(block, between=None, even=False):
    size = lax.axis_size("col")
    if size != 4:
        return [(block,)] + [(swap(block, "col", k),) for k in range(1, size)]
    near = along_col(block, [(0, 1), (1, 0), (2, 3), (3, 2)], even)
    far = along_col(block, [(0, 2), (2, 0), (1, 3), (3, 1)], even)
    later = between((near, far)) if between else ()
    mine, passed = after((block, far), near, *later)
    middle = along_col(mine, [(1, 2), (2, 1)], even)
    ends = along_col(passed, [(2, 3), (1, 0)], even)
    return [(block,), (near,), (far,), (middle, ends)]


def collect(terms, even=False):
    if lax.axis_size("col") != 4:
        return exchange(terms)
    early = along_col(terms[3], [(3, 2), (0, 1)], even)
    middle = along_col(terms[3], [(1, 2), (2, 1)], even)
    near = along_col(after(terms[1], early), [(0, 1), (1, 0), (2, 3), (3, 2)], even)
    both = terms[2].astype(jnp.float32) + early.astype(jnp.float32)
    far = along_col(both.astype(jnp.bfloat16), [(0, 2), (2, 0), (1, 3), (3, 1)], even)
    return [terms[0], near, far, middle]


def gather_even(block):
    rows = lax.axis_size("row")
    pieces = [block]
    for j in (2, 4, 6):
        pieces.append(lax.ppermute(block, "row", [(i, i ^ j) for i in range(0, rows, 2)]))
    return pieces + [lax.ppermute(piece, "row", [(i, i + 1) for i in range(0, rows, 2)]) for piece in pieces]


def added(parts):
    return sum(part.astype(jnp.float32) for part in parts)


def cut_front_kernel(cols, place, qkvg, out, *blocks):
    units = out.shape[1] // cols
    width = blocks[0].shape[1] - units
    for k in range(cols):
        target = lax.bitwise_xor(place[1], k)
        columns = pl.ds(pl.multiple_of(target * width, 128), width)
        blocks[k][:, :width] = qkvg[:, columns].astype(jnp.bfloat16)
        columns = pl.ds(pl.multiple_of(target * units, 128), units)
        blocks[k][:, width:] = out[:, columns].astype(jnp.bfloat16)


def cut_feed_kernel(cols, place, down, gateup, *blocks):
    units = blocks[0].shape[2]
    for k in range(cols):
        target = lax.bitwise_xor(place[1], k)
        columns = pl.ds(pl.multiple_of(target * units, 128), units)
        blocks[k][0] = down[:, columns].astype(jnp.bfloat16)
        blocks[k][1] = gateup[0, :, columns].astype(jnp.bfloat16)
        blocks[k][2] = gateup[1, :, columns].astype(jnp.bfloat16)


def cut(kernel, shape, place, *masters):
    cols = lax.axis_size("col")
    return pl.pallas_call(
        functools.partial(kernel, cols),
        out_shape=[jax.ShapeDtypeStruct(shape, jnp.bfloat16)] * cols,
        in_specs=[SMEM] + [VMEM] * len(masters),
        out_specs=[VMEM] * cols,
        compiler_params=params(),
        cost_estimate=cost(0, 6 * math.prod(shape) * cols),
    )(place, *masters)


def join_kernel(cols, place, *refs):
    out = refs[cols]
    rows = refs[0].shape[-2]
    for k in range(cols):
        source = lax.bitwise_xor(place[1], k)
        where = pl.ds(pl.multiple_of(source * rows, 16), rows)
        if len(out.shape) == 2:
            out[where, :] = refs[k][...]
        else:
            out[:, where, :] = refs[k][...]


def join(blocks, place):
    cols = len(blocks)
    shape = list(blocks[0].shape)
    shape[-2] *= cols
    return pl.pallas_call(
        functools.partial(join_kernel, cols),
        out_shape=jax.ShapeDtypeStruct(tuple(shape), jnp.bfloat16),
        in_specs=[SMEM] + [VMEM] * cols,
        out_specs=VMEM,
        compiler_params=params(),
        cost_estimate=cost(0, 4 * math.prod(shape)),
    )(place, *blocks)


def deliver_kernel(front, feed, qkvg, gateup, out, down):
    width = qkvg.shape[1]
    turned = lambda values: values.astype(jnp.float32).T.astype(jnp.bfloat16)
    qkvg[...] = front[:, :width]
    gateup[...] = feed[1:]
    out[...] = turned(front[:, width:])
    down[...] = turned(feed[0])


def deliver(front, feed, width):
    depth, units = feed.shape[1:]
    shapes = [(depth, width), (2, depth, units), (units, depth), (units, depth)]
    return tuple(
        pl.pallas_call(
            deliver_kernel,
            out_shape=[jax.ShapeDtypeStruct(shape, jnp.bfloat16) for shape in shapes],
            in_specs=[VMEM] * 2,
            out_specs=[VMEM] * 4,
            compiler_params=params(),
            cost_estimate=cost(0, 4 * depth * (width + 4 * units)),
        )(front, feed)
    )


def pack_kernel(requests, rows, passes, place, lengths, table, bins, starts, count, used):
    row = place[0]
    per_row = requests // rows

    def clear(i, carry):
        table[i] = -1
        return carry

    lax.fori_loop(0, (passes + 1) * TILES, clear, 0)

    def clear_used(i, carry):
        used[i] = 0
        return carry

    lax.fori_loop(0, requests, clear_used, 0)

    def put(q, top):
        owner = q // per_row
        length = lengths[lax.bitwise_xor(owner, row) * per_row + (q - owner * per_row)]
        tiles = (length + (TILE - 1)) // TILE

        def look(i, best):
            b = requests - 1 - i
            return jnp.where(used[b] + tiles <= TILES, b, best)

        b = lax.fori_loop(0, requests, look, requests - 1)
        start = used[b]
        used[b] = start + tiles
        bins[q] = b
        starts[q] = start
        turn = b // rows

        @pl.when(b - turn * rows == row)
        def _():
            def note(i, carry):
                table[turn * TILES + start + i] = q * TILES + i
                return carry

            lax.fori_loop(0, tiles, note, 0)

        @pl.when((turn == 1) & ((b - rows) * 2 == row))
        def _():
            def note(i, carry):
                table[passes * TILES + start + i] = q * TILES + i
                return carry

            lax.fori_loop(0, tiles, note, 0)

        return jnp.maximum(top, b + 1)

    count[0] = lax.fori_loop(0, requests, put, 0)


def pack(place, lengths, rows):
    requests = lengths.shape[0]
    passes = requests // rows
    whole = lambda n: jax.ShapeDtypeStruct((n,), jnp.int32)
    return pl.pallas_call(
        functools.partial(pack_kernel, requests, rows, passes),
        out_shape=[whole((passes + 1) * TILES), whole(requests), whole(requests), whole(1)],
        in_specs=[SMEM, SMEM],
        out_specs=[SMEM] * 4,
        scratch_shapes=[pltpu.SMEM((requests,), jnp.int32)],
        compiler_params=params(),
    )(place, lengths)


def pick_kernel(rows, per_row, turn, place, table, *refs):
    pieces, out, sem = refs[:rows], refs[rows], refs[rows + 1]
    row = place[0]

    def step(i, carry):
        code = jnp.maximum(table[turn * TILES + i], 0)
        request = code // TILES
        owner = request // per_row
        tile = (request - owner * per_row) * TILES + (code - request * TILES)
        piece = lax.bitwise_xor(owner, row)
        source = pl.ds(pl.multiple_of(tile * TILE, TILE), TILE)
        target = pl.ds(pl.multiple_of(i * TILE, TILE), TILE)
        for j in range(rows):

            @pl.when(piece == j)
            def _():
                pltpu.make_async_copy(pieces[j].at[source, :], out.at[target, :], sem).start()

        return carry

    lax.fori_loop(0, TILES, step, 0)
    pltpu.make_async_copy(out, out, sem).wait()


def pick(place, table, pieces, turn):
    rows = len(pieces)
    width = pieces[0].shape[1]
    return pl.pallas_call(
        functools.partial(pick_kernel, rows, pieces[0].shape[0] // S, turn),
        out_shape=jax.ShapeDtypeStruct((S, width), jnp.bfloat16),
        in_specs=[SMEM, SMEM] + [ANY] * rows,
        out_specs=VMEM,
        scratch_shapes=[pltpu.SemaphoreType.DMA],
        compiler_params=params(),
        cost_estimate=cost(0, 4 * S * width),
    )(place, table, *pieces)


def spread_kernel(rows, per_row, total, few, place, lengths, bins, starts, *refs):
    pieces, out = refs[:total], refs[total]
    row = place[0]
    width = out.shape[1]
    for a in range(per_row):
        request = row * per_row + a
        length = lengths[a]
        b = bins[request]
        start = starts[request]
        turn = b // rows
        index = lax.bitwise_xor(b - turn * rows, row) + turn * rows
        if few:
            chip = row // 2
            other = rows + lax.bitwise_xor(b - rows, chip) + 4 * (row - 2 * chip)
            index = jnp.where(turn == 1, other, index)
        tiles = (length + (TILE - 1)) // TILE

        def blank(i, carry):
            out[pl.ds(pl.multiple_of(a * S + i * TILE, TILE), TILE), :] = jnp.zeros((TILE, width), jnp.bfloat16)
            return carry

        lax.fori_loop(tiles, TILES, blank, 0)
        for j in range(total):

            @pl.when(index == j)
            def _():
                def move(i, carry):
                    values = pieces[j][pl.ds(pl.multiple_of((start + i) * TILE, TILE), TILE), :]
                    position = i * TILE + lax.broadcasted_iota(jnp.int32, (TILE, width), 0)
                    kept = jnp.where(position < length, values.astype(jnp.float32), 0.0)
                    out[pl.ds(pl.multiple_of(a * S + i * TILE, TILE), TILE), :] = kept.astype(jnp.bfloat16)
                    return carry

                lax.fori_loop(0, tiles, move, 0)


def spread(place, lengths, bins, starts, pieces, rows, per_row, few=False):
    width = pieces[0].shape[1]
    return pl.pallas_call(
        functools.partial(spread_kernel, rows, per_row, len(pieces), few),
        out_shape=jax.ShapeDtypeStruct((per_row * S, width), jnp.bfloat16),
        in_specs=[SMEM] * 4 + [VMEM] * len(pieces),
        out_specs=VMEM,
        compiler_params=params(),
        cost_estimate=cost(0, 2 * S * width * (len(pieces) + per_row)),
    )(place, lengths, bins, starts, *pieces)


DOT = functools.partial(jnp.dot, preferred_element_type=jnp.float32)


def DOT_T(left, right):
    return lax.dot_general(left, right, (((1,), (1,)), ((), ())), preferred_element_type=jnp.float32)


def flatten(parts):
    return [part for entry in parts for part in entry], tuple(len(entry) for entry in parts)


def read_parts(refs, counts):
    at = 0
    for count in counts:
        block = refs[at][...]
        for other in refs[at + 1 : at + count]:
            block = block + other[...]
        at += count
        yield block


def silu(values):
    return values * (1.0 / (1.0 + jnp.exp(-values)))


def retain_kernel(rows, counts, heads, place, decays, cosine, sine, seg_col, seg_row, *refs):
    cols, number = len(counts), sum(counts)
    tokens, weights = refs[:number], refs[number : number + rows]
    mixed, normed, gathered, sems = refs[number + rows :]
    depth = D // rows
    width = D // cols
    parts = ((0, 2 * KEY), (2 * KEY, VAL), (2 * KEY + VAL, VAL))

    for head in range(heads):
        for i, (low, size) in enumerate(parts):
            columns = pl.ds(head * HEAD_WIDTH + low, size)
            for j in range(rows):
                where = pl.ds(pl.multiple_of(lax.bitwise_xor(place[0], j) * depth, depth), depth)
                pltpu.make_async_copy(
                    weights[j].at[:, columns], gathered.at[where, columns], sems.at[head * 3 + i]
                ).start()

    total = jnp.zeros((S, 1), jnp.float32)
    for block in read_parts(tokens, counts):
        values = block.astype(jnp.float32)
        total += jnp.sum(values * values, axis=1, keepdims=True)
    scale = lax.rsqrt(total / D + epsilon)
    for k, block in enumerate(read_parts(tokens, counts)):
        where = pl.ds(pl.multiple_of(lax.bitwise_xor(place[1], k) * width, width), width)
        normed[:, where] = (block.astype(jnp.float32) * scale).astype(jnp.bfloat16)

    def arrive(head, i):
        low, size = parts[i]
        view = gathered.at[:, pl.ds(head * HEAD_WIDTH + low, size)]
        pltpu.make_async_copy(view, view, sems.at[head * 3 + i]).wait()

    def project(head, i):
        low, size = parts[i]
        return DOT(normed[...], gathered[:, pl.ds(head * HEAD_WIDTH + low, size)]).astype(jnp.bfloat16)

    def rotate(values):
        values = values.astype(jnp.float32)
        first, second = values[:, : KEY // 2], values[:, KEY // 2 :]
        cos, sin = cosine[...], sine[...]
        return jnp.concatenate([first * cos - second * sin, first * sin + second * cos], axis=1)

    lag = lax.broadcasted_iota(jnp.int32, (S, S), 0) - lax.broadcasted_iota(jnp.int32, (S, S), 1)
    allowed = (lag >= 0) & (seg_col[...] == seg_row[...])
    span = jnp.where(allowed, lag.astype(jnp.float32), 1e6)
    for head in range(heads):
        arrive(head, 0)
        if head:
            arrive(head, 1)
            arrive(head, 2)
        both = project(head, 0)
        if not head:
            arrive(head, 1)
            arrive(head, 2)
        value = project(head, 1)
        gate = project(head, 2).astype(jnp.float32)
        query = rotate(both[:, :KEY]).astype(jnp.bfloat16)
        keyed = (rotate(both[:, KEY:]) * (1.0 / math.sqrt(KEY))).astype(jnp.bfloat16)
        scores = DOT_T(query, keyed)
        scores = scores * jnp.exp(span * decays[head])
        denom = jnp.sum(scores, axis=1, keepdims=True)
        retained = DOT(scores.astype(jnp.bfloat16), value) / jnp.maximum(jnp.abs(denom), 1.0)
        centred = retained - jnp.mean(retained, axis=1, keepdims=True)
        spread_of = jnp.mean(centred * centred, axis=1, keepdims=True)
        grouped = centred * lax.rsqrt(spread_of + epsilon)
        mixed[:, head * VAL : (head + 1) * VAL] = (silu(gate) * grouped).astype(jnp.bfloat16)


def retain(place, decays, cosine, sine, seg_col, seg_row, tokens, weights):
    rows, cols = len(weights), len(tokens)
    heads = HEADS // cols
    flat, counts = flatten(tokens)
    return pl.pallas_call(
        functools.partial(retain_kernel, rows, counts, heads),
        out_shape=jax.ShapeDtypeStruct((S, heads * VAL), jnp.bfloat16),
        in_specs=[SMEM, SMEM] + [VMEM] * (4 + len(flat)) + [ANY] * rows,
        out_specs=VMEM,
        scratch_shapes=[
            pltpu.VMEM((S, D), jnp.bfloat16),
            pltpu.VMEM((D, heads * HEAD_WIDTH), jnp.bfloat16),
            pltpu.SemaphoreType.DMA((heads * 3,)),
        ],
        compiler_params=params(),
        cost_estimate=cost(2 * S * D * HEAD_WIDTH * heads * 1.3, 2 * D * HEAD_WIDTH * heads),
    )(place, decays, cosine, sine, seg_col, seg_row, *flat, *weights)


def load_terms(rows, cols, place, views, gathered, sem):
    ratio = rows // cols
    for j in range(rows):
        owner = lax.bitwise_xor(place[0], j)
        target = owner // ratio
        slot = lax.bitwise_xor(target, place[1]) * ratio + (owner - target * ratio)
        pltpu.make_async_copy(views[j], gathered.at[slot], sem).start()


def put_terms(rows, cols, left, gathered, sem, outs):
    ratio = rows // cols
    depth = D // rows
    pltpu.make_async_copy(gathered, gathered, sem).wait()
    for slot in range(rows):
        k, i = slot // ratio, slot % ratio
        outs[k][:, i * depth : (i + 1) * depth] = DOT_T(left, gathered[slot]).astype(jnp.bfloat16)


def mix_kernel(rows, cols, place, mixed, *refs):
    weights, outs = refs[:rows], refs[rows : rows + cols]
    gathered, sem = refs[rows + cols :]
    units = mixed.shape[1]
    views = [ref.at[:, pl.ds(ref.shape[1] - units, units)] for ref in weights]
    load_terms(rows, cols, place, views, gathered, sem)
    put_terms(rows, cols, mixed[...], gathered, sem, outs)


def mix(place, mixed, weights, cols):
    rows = len(weights)
    width = D // cols
    return pl.pallas_call(
        functools.partial(mix_kernel, rows, cols),
        out_shape=[jax.ShapeDtypeStruct((S, width), jnp.bfloat16)] * cols,
        in_specs=[SMEM, VMEM] + [ANY] * rows,
        out_specs=[VMEM] * cols,
        scratch_shapes=[
            pltpu.VMEM((rows, D // rows, mixed.shape[1]), jnp.bfloat16),
            pltpu.SemaphoreType.DMA,
        ],
        compiler_params=params(),
        cost_estimate=cost(2 * S * D * mixed.shape[1], 2 * D * mixed.shape[1]),
    )(place, mixed, *weights)


def feed_kernel(rows, counts, tile, place, *refs):
    cols, number = len(counts), sum(counts)
    tokens = refs[:number]
    weights = refs[number : number + rows]
    outs = refs[number + rows : number + rows + cols]
    ordered, hidden, gathered, gathered_down, sems, sem_down = refs[number + rows + cols :]
    depth = D // rows
    width = D // cols
    steps = gathered.shape[2] // tile

    for step in range(steps):
        columns = pl.ds(step * tile, tile)
        for j in range(rows):
            where = pl.ds(pl.multiple_of(lax.bitwise_xor(place[0], j) * depth, depth), depth)
            pltpu.make_async_copy(
                weights[j].at[pl.ds(1, 2), :, columns], gathered.at[:, where, columns], sems.at[step]
            ).start()
    load_terms(rows, cols, place, [ref.at[0] for ref in weights], gathered_down, sem_down)

    total = jnp.zeros((S, 1), jnp.float32)
    for k, block in enumerate(read_parts(tokens, counts)):
        values = block.astype(jnp.float32)
        total += jnp.sum(values * values, axis=1, keepdims=True)
        where = pl.ds(pl.multiple_of(lax.bitwise_xor(place[1], k) * width, width), width)
        ordered[:, where] = block
    scale = lax.rsqrt(total / D + epsilon)

    for step in range(steps):
        columns = pl.ds(step * tile, tile)
        view = gathered.at[:, :, columns]
        pltpu.make_async_copy(view, view, sems.at[step]).wait()
        gate = DOT(ordered[...], gathered[0, :, columns]) * scale
        up = DOT(ordered[...], gathered[1, :, columns]) * scale
        hidden[:, columns] = (silu(gate) * up).astype(jnp.bfloat16)
    put_terms(rows, cols, hidden[...], gathered_down, sem_down, outs)


def feed(place, tokens, weights):
    rows, cols = len(weights), len(tokens)
    units = weights[0].shape[2]
    tile = min(units, 512)
    flat, counts = flatten(tokens)
    return pl.pallas_call(
        functools.partial(feed_kernel, rows, counts, tile),
        out_shape=[jax.ShapeDtypeStruct((S, D // cols), jnp.bfloat16)] * cols,
        in_specs=[SMEM] + [VMEM] * len(flat) + [ANY] * rows,
        out_specs=[VMEM] * cols,
        scratch_shapes=[
            pltpu.VMEM((S, D), jnp.bfloat16),
            pltpu.VMEM((S, units), jnp.bfloat16),
            pltpu.VMEM((2, D, units), jnp.bfloat16),
            pltpu.VMEM((rows, D // rows, units), jnp.bfloat16),
            pltpu.SemaphoreType.DMA((units // tile,)),
            pltpu.SemaphoreType.DMA,
        ],
        compiler_params=params(),
        cost_estimate=cost(6 * S * D * units, 6 * D * units),
    )(place, *flat, *weights)


def shards(hidden_states, lengths, qkvg_master, gateup_master, out_master, down_master):
    rows, cols = lax.axis_size("row"), lax.axis_size("col")
    per_row = lengths.shape[0]
    heads = HEADS // cols
    place = jnp.stack([lax.axis_index("row"), lax.axis_index("col")]).astype(jnp.int32)

    depth = qkvg_master.shape[0]
    units = gateup_master.shape[2] // cols
    width = heads * HEAD_WIDTH
    front_cut = cut(cut_front_kernel, (depth, width + units), place, qkvg_master, out_master.T)
    front_parts = exchange(front_cut)
    all_lengths = gather_lengths(after(lengths, front_cut[0]))
    everyone = gather_rows(after(hidden_states, front_cut[0]), halves=(*front_parts[1:3], all_lengths))
    front_blocks = join(front_parts, place)

    table, bins, starts, count = pack(place, all_lengths, rows)

    head_ids = lax.axis_index("col") * heads + jnp.arange(heads)
    decays = jnp.log1p(-jnp.power(2.0, -5.0 - head_ids.astype(jnp.float32)))
    freq = jnp.power(10000.0, -2.0 * jnp.arange(KEY // 2).astype(jnp.float32) / KEY)

    def begin(turn):
        codes = table[turn * TILES : (turn + 1) * TILES]
        segments = jnp.where(codes < 0, -1, codes // TILES)
        seg = jnp.broadcast_to(segments[:, None], (TILES, TILE)).reshape(S)
        positions = ((jnp.maximum(codes, 0) % TILES)[:, None] * TILE + jnp.arange(TILE)[None, :]).reshape(S)
        angle = positions.astype(jnp.float32)[:, None] * freq[None, :]
        own = pick(place, table, everyone, turn)
        return own, (jnp.cos(angle), jnp.sin(angle), seg[:, None], seg[None, :])

    own, tables = begin(0)
    tokens = gather_cols(own)
    ahead = [tokens[1][0], tokens[2][0]]
    rest = [part for entry in tokens[3:] for part in entry]
    feed_cut = cut(cut_feed_kernel, (3, depth, units), place, down_master.T, gateup_master)
    front_pieces = gather_rows(
        after(front_blocks, *last_parts(everyone)), halves=ahead, whole=(*rest, *tables, feed_cut[0])
    )
    feed_parts = exchange(list(after(tuple(feed_cut), *rest)))

    mixed = retain(place, decays, *tables, tokens, front_pieces)
    terms = mix(place, mixed, front_pieces, cols)
    attended = collect(terms)
    feed_blocks = join(list(after(tuple(feed_parts), terms[0])), place)
    residual = own.astype(jnp.float32) + added(attended)
    feed_pieces = []

    def between(first):
        feed_pieces.extend(gather_rows(feed_blocks, halves=attended[1:], whole=first))
        return feed_pieces[1:6:2]

    mid_tokens = gather_cols(residual.astype(jnp.bfloat16), between)
    if not feed_pieces:
        feed_pieces = gather_rows(feed_blocks)

    weights = deliver(front_blocks, feed_blocks, width)

    terms = feed(place, mid_tokens, [after(feed_pieces[0], *weights)] + feed_pieces[1:])
    first = gather_rows((residual + added(collect(terms))).astype(jnp.bfloat16), direct=True)

    def again(turn, even):
        own, tables = begin(turn)
        mixed = retain(place, decays, *tables, gather_cols(own, even=even), front_pieces)
        attended = collect(mix(place, mixed, front_pieces, cols), even)
        residual = own.astype(jnp.float32) + added(attended)
        mid_tokens = gather_cols(residual.astype(jnp.bfloat16), even=even)
        fed = collect(feed(place, mid_tokens, feed_pieces), even)
        block = (residual + added(fed)).astype(jnp.bfloat16)
        return gather_even(block) if even else gather_rows(block, direct=True)

    def finish(pieces, few=False):
        return spread(place, lengths, bins, starts, pieces, rows, per_row, few)

    def more(pieces):
        for turn in range(1, per_row):
            pieces = pieces + again(turn, False)
        return finish(pieces)

    def some(pieces):
        return finish(pieces + again(per_row, True), True)

    if rows == 8 and cols == 4:
        case = (count[0] > rows).astype(jnp.int32) + (count[0] > rows + rows // 2).astype(jnp.int32)
        layer_output = lax.switch(case, [finish, some, more], first)
    else:
        layer_output = lax.cond(count[0] > rows, more, finish, first)
    return (layer_output,) + weights


def solution(mesh):
    return jax.shard_map(
        shards,
        mesh=mesh,
        in_specs=(
            P("row", "col"),
            P("row"),
            P(("row", "col"), None),
            P(None, ("row", "col"), None),
            P(None, ("row", "col")),
            P(None, ("row", "col")),
        ),
        out_specs=(
            P("row", "col"),
            P("row", "col"),
            P(None, "row", "col"),
            P("col", "row"),
            P("col", "row"),
        ),
        check_vma=False,
    )
```
